128 devices in a mesh: wide: 32 (over z_lo, y, x), dp: 4 (over z_hi, core).
Axes of the slice: x: 4, y: 4, z: 4 (z_hi: 2, z_lo: 2; z = z_hi * 2 + z_lo), core: 2. Of those that a mesh axis runs over, the one named last changes fastest.
Arguments:
- layer_input: bfloat16 [4, 8192, 4096], P('dp', 'wide'), may hold values from -6 to 6
- inner_acts: bfloat16 [4, 8192, 4096], P('dp', 'wide'), may hold values from -6 to 6
- w_bc: bfloat16 [4096, 256], replicated, may hold values from -0.0234375 to 0.0234375
- w_dt: bfloat16 [4096, 64], replicated, may hold values from -0.09375 to 0.09375
- a_log: float32 [64], replicated, may hold values from -20 to 2
- dt_bias: float32 [64], replicated, may hold values from -5 to -2
- d_skip: float32 [64], replicated, may hold values from 0.5 to 1.5
- out_grad: bfloat16 [4, 8192, 4096], P('dp', 'wide'), may hold values from -16 to 16
Outputs:
- x_grad: bfloat16 [4, 8192, 4096], P('dp', 'wide')
- input_grad: bfloat16 [4, 8192, 4096], P('dp', 'wide')
- w_bc_grad: float32 [4096, 256], P(('wide', 'dp'))
- w_dt_grad: float32 [4096, 64], P(('wide', 'dp'))
- head_grads: float32 [3, 64], P(None, 'wide')
The draws below stay inside these ranges and needn't reach their ends.
All inputs are finite; a program needn't handle non-finite values.
Results may differ from the reference program's by a relative error of at most 0.03.
Values may be sent and summed in bfloat16 or wider, within the bound.
A program may use at most 448 MiB of HBM per device.

```python
import math
import jax
import jax.numpy as jnp
from jax import lax

D = 4096
H = 64
P_SIZE = 64
NSTATE = 128
STRETCH = 256
SEQ = 8192
BATCH = 4


def draw_a_log(key, part):
    key = jax.random.fold_in(key, 11)
    pick_key, slow_key, fast_key = jax.random.split(key, 3)
    slow_share = 0.5
    chosen = jax.random.uniform(pick_key, (H,)) < slow_share
    slow_value = jax.random.uniform(slow_key, (H,), minval=math.log(1.0 / SEQ), maxval=math.log(20.0 / SEQ))
    fast_value = jax.random.uniform(fast_key, (H,), minval=0.0, maxval=math.log(4.0))
    return jnp.where(chosen, slow_value, fast_value).astype(jnp.float32)


def draw_out_grad(key, part):
    key = jax.random.fold_in(key, 23)
    base_value = jax.random.truncated_normal(key, -4.0, 4.0, (BATCH, SEQ, H * P_SIZE))
    top_rise = 2.0
    position = (jnp.arange(BATCH)[:, None] * SEQ + jnp.arange(SEQ)[None, :]).astype(jnp.float32) / (BATCH * SEQ)
    return (base_value * (1.0 + top_rise * position)[:, :, None]).astype(jnp.bfloat16)


def spiked(result, stream_key, source, target, parts, factor):
    def block_of(dim):
        return (jnp.arange(result.shape[dim]) // (result.shape[dim] // parts)).reshape((-1,) + (1,) * (result.ndim - 1 - dim))

    first = jax.random.permutation(stream_key, parts)[block_of(target)]
    second = (block_of(target) + parts // 2) % parts
    return jnp.where((block_of(source) == first) | (block_of(source) == second), factor * result, result)


def level_of(own_key, shape, cuts, smallest, top_value):
    factor_of, own = 1.0, jax.random.fold_in(own_key, 6)
    for axis_at, blocks in cuts:
        steps = jnp.exp(jax.random.uniform(jax.random.fold_in(own, axis_at), (blocks,), jnp.float32, smallest / len(cuts), top_value / len(cuts)))
        factor_of = factor_of * jnp.repeat(steps, shape[axis_at] // blocks).reshape([-1 if axis == axis_at else 1 for axis in range(len(shape))])
    return factor_of


def gaussian(rng, shape, spread, bound, cuts=(), held_as=jnp.bfloat16):
    result = spread * jax.random.normal(rng, shape, jnp.float32)
    if cuts:
        result = result * level_of(rng, shape, cuts, -0.22, 0.18)
    return jnp.clip(result, -bound, bound).astype(held_as)


def gaussian_with(key, extent, scale, most, cuts, heavy, held_as=jnp.bfloat16):
    entries = scale * jax.random.normal(key, extent, jnp.float32)
    if cuts:
        entries = entries * level_of(key, extent, cuts, -0.22, 0.18)
    return jnp.clip(spiked(entries, jax.random.fold_in(key, 3), *heavy), -most, most).astype(held_as)


def setup_inputs(seed: int = 0) -> dict:
    seeds = jax.random.split(jax.random.key(seed), 9)
    return {
        "layer_input": gaussian_with(seeds[0], (BATCH, SEQ, D), 1.0, 6.0, ((0, 4), (1, 32)), (1, 2, 32, 2.75)),
        "inner_acts": gaussian(seeds[1], (BATCH, SEQ, H * P_SIZE), 1.0, 6.0, ((0, 4), (1, 32))),
        "w_bc": gaussian(seeds[2], (D, 2 * NSTATE), (16 * D) ** -0.5, 0.0234375),
        "w_dt": gaussian(seeds[3], (D, H), D ** -0.5, 0.09375),
        "a_log": draw_a_log(jax.random.fold_in(seeds[8], 71), 0),
        "dt_bias": jnp.clip(jax.random.uniform(seeds[5], (H,), jnp.float32, -5.0, -2.0), -5.0, -2.0),
        "d_skip": jnp.clip(jax.random.uniform(seeds[6], (H,), jnp.float32, 0.5, 1.5), 0.5, 1.5),
        "out_grad": draw_out_grad(jax.random.fold_in(seeds[8], 71), 0),
    }


precise = lax.Precision.HIGHEST

def stretch_forward(carried, pieces, a_log, d_skip):
    values, b_rows, c_rows, dt_pre = pieces
    steps_dt = jax.nn.softplus(dt_pre)
    log_rate = steps_dt * (-jnp.exp(a_log))[None, :]
    cumul = jnp.cumsum(log_rate, axis=0)
    length = values.shape[0]
    causal = jnp.arange(length)[:, None] >= jnp.arange(length)[None, :]
    gaps = cumul.T[:, :, None] - cumul.T[:, None, :]
    decay = jnp.exp(jnp.where(causal[None, :, :], gaps, -1e+30))
    scores = jnp.dot(c_rows, b_rows.T, precision=precise)
    mixing = decay * scores[None, :, :] * steps_dt.T[:, None, :]
    within = jnp.einsum('hts,shp->thp', mixing, values, precision=precise)
    from_state = jnp.einsum('tn,hpn->thp', c_rows, carried, precision=precise) * jnp.exp(cumul)[:, :, None]
    output = within + from_state + d_skip[None, :, None] * values
    tail_weight = jnp.exp(cumul[-1][None, :] - cumul) * steps_dt
    fresh = jnp.einsum('sh,shp,sn->hpn', tail_weight, values, b_rows, precision=precise)
    updated = jnp.exp(cumul[-1])[:, None, None] * carried + fresh
    return (updated, output)

def run_sequence(values, b_rows, c_rows, dt_pre, a_log, d_skip, initial):
    blocks = values.shape[0] // STRETCH

    def split_blocks(array):
        return array.reshape((blocks, STRETCH) + array.shape[1:])

    def advance(carried, pieces):
        return stretch_forward(carried, pieces, a_log, d_skip)
    final, outputs = lax.scan(jax.checkpoint(advance), initial, (split_blocks(values), split_blocks(b_rows), split_blocks(c_rows), split_blocks(dt_pre)))
    return (final, outputs.reshape(values.shape))

def reference(layer_input, inner_acts, w_bc, w_dt, a_log, dt_bias, d_skip, out_grad):
    heads = a_log.shape[0]
    head_dim = inner_acts.shape[2] // heads
    state_width = w_bc.shape[1] // 2
    length = layer_input.shape[1]

    def one_sequence(items):
        seq_input, seq_inner, seq_grad = items
        bc_rows = jnp.dot(seq_input, w_bc, preferred_element_type=jnp.float32).astype(jnp.bfloat16)
        dt_raw = jnp.dot(seq_input, w_dt, preferred_element_type=jnp.float32).astype(jnp.bfloat16)
        values = seq_inner.astype(jnp.float32).reshape(length, heads, head_dim)
        b_rows = bc_rows[:, :state_width].astype(jnp.float32)
        c_rows = bc_rows[:, state_width:].astype(jnp.float32)
        dt_pre = dt_raw.astype(jnp.float32) + dt_bias[None, :]

        def forward(values_in, b_in, c_in, dt_in, alog_in, skip_in):
            initial = jnp.zeros((heads, head_dim, state_width), jnp.float32)
            return run_sequence(values_in, b_in, c_in, dt_in, alog_in, skip_in, initial)[1]
        _, pull = jax.vjp(forward, values, b_rows, c_rows, dt_pre, a_log, d_skip)
        g_values, g_b, g_c, g_dt, g_alog, g_skip = pull(seq_grad.astype(jnp.float32).reshape(length, heads, head_dim))
        d_bc = jnp.concatenate([g_b, g_c], axis=1).astype(jnp.bfloat16)
        g_dtraw = g_dt.astype(jnp.bfloat16)
        d_input = (jnp.dot(d_bc, w_bc.T, preferred_element_type=jnp.float32) + jnp.dot(g_dtraw, w_dt.T, preferred_element_type=jnp.float32)).astype(jnp.bfloat16)
        grad_bc = jnp.dot(seq_input.T, d_bc, preferred_element_type=jnp.float32)
        grad_dt = jnp.dot(seq_input.T, g_dtraw, preferred_element_type=jnp.float32)
        head_sums = jnp.stack([g_alog, lax.optimization_barrier(jnp.sum(g_dt, axis=0)), g_skip])
        return (g_values.reshape(length, heads * head_dim).astype(jnp.bfloat16), d_input, grad_bc, grad_dt, head_sums)
    x_grad, input_grad, grad_bc, grad_dt, head_sums = lax.map(one_sequence, (layer_input, inner_acts, out_grad))
    return (x_grad, input_grad, lax.optimization_barrier(jnp.sum(grad_bc, axis=0)), lax.optimization_barrier(jnp.sum(grad_dt, axis=0)), lax.optimization_barrier(jnp.sum(head_sums, axis=0)))
```

```python
import functools

import jax
import jax.numpy as jnp
from jax import lax
from jax.experimental import pallas as pl
from jax.experimental.pallas import tpu as pltpu
from jax.sharding import PartitionSpec as P

MESH = pl.DeviceIdType.MESH
BF = jnp.bfloat16
F32 = jnp.float32
LANES = 128
BLOCK = 512


def mm(a, b):
    return jnp.dot(a, b, preferred_element_type=F32)


def mm_nt(a, b):
    return lax.dot_general(a, b, (((1,), (1,)), ((), ())), preferred_element_type=F32)


def split2(v):
    hi = v.astype(BF)
    return hi, (v - hi.astype(F32)).astype(BF)


def split3(v):
    hi = v.astype(BF)
    rest = v - hi.astype(F32)
    mid = rest.astype(BF)
    return hi, mid, (rest - mid.astype(F32)).astype(BF)


def scan_kernel(
    wide, dp, in_hbm, x_hbm, g_hbm, wbc_hbm, wdt_hbm, alog_ref, bias_ref, skip_ref,
    xg_hbm, ig_hbm, wpart_ref,
    in_ref, x_ref, g_ref, wbc_ref, wdt_ref, fg_ref, got1_ref, back_ref, got2_ref,
    xs_ref, gs_ref, gxw_ref, int_ref, nt_ref, st_ref, lt_ref, rt_ref, col_ref, hrow_ref, srow_ref,
    xo_ref, io_ref, load_sem, store_sem, s1_sem, r1_sem, s2_sem, r2_sem,
):
    me = lax.axis_index("wide")
    seq, width = in_ref.shape
    heads = alog_ref.shape[1]
    half = seq // 2
    nst = wbc_ref.shape[1] // 2
    owners = BLOCK // LANES
    blocks = width // BLOCK
    per_block = BLOCK // 64

    barrier = pltpu.get_barrier_semaphore()

    def greet(k, _):
        pl.semaphore_signal(
            barrier, inc=1, device_id={"wide": lax.rem(me + k, wide)}, device_id_type=MESH
        )
        return 0

    lax.fori_loop(1, wide, greet, 0)

    loads = [
        pltpu.make_async_copy(src, dst, load_sem.at[i])
        for i, (src, dst) in enumerate(
            ((in_hbm, in_ref), (wbc_hbm, wbc_ref), (wdt_hbm, wdt_ref), (x_hbm, x_ref), (g_hbm, g_ref))
        )
    ]
    for load in loads:
        load.start()
    loads[0].wait()
    loads[1].wait()
    bc = mm(in_ref[...], wbc_ref[...]).astype(BF)
    loads[2].wait()
    dt_raw = mm(in_ref[...], wdt_ref[...]).astype(BF).astype(F32)
    b_rows = bc[:, :nst]
    c_rows = bc[:, nst:]
    b_t = b_rows.astype(F32).T.astype(BF)
    c_t = c_rows.astype(F32).T.astype(BF)
    dt_pre = dt_raw + bias_ref[...]
    dt = jnp.maximum(dt_pre, 0.0) + jnp.log1p(jnp.exp(-jnp.abs(dt_pre)))
    rate = -jnp.exp(alog_ref[...])
    log_rate = dt * rate
    pos_r = lax.broadcasted_iota(jnp.int32, (seq, seq), 0)
    pos_c = lax.broadcasted_iota(jnp.int32, (seq, seq), 1)
    lower = (pos_r >= pos_c).astype(BF)
    lr_hi, lr_mid, lr_lo = split3(log_rate)
    cumul = mm(lower, lr_hi) + mm(lower, lr_mid) + mm(lower, lr_lo)
    last = cumul[seq - 1 :, :]
    tail = dt * jnp.exp(last - cumul)
    head_exp = jnp.exp(cumul)
    tail2 = jnp.concatenate(split2(tail), axis=1)
    exp2 = jnp.concatenate(split2(head_exp), axis=1)
    lq_hi, lq_mid, lq_lo = split3(last)
    none = jnp.zeros((1, heads), BF)
    lq_rows = jnp.concatenate(
        [jnp.concatenate([v, none], axis=1) for v in (lq_hi, lq_mid, lq_lo)]
        + [jnp.zeros((13, 2 * heads), BF)],
        axis=0,
    )
    lt_ref[...] = cumul.T
    u3 = jnp.concatenate(split3(jnp.log(jnp.maximum(dt, 1e-37)) - cumul), axis=1)
    st_ref[...] = mm_nt(b_rows, c_rows)

    delta = lax.rem(
        lax.broadcasted_iota(jnp.int32, (2 * heads, BLOCK), 0), heads
    ) - lax.broadcasted_iota(jnp.int32, (2 * heads, BLOCK), 1) // 64

    def spread(j):
        return (delta == j * per_block).astype(BF)

    loads[3].wait()
    loads[4].wait()
    pl.semaphore_wait(barrier, wide - 1)

    def first_copy(peer):
        return pltpu.make_async_remote_copy(
            src_ref=fg_ref.at[peer],
            dst_ref=got1_ref.at[me],
            send_sem=s1_sem.at[peer],
            recv_sem=r1_sem.at[me],
            device_id={"wide": peer},
            device_id_type=MESH,
        )

    def second_copy(peer):
        return pltpu.make_async_remote_copy(
            src_ref=back_ref.at[peer],
            dst_ref=got2_ref.at[me],
            send_sem=s2_sem.at[peer],
            recv_sem=r2_sem.at[me],
            device_id={"wide": peer},
            device_id_type=MESH,
        )

    def fresh(step, _):
        j = lax.rem(step + me // owners + 1, blocks)
        cols = pl.ds(pl.multiple_of(j * BLOCK, BLOCK), BLOCK)
        r = spread(j)
        xs = (x_ref[:, cols].astype(F32) * mm(tail2, r)).astype(BF)
        xs_ref[:, cols] = xs
        f_t = mm(b_t, xs).astype(BF)
        gs = (g_ref[:, cols].astype(F32) * mm(exp2, r)).astype(BF)
        gs_ref[:, cols] = gs
        g_t = mm(c_t, gs).astype(BF)
        lq = mm(lq_rows, r).astype(BF)
        for i in range(owners):
            lanes = slice(i * LANES, (i + 1) * LANES)
            peer = j * owners + i
            fg_ref[peer, :nst, :] = f_t[:, lanes]
            fg_ref[peer, nst : 2 * nst, :] = g_t[:, lanes]
            fg_ref[peer, 2 * nst :, :] = lq[:, lanes]

            @pl.when(peer != me)
            def _():
                first_copy(peer).start()

        return 0

    lax.fori_loop(0, blocks, fresh, 0)

    lane = lax.broadcasted_iota(jnp.int32, (seq, LANES), 1)
    lane_head = lax.broadcasted_iota(jnp.int32, (half, heads), 1)
    upper = lax.broadcasted_iota(jnp.int32, (half, half), 0) <= lax.broadcasted_iota(
        jnp.int32, (half, half), 1
    )
    row_head = lax.rem(lax.broadcasted_iota(jnp.int32, (3 * heads, LANES), 0), heads)
    nt_ref[...] = jnp.zeros_like(nt_ref)
    col_ref[...] = jnp.zeros_like(col_ref)

    def within(pair, _):
        cols = pl.ds(pl.multiple_of(pair * LANES, LANES), LANES)
        xk = x_ref[:, cols]
        gk = g_ref[:, cols]
        total_lo = jnp.zeros((half, LANES), F32)
        total_hi = jnp.zeros((half, LANES), F32)
        for side in range(2):
            h = pair * 2 + side
            mine = (lane < 64) if side == 0 else (lane >= 64)
            xm = jnp.where(mine, xk, jnp.zeros_like(xk))
            gm = jnp.where(mine, gk, jnp.zeros_like(gk))
            u = mm(u3, (row_head == h).astype(BF))
            lt = lt_ref[pl.ds(h, 1), :]
            w0 = mm_nt(xm[:half], gk)
            w1 = mm_nt(xm[half:], gk[half:])
            a00 = jnp.where(upper, jnp.exp(u[:half] + lt[:, :half]), 0.0)
            a01 = jnp.exp(u[:half] + lt[:, half:])
            a11 = jnp.where(upper, jnp.exp(u[half:] + lt[:, half:]), 0.0)
            s00 = st_ref[:half, :half]
            s01 = st_ref[:half, half:]
            s11 = st_ref[half:, half:]
            p00 = a00 * w0[:, :half]
            p01 = a01 * w0[:, half:]
            p11 = a11 * w1
            nt_ref[:half, :half] += p00
            nt_ref[:half, half:] += p01
            nt_ref[half:, half:] += p11
            total_lo += mm((a00 * s00).astype(BF), gm[:half]) + mm((a01 * s01).astype(BF), gm[half:])
            total_hi += mm((a11 * s11).astype(BF), gm[half:])
            z00 = p00 * s00
            z01 = p01 * s01
            z11 = p11 * s11
            rt_ref[h, :, :half] = jnp.sum(z00, axis=0, keepdims=True)
            rt_ref[h, :, half:] = jnp.sum(z01 + z11, axis=0, keepdims=True)
            col_ref[:half, :] += jnp.where(
                lane_head == h, jnp.sum(z00 + z01, axis=1, keepdims=True), 0.0
            )
            col_ref[half:, :] += jnp.where(
                lane_head == h, jnp.sum(z11, axis=1, keepdims=True), 0.0
            )
        gxw_ref[:half, cols] = total_lo
        gxw_ref[half:, cols] = total_hi
        int_ref[cols, :] = in_ref[:, cols].astype(F32).T.astype(BF)
        return 0

    pairs = width // LANES
    lax.fori_loop(0, pairs // 2, within, 0)

    got1_ref[me] = fg_ref[me]

    def take1(k, _):
        peer = lax.rem(me + k, wide)
        pltpu.make_async_copy(fg_ref.at[peer], got1_ref.at[peer], r1_sem.at[peer]).wait()
        return 0

    lax.fori_loop(1, wide, take1, 0)

    def decay_of(i):
        parts = got1_ref[i, 2 * nst :, :].astype(F32)
        return jnp.exp(parts[0:1] + parts[1:2] + parts[2:3])

    def advance(i, carried):
        state, pull = carried
        later = wide - 1 - i
        back_ref[i, :nst, :] = state.astype(BF)
        back_ref[later, nst:, :] = pull.astype(BF)
        state = state * decay_of(i) + got1_ref[i, :nst, :].astype(F32)
        pull = pull * decay_of(later) + got1_ref[later, nst : 2 * nst, :].astype(F32)
        return state, pull

    start = jnp.zeros((nst, LANES), F32)
    lax.fori_loop(0, wide, advance, (start, start))

    def give2(k, _):
        second_copy(lax.rem(me + k, wide)).start()
        return 0

    lax.fori_loop(1, wide, give2, 0)
    got2_ref[me] = back_ref[me]

    lax.fori_loop(pairs // 2, pairs, within, 0)

    n_low = nt_ref[...].astype(BF)
    g_b = mm(n_low, c_rows)
    g_c = mm(nt_ref[...].T.astype(BF), b_rows)

    def take2(k, _):
        peer = lax.rem(me + k, wide)
        pltpu.make_async_copy(back_ref.at[peer], got2_ref.at[peer], r2_sem.at[peer]).wait()
        first_copy(peer).wait_send()
        second_copy(peer).wait_send()
        return 0

    lax.fori_loop(1, wide, take2, 0)

    skip_hi, skip_lo = split2(skip_ref[...])
    skip_rows = jnp.concatenate(
        [jnp.concatenate([skip_hi, skip_lo], axis=1)]
        + [jnp.concatenate([v, none], axis=1) for v in (lq_hi, lq_mid, lq_lo)]
        + [jnp.zeros((12, 2 * heads), BF)],
        axis=0,
    )
    gather_delta = lax.broadcasted_iota(jnp.int32, (BLOCK, heads), 1) - lax.broadcasted_iota(
        jnp.int32, (BLOCK, heads), 0
    ) // 64

    def finish(j, carried):
        row_st, col_st, gb, gc = carried
        cols = pl.ds(pl.multiple_of(j * BLOCK, BLOCK), BLOCK)
        r = spread(j)
        gather = (gather_delta == j * per_block).astype(BF)
        h0 = jnp.concatenate([got2_ref[j * owners + i, :nst, :] for i in range(owners)], axis=1)
        dh = jnp.concatenate([got2_ref[j * owners + i, nst:, :] for i in range(owners)], axis=1)
        own = jnp.concatenate([fg_ref[j * owners + i, :nst, :] for i in range(owners)], axis=1)
        xs = xs_ref[:, cols]
        gs = gs_ref[:, cols]
        g32 = g_ref[:, cols].astype(F32)
        y_st = mm(c_rows, h0)
        u_st = mm(b_rows, dh)
        rows = mm(skip_rows, r)
        gx = gxw_ref[:, cols] + mm(tail2, r) * u_st + rows[0:1] * g32
        xo_ref[:, cols] = gx.astype(BF)
        row_st += mm((gs.astype(F32) * y_st).astype(BF), gather)
        col_st += mm((xs.astype(F32) * u_st).astype(BF), gather)
        gb += mm_nt(xs, dh)
        gc += mm_nt(gs, h0)
        ended = h0.astype(F32) * jnp.exp(rows[1:2] + rows[2:3] + rows[3:4]) + own.astype(F32)
        hrow_ref[0:1, cols] = jnp.sum(ended * dh.astype(F32), axis=0, keepdims=True)
        hrow_ref[1:2, cols] = jnp.sum(x_ref[:, cols].astype(F32) * g32, axis=0, keepdims=True)
        pltpu.make_async_copy(xo_ref.at[:, cols], xg_hbm.at[:, cols], store_sem.at[0, j]).start()
        return row_st, col_st, gb, gc

    zero_h = jnp.zeros((seq, heads), F32)
    row_st, col_st, g_b, g_c = lax.fori_loop(0, blocks, finish, (zero_h, zero_h, g_b, g_c))

    head_of = lax.broadcasted_iota(jnp.int32, (width, heads), 0) // 64
    gather_all = (head_of == lax.broadcasted_iota(jnp.int32, (width, heads), 1)).astype(BF)
    hr_hi, hr_lo = split2(hrow_ref[...])
    sums = mm(hr_hi, gather_all) + mm(hr_lo, gather_all)
    crossing, g_skip = sums[0:1], sums[1:2]

    row_all = rt_ref[:, 0, :].T + row_st
    col_all = col_ref[...] + col_st
    upper_all = (pos_r <= pos_c).astype(BF)
    d_hi, d_mid, d_lo = split3(row_all - col_all)
    d_log = mm(upper_all, d_hi) + mm(upper_all, d_mid) + mm(upper_all, d_lo) + crossing
    gate = 1.0 / (1.0 + jnp.exp(-dt_pre))
    ratio = jnp.where(dt > 0.0, gate / jnp.where(dt > 0.0, dt, 1.0), 1.0)
    g_dt = col_all * ratio + rate * d_log * gate
    g_alog = jnp.sum(d_log * log_rate, axis=0, keepdims=True)
    g_bias = jnp.sum(g_dt, axis=0, keepdims=True)
    d_bc = jnp.concatenate([g_b, g_c], axis=1).astype(BF)
    g_raw = g_dt.astype(BF)
    head_rows = jnp.concatenate([g_alog, g_bias, g_skip, jnp.zeros((13, heads), F32)], axis=0)
    head_rows = jnp.concatenate(split2(head_rows), axis=1)

    def emit(j, _):
        cols = pl.ds(pl.multiple_of(j * BLOCK, BLOCK), BLOCK)
        d_in = mm_nt(d_bc, wbc_ref[cols, :]) + mm_nt(g_raw, wdt_ref[cols, :])
        io_ref[:, cols] = d_in.astype(BF)
        pltpu.make_async_copy(io_ref.at[:, cols], ig_hbm.at[:, cols], store_sem.at[1, j]).start()
        rows = int_ref[cols, :]
        w_bc = mm(rows, d_bc).astype(BF)
        w_dt = mm(rows, g_raw)
        for i in range(BLOCK // 32):
            d = i % dp
            slot = (j * (BLOCK // 32 // dp) + i // dp) * (dp // 2) + d // 2
            at = slice(i * 32, (i + 1) * 32)
            wpart_ref[d % 2, slot, 0:32, :] = w_bc[at, :LANES]
            wpart_ref[d % 2, slot, 32:64, :] = w_bc[at, LANES:]
            wpart_ref[d % 2, slot, 64:80, : 2 * heads] = jnp.concatenate(
                [w_dt[i * 32 : i * 32 + 16], w_dt[i * 32 + 16 : i * 32 + 32]], axis=1
            ).astype(BF)
            wpart_ref[d % 2, slot, 80:96, : 2 * heads] = head_rows
        return 0

    lax.fori_loop(0, blocks, emit, 0)

    def drain(j, _):
        cols = pl.ds(pl.multiple_of(j * BLOCK, BLOCK), BLOCK)
        pltpu.make_async_copy(xo_ref.at[:, cols], xg_hbm.at[:, cols], store_sem.at[0, j]).wait()
        pltpu.make_async_copy(io_ref.at[:, cols], ig_hbm.at[:, cols], store_sem.at[1, j]).wait()
        return 0

    lax.fori_loop(0, blocks, drain, 0)


def sum_kernel(
    wide, dp, heads, wpart_ref, wbc_out, wdt_out, head_out,
    pair_ref, sent_ref, got_ref, sp_sem, rp_sem, s_sem, r_sem,
):
    me = lax.axis_index("wide")
    place = lax.axis_index("dp")
    core = lax.rem(place, 2)
    other = 1 - core
    sets = dp // 2
    mine = me * sets + place // 2
    slots = wide * sets
    group = 8
    groups = slots // group
    sibling = {"wide": me, "dp": place - core + other}

    def at_slot(slot):
        return {"wide": slot // sets, "dp": lax.rem(slot, sets) * 2 + core}

    barrier = pltpu.get_barrier_semaphore()
    pl.semaphore_signal(barrier, inc=1, device_id=sibling, device_id_type=MESH)

    def greet(k, _):
        pl.semaphore_signal(
            barrier, inc=1, device_id=at_slot(lax.rem(mine + k, slots)), device_id_type=MESH
        )
        return 0

    lax.fori_loop(1, slots, greet, 0)
    pl.semaphore_wait(barrier, slots)

    def pair_copy(c):
        part = pl.ds(c * group, group)
        return pltpu.make_async_remote_copy(
            src_ref=wpart_ref.at[other, part],
            dst_ref=pair_ref.at[part],
            send_sem=sp_sem.at[c],
            recv_sem=rp_sem.at[c],
            device_id=sibling,
            device_id_type=MESH,
        )

    def slot_copy(slot):
        return pltpu.make_async_remote_copy(
            src_ref=sent_ref.at[slot],
            dst_ref=got_ref.at[mine],
            send_sem=s_sem.at[slot],
            recv_sem=r_sem.at[mine],
            device_id=at_slot(slot),
            device_id_type=MESH,
        )

    def turn(k):
        return lax.rem(mine // group + k + 1, groups)

    def give(k, _):
        pair_copy(turn(k)).start()
        return 0

    lax.fori_loop(0, groups, give, 0)

    def add(k, _):
        c = turn(k)
        pair_copy(c).wait_recv()
        for i in range(group):
            slot = c * group + i
            sent_ref[slot, :80, :] = (
                wpart_ref[core, slot, :80, :].astype(F32) + pair_ref[slot, :80, :].astype(F32)
            ).astype(BF)
            ours = wpart_ref[core, slot, 80:, :].astype(F32)
            theirs = pair_ref[slot, 80:, :].astype(F32)
            both = ours + theirs
            sent_ref[slot, 80:, : 2 * heads] = jnp.concatenate(
                split2(both[:, :heads] + both[:, heads : 2 * heads]), axis=1
            )

            @pl.when(slot != mine)
            def _():
                slot_copy(slot).start()

        return 0

    lax.fori_loop(0, groups, add, 0)

    def total(k, acc):
        slot = lax.rem(mine + k, slots)
        pltpu.make_async_copy(sent_ref.at[slot], got_ref.at[slot], r_sem.at[slot]).wait()
        return acc + got_ref[slot].astype(F32)

    acc = lax.fori_loop(1, slots, total, sent_ref[mine].astype(F32))
    wbc_out[:, :LANES] = acc[0:32]
    wbc_out[:, LANES:] = acc[32:64]
    wdt_out[0:16, :] = acc[64:80, :heads]
    wdt_out[16:32, :] = acc[64:80, heads : 2 * heads]
    rows = acc[80:88, :heads] + acc[80:88, heads : 2 * heads]
    at = lax.broadcasted_iota(jnp.int32, rows.shape, 1)
    per = heads // wide
    for i in range(per):
        picked = jnp.sum(jnp.where(at == me * per + i, rows, 0.0), axis=1, keepdims=True)
        head_out[:, i : i + 1] = picked[:3]

    def done(k, _):
        slot_copy(lax.rem(mine + k, slots)).wait_send()
        return 0

    lax.fori_loop(1, slots, done, 0)

    def done_pair(c, _):
        pair_copy(c).wait_send()
        return 0

    lax.fori_loop(0, groups, done_pair, 0)


def local(wide, dp, layer_input, inner_acts, w_bc, w_dt, a_log, dt_bias, d_skip, out_grad):
    seq, width = layer_input.shape[1:]
    heads = a_log.shape[0]
    nst = w_bc.shape[1] // 2
    slots = wide * dp // 2
    any_spec = pl.BlockSpec(memory_space=pl.ANY)
    vmem = pl.BlockSpec(memory_space=pltpu.VMEM)
    dma = pltpu.SemaphoreType.DMA
    x_grad, input_grad, wpart = pl.pallas_call(
        functools.partial(scan_kernel, wide, dp),
        out_shape=(
            jax.ShapeDtypeStruct((seq, width), BF),
            jax.ShapeDtypeStruct((seq, width), BF),
            jax.ShapeDtypeStruct((2, slots, 96, LANES), BF),
        ),
        in_specs=[any_spec] * 5 + [vmem] * 3,
        out_specs=(any_spec, any_spec, vmem),
        scratch_shapes=[
            pltpu.VMEM((seq, width), BF),
            pltpu.VMEM((seq, width), BF),
            pltpu.VMEM((seq, width), BF),
            pltpu.VMEM((width, 2 * nst), BF),
            pltpu.VMEM((width, heads), BF),
            pltpu.VMEM((wide, 2 * nst + 16, LANES), BF),
            pltpu.VMEM((wide, 2 * nst + 16, LANES), BF),
            pltpu.VMEM((wide, 2 * nst, LANES), BF),
            pltpu.VMEM((wide, 2 * nst, LANES), BF),
            pltpu.VMEM((seq, width), BF),
            pltpu.VMEM((seq, width), BF),
            pltpu.VMEM((seq, width), F32),
            pltpu.VMEM((width, seq), BF),
            pltpu.VMEM((seq, seq), F32),
            pltpu.VMEM((seq, seq), F32),
            pltpu.VMEM((heads, seq), F32),
            pltpu.VMEM((heads, 1, seq), F32),
            pltpu.VMEM((seq, heads), F32),
            pltpu.VMEM((2, width), F32),
            pltpu.VMEM((2, width), F32),
            pltpu.VMEM((seq, width), BF),
            pltpu.VMEM((seq, width), BF),
            dma((5,)),
            dma((2, width // BLOCK)),
            dma((wide,)),
            dma((wide,)),
            dma((wide,)),
            dma((wide,)),
        ],
        compiler_params=pltpu.CompilerParams(
            collective_id=0, has_side_effects=True, vmem_limit_bytes=56 * 1024 * 1024
        ),
        cost_estimate=pl.CostEstimate(
            flops=30 * seq * width * 256, bytes_accessed=8 * seq * width, transcendentals=0
        ),
        name="scan_backward",
    )(
        layer_input[0], inner_acts[0], out_grad[0], w_bc, w_dt,
        a_log[None], dt_bias[None], d_skip[None],
    )
    rows = width // (wide * dp)
    wbc_grad, wdt_grad, head_grads = pl.pallas_call(
        functools.partial(sum_kernel, wide, dp, heads),
        out_shape=(
            jax.ShapeDtypeStruct((rows, 2 * nst), F32),
            jax.ShapeDtypeStruct((rows, heads), F32),
            jax.ShapeDtypeStruct((3, heads // wide), F32),
        ),
        in_specs=[vmem],
        out_specs=(vmem, vmem, vmem),
        scratch_shapes=[
            pltpu.VMEM((slots, 96, LANES), BF),
            pltpu.VMEM((slots, 96, LANES), BF),
            pltpu.VMEM((slots, 96, LANES), BF),
            dma((slots // 8,)),
            dma((slots // 8,)),
            dma((slots,)),
            dma((slots,)),
        ],
        compiler_params=pltpu.CompilerParams(
            collective_id=1, has_side_effects=True, vmem_limit_bytes=24 * 1024 * 1024
        ),
        name="weight_sums",
    )(wpart)
    return x_grad[None], input_grad[None], wbc_grad, wdt_grad, head_grads


def solution(mesh):
    in_specs = (
        P("dp", "wide", None),
        P("dp", "wide", None),
        P(),
        P(),
        P(),
        P(),
        P(),
        P("dp", "wide", None),
    )
    out_specs = (
        P("dp", "wide", None),
        P("dp", "wide", None),
        P(("wide", "dp"), None),
        P(("wide", "dp"), None),
        P(None, "wide"),
    )
    return jax.shard_map(
        functools.partial(local, mesh.shape["wide"], mesh.shape["dp"]),
        mesh=mesh,
        in_specs=in_specs,
        out_specs=out_specs,
        check_vma=False,
    )
```

```python
import functools

import jax
import jax.numpy as jnp
from jax import lax
from jax.experimental import pallas as pl
from jax.experimental.pallas import tpu as pltpu
from jax.sharding import PartitionSpec as P

MESH = pl.DeviceIdType.MESH
BF = jnp.bfloat16
F32 = jnp.float32
LANES = 128
BLOCK = 512
STRIDE = 13


def mm(a, b):
    return jnp.dot(a, b, preferred_element_type=F32)


def mm_nt(a, b):
    return lax.dot_general(a, b, (((1,), (1,)), ((), ())), preferred_element_type=F32)


def split2(v):
    hi = v.astype(BF)
    return hi, (v - hi.astype(F32)).astype(BF)


def split3(v):
    hi = v.astype(BF)
    rest = v - hi.astype(F32)
    mid = rest.astype(BF)
    return hi, mid, (rest - mid.astype(F32)).astype(BF)


def scan_kernel(
    wide, dp, in_hbm, x_hbm, g_hbm, wbc_hbm, wdt_hbm, alog_ref, bias_ref, skip_ref,
    xg_hbm, ig_hbm, wbc_out, wdt_out, head_out,
    in_ref, x_ref, g_ref, wbc_ref, wdt_ref, f_ref, gt_ref, gotf_ref, gotg_ref, h_ref, p_ref,
    goth_ref, gotp_ref, xs_ref, gs_ref, gxw_ref, int_ref, sib_ref, nt_ref, st_ref, lt_ref, rt_ref,
    col_ref, hrow_ref, xo_ref, io_ref, dproj_ref, sibd_ref, hg_ref, hsib_ref, ha_ref, hb_ref,
    out_ref, got_ref,
    load_sem, store_sem, sib_send, sib_recv, hs_sem, hr_sem,
    sf_sem, rf_sem, sg_sem, rg_sem, sh_sem, rh_sem, sp_sem, rp_sem, sw_sem, rw_sem,
):
    me = lax.axis_index("wide")
    place = lax.axis_index("dp")
    core = lax.rem(place, 2)
    other = 1 - core
    sets = dp // 2
    slots = wide * sets
    mine = me * sets + place // 2
    seq, width = in_ref.shape
    heads = alog_ref.shape[1]
    half = seq // 2
    nst = wbc_ref.shape[1] // 2
    owners = BLOCK // LANES
    blocks = width // BLOCK
    per_block = BLOCK // 64
    pairs = width // LANES
    group = 8
    groups = slots // group
    sibling = {"wide": me, "dp": place - core + other}

    def at_slot(slot):
        return {"wide": slot // sets, "dp": lax.rem(slot, sets) * 2 + core}

    def to_peer(k):
        return lax.rem(me + k * STRIDE, wide)

    def from_peer(k):
        return lax.rem(me + (wide - k) * STRIDE, wide)

    barrier = pltpu.get_barrier_semaphore()
    pl.semaphore_signal(barrier, inc=1, device_id=sibling, device_id_type=MESH)

    def greet(k, _):
        pl.semaphore_signal(
            barrier, inc=1, device_id=at_slot(lax.rem(mine + k, slots)), device_id_type=MESH
        )
        return 0

    lax.fori_loop(1, slots, greet, 0)

    loads = [
        pltpu.make_async_copy(src, dst, load_sem.at[i])
        for i, (src, dst) in enumerate(
            ((in_hbm, in_ref), (wbc_hbm, wbc_ref), (wdt_hbm, wdt_ref), (x_hbm, x_ref), (g_hbm, g_ref))
        )
    ]
    for load in loads:
        load.start()

    delta = lax.rem(
        lax.broadcasted_iota(jnp.int32, (2 * heads, BLOCK), 0), heads
    ) - lax.broadcasted_iota(jnp.int32, (2 * heads, BLOCK), 1) // 64

    def spread(j):
        return (delta == j * per_block).astype(BF)

    def remote(src, dst, send, recv, target):
        return pltpu.make_async_remote_copy(
            src_ref=src, dst_ref=dst, send_sem=send, recv_sem=recv, device_id=target,
            device_id_type=MESH,
        )

    def send_f(peer):
        return remote(f_ref.at[peer], gotf_ref.at[me], sf_sem.at[peer], rf_sem.at[me], {"wide": peer})

    def send_g(peer):
        return remote(gt_ref.at[peer], gotg_ref.at[me], sg_sem.at[peer], rg_sem.at[me], {"wide": peer})

    def send_h(peer):
        return remote(h_ref.at[peer], goth_ref.at[me], sh_sem.at[peer], rh_sem.at[me], {"wide": peer})

    def send_p(peer):
        return remote(p_ref.at[peer], gotp_ref.at[me], sp_sem.at[peer], rp_sem.at[me], {"wide": peer})

    def send_w(slot):
        return remote(out_ref.at[slot], got_ref.at[mine], sw_sem.at[slot], rw_sem.at[mine], at_slot(slot))

    sib_in = remote(int_ref.at[other], sib_ref, sib_send.at[0], sib_recv.at[0], sibling)
    sib_d = remote(dproj_ref, sibd_ref, sib_send.at[1], sib_recv.at[1], sibling)
    sib_h = remote(hg_ref, hsib_ref, sib_send.at[2], sib_recv.at[2], sibling)

    loads[0].wait()
    loads[1].wait()
    bc = mm(in_ref[...], wbc_ref[...]).astype(BF)
    loads[2].wait()
    dt_raw = mm_nt(in_ref[...], wdt_ref[...]).astype(BF).astype(F32)
    b_rows = bc[:, :nst]
    c_rows = bc[:, nst:]
    b_t = b_rows.astype(F32).T.astype(BF)
    c_t = c_rows.astype(F32).T.astype(BF)
    dt_pre = dt_raw + bias_ref[...]
    dt = jnp.maximum(dt_pre, 0.0) + jnp.log1p(jnp.exp(-jnp.abs(dt_pre)))
    rate = -jnp.exp(alog_ref[...])
    log_rate = dt * rate
    pos_r = lax.broadcasted_iota(jnp.int32, (seq, seq), 0)
    pos_c = lax.broadcasted_iota(jnp.int32, (seq, seq), 1)
    lower = (pos_r >= pos_c).astype(BF)
    lr_hi, lr_mid, lr_lo = split3(log_rate)
    cumul = mm(lower, lr_hi) + mm(lower, lr_mid) + mm(lower, lr_lo)
    last = cumul[seq - 1 :, :]
    tail = dt * jnp.exp(last - cumul)
    tail2 = jnp.concatenate(split2(tail), axis=1)
    lq_hi, lq_mid, lq_lo = split3(last)
    none = jnp.zeros((1, heads), BF)
    lq_rows = jnp.concatenate(
        [jnp.concatenate([v, none], axis=1) for v in (lq_hi, lq_mid, lq_lo)]
        + [jnp.zeros((13, 2 * heads), BF)],
        axis=0,
    )

    def block_at(step):
        return lax.rem(me // owners + (step + 1) * 5, blocks)

    loads[3].wait()
    pl.semaphore_wait(barrier, slots)

    def fresh_f(step, _):
        j = block_at(step)
        cols = pl.ds(pl.multiple_of(j * BLOCK, BLOCK), BLOCK)
        r = spread(j)
        xs = (x_ref[:, cols].astype(F32) * mm(tail2, r)).astype(BF)
        xs_ref[:, cols] = xs
        f_t = mm(b_t, xs).astype(BF)
        lq = mm(lq_rows, r).astype(BF)
        for i in range(owners):
            lanes = slice(i * LANES, (i + 1) * LANES)
            peer = j * owners + i
            f_ref[peer, :nst, :] = f_t[:, lanes]
            f_ref[peer, nst:, :] = lq[:, lanes]

            @pl.when(peer != me)
            def _():
                send_f(peer).start()

        return 0

    lax.fori_loop(0, blocks, fresh_f, 0)

    head_exp = jnp.exp(cumul)
    exp2 = jnp.concatenate(split2(head_exp), axis=1)
    loads[4].wait()

    def fresh_g(step, _):
        j = block_at(step)
        cols = pl.ds(pl.multiple_of(j * BLOCK, BLOCK), BLOCK)
        gs = (g_ref[:, cols].astype(F32) * mm(exp2, spread(j))).astype(BF)
        gs_ref[:, cols] = gs
        g_t = mm(c_t, gs).astype(BF)
        for i in range(owners):
            peer = j * owners + i
            gt_ref[peer] = g_t[:, i * LANES : (i + 1) * LANES]

            @pl.when(peer != me)
            def _():
                send_g(peer).start()

        return 0

    lax.fori_loop(0, blocks, fresh_g, 0)

    lt_ref[...] = cumul.T
    u3 = jnp.concatenate(split3(jnp.log(jnp.maximum(dt, 1e-37)) - cumul), axis=1)
    st_ref[...] = mm_nt(b_rows, c_rows)
    lane = lax.broadcasted_iota(jnp.int32, (seq, LANES), 1)
    lane_head = lax.broadcasted_iota(jnp.int32, (half, heads), 1)
    upper = lax.broadcasted_iota(jnp.int32, (half, half), 0) <= lax.broadcasted_iota(
        jnp.int32, (half, half), 1
    )
    row_head = lax.rem(lax.broadcasted_iota(jnp.int32, (3 * heads, LANES), 0), heads)
    nt_ref[...] = jnp.zeros_like(nt_ref)
    col_ref[...] = jnp.zeros_like(col_ref)

    def within(pair, _):
        cols = pl.ds(pl.multiple_of(pair * LANES, LANES), LANES)
        xk = x_ref[:, cols]
        gk = g_ref[:, cols]
        total_lo = jnp.zeros((half, LANES), F32)
        total_hi = jnp.zeros((half, LANES), F32)
        for side in range(2):
            h = pair * 2 + side
            mine_lane = (lane < 64) if side == 0 else (lane >= 64)
            xm = jnp.where(mine_lane, xk, jnp.zeros_like(xk))
            gm = jnp.where(mine_lane, gk, jnp.zeros_like(gk))
            u = mm(u3, (row_head == h).astype(BF))
            lt = lt_ref[pl.ds(h, 1), :]
            w0 = mm_nt(xm[:half], gk)
            w1 = mm_nt(xm[half:], gk[half:])
            a00 = jnp.where(upper, jnp.exp(u[:half] + lt[:, :half]), 0.0)
            a01 = jnp.exp(u[:half] + lt[:, half:])
            a11 = jnp.where(upper, jnp.exp(u[half:] + lt[:, half:]), 0.0)
            s00 = st_ref[:half, :half]
            s01 = st_ref[:half, half:]
            s11 = st_ref[half:, half:]
            p00 = a00 * w0[:, :half]
            p01 = a01 * w0[:, half:]
            p11 = a11 * w1
            nt_ref[:half, :half] += p00
            nt_ref[:half, half:] += p01
            nt_ref[half:, half:] += p11
            total_lo += mm((a00 * s00).astype(BF), gm[:half]) + mm((a01 * s01).astype(BF), gm[half:])
            total_hi += mm((a11 * s11).astype(BF), gm[half:])
            z00 = p00 * s00
            z01 = p01 * s01
            z11 = p11 * s11
            rt_ref[h, :, :half] = jnp.sum(z00, axis=0, keepdims=True)
            rt_ref[h, :, half:] = jnp.sum(z01 + z11, axis=0, keepdims=True)
            col_ref[:half, :] += jnp.where(
                lane_head == h, jnp.sum(z00 + z01, axis=1, keepdims=True), 0.0
            )
            col_ref[half:, :] += jnp.where(
                lane_head == h, jnp.sum(z11, axis=1, keepdims=True), 0.0
            )
        gxw_ref[:half, cols] = total_lo
        gxw_ref[half:, cols] = total_hi
        turned = in_ref[:, cols].astype(F32).T.astype(BF)
        for i in range(dp):
            int_ref[i % 2, pair * sets + i // 2] = turned[i * 32 : (i + 1) * 32]
        return 0

    first_part = (pairs * 5) // 8
    lax.fori_loop(0, first_part, within, 0)

    def decay_of(i):
        parts = gotf_ref[i, nst:, :].astype(F32)
        return jnp.exp(parts[0:1] + parts[1:2] + parts[2:3])

    def take_f(k, _):
        peer = from_peer(k)
        pltpu.make_async_copy(f_ref.at[peer], gotf_ref.at[peer], rf_sem.at[peer]).wait()
        return 0

    gotf_ref[me] = f_ref[me]
    lax.fori_loop(1, wide, take_f, 0)

    def advance_f(i, state):
        h_ref[i] = state.astype(BF)
        return state * decay_of(i) + gotf_ref[i, :nst, :].astype(F32)

    start = jnp.zeros((nst, LANES), F32)
    lax.fori_loop(0, wide, advance_f, start)

    def give_h(k, _):
        send_h(to_peer(k)).start()
        return 0

    lax.fori_loop(1, wide, give_h, 0)
    goth_ref[me] = h_ref[me]

    lax.fori_loop(first_part, pairs, within, 0)
    sib_in.start()

    def take_g(k, _):
        peer = from_peer(k)
        pltpu.make_async_copy(gt_ref.at[peer], gotg_ref.at[peer], rg_sem.at[peer]).wait()
        return 0

    gotg_ref[me] = gt_ref[me]
    lax.fori_loop(1, wide, take_g, 0)

    def advance_g(k, pull):
        i = wide - 1 - k
        p_ref[i] = pull.astype(BF)
        return pull * decay_of(i) + gotg_ref[i].astype(F32)

    lax.fori_loop(0, wide, advance_g, start)

    def give_p(k, _):
        send_p(to_peer(k)).start()
        return 0

    lax.fori_loop(1, wide, give_p, 0)
    gotp_ref[me] = p_ref[me]

    n_low = nt_ref[...].astype(BF)
    g_b = mm(n_low, c_rows)
    g_c = mm(nt_ref[...].T.astype(BF), b_rows)

    skip_hi, skip_lo = split2(skip_ref[...])
    skip_rows = jnp.concatenate(
        [jnp.concatenate([skip_hi, skip_lo], axis=1)]
        + [jnp.concatenate([v, none], axis=1) for v in (lq_hi, lq_mid, lq_lo)]
        + [jnp.zeros((12, 2 * heads), BF)],
        axis=0,
    )
    narrow = lax.rem(
        lax.broadcasted_iota(jnp.int32, (2 * heads, LANES), 0), heads
    ) - lax.broadcasted_iota(jnp.int32, (2 * heads, LANES), 1) // 64
    gather_delta = lax.broadcasted_iota(jnp.int32, (LANES, heads), 1) - lax.broadcasted_iota(
        jnp.int32, (LANES, heads), 0
    ) // 64

    def finish_f(p, carried):
        row_st, gc = carried
        cols = pl.ds(pl.multiple_of(p * LANES, LANES), LANES)
        gather = (gather_delta == 2 * p).astype(BF)
        h0 = goth_ref[p]
        gs = gs_ref[:, cols]
        y_st = mm(c_rows, h0)
        row_st += mm((gs.astype(F32) * y_st).astype(BF), gather)
        gc += mm_nt(gs, h0)
        hrow_ref[1:2, cols] = jnp.sum(
            x_ref[:, cols].astype(F32) * g_ref[:, cols].astype(F32), axis=0, keepdims=True
        )
        return row_st, gc

    def use_f(k, carried):
        peer = from_peer(k)
        pltpu.make_async_copy(h_ref.at[peer], goth_ref.at[peer], rh_sem.at[peer]).wait()
        return finish_f(peer, carried)

    zero_h = jnp.zeros((seq, heads), F32)
    row_st, g_c = lax.fori_loop(1, wide, use_f, finish_f(me, (zero_h, g_c)))

    def finish_g(p, carried):
        col_st, gb = carried
        cols = pl.ds(pl.multiple_of(p * LANES, LANES), LANES)
        r = (narrow == 2 * p).astype(BF)
        gather = (gather_delta == 2 * p).astype(BF)
        dh = gotp_ref[p]
        xs = xs_ref[:, cols]
        u_st = mm(b_rows, dh)
        rows = mm(skip_rows, r)
        gx = gxw_ref[:, cols] + mm(tail2, r) * u_st + rows[0:1] * g_ref[:, cols].astype(F32)
        xo_ref[:, cols] = gx.astype(BF)
        col_st += mm((xs.astype(F32) * u_st).astype(BF), gather)
        gb += mm_nt(xs, dh)
        ended = goth_ref[p].astype(F32) * jnp.exp(rows[1:2] + rows[2:3] + rows[3:4])
        ended += f_ref[p, :nst, :].astype(F32)
        hrow_ref[0:1, cols] = jnp.sum(ended * dh.astype(F32), axis=0, keepdims=True)
        pltpu.make_async_copy(xo_ref.at[:, cols], xg_hbm.at[:, cols], store_sem.at[0, p]).start()
        return col_st, gb

    def use_g(k, carried):
        peer = from_peer(k)
        pltpu.make_async_copy(p_ref.at[peer], gotp_ref.at[peer], rp_sem.at[peer]).wait()
        return finish_g(peer, carried)

    col_st, g_b = lax.fori_loop(1, wide, use_g, finish_g(me, (zero_h, g_b)))

    head_of = lax.broadcasted_iota(jnp.int32, (width, heads), 0) // 64
    gather_all = (head_of == lax.broadcasted_iota(jnp.int32, (width, heads), 1)).astype(BF)
    hr_hi, hr_lo = split2(hrow_ref[...])
    sums = mm(hr_hi, gather_all) + mm(hr_lo, gather_all)
    crossing, g_skip = sums[0:1], sums[1:2]

    row_all = rt_ref[:, 0, :].T + row_st
    col_all = col_ref[...] + col_st
    upper_all = (pos_r <= pos_c).astype(BF)
    d_hi, d_mid, d_lo = split3(row_all - col_all)
    d_log = mm(upper_all, d_hi) + mm(upper_all, d_mid) + mm(upper_all, d_lo) + crossing
    gate = 1.0 / (1.0 + jnp.exp(-dt_pre))
    ratio = jnp.where(dt > 0.0, gate / jnp.where(dt > 0.0, dt, 1.0), 1.0)
    g_dt = col_all * ratio + rate * d_log * gate
    d_bc = jnp.concatenate([g_b, g_c], axis=1).astype(BF)
    g_raw = g_dt.astype(BF)
    dproj_ref[:, : 2 * nst] = d_bc
    dproj_ref[:, 2 * nst :] = g_raw
    sib_d.start()
    g_alog = jnp.sum(d_log * log_rate, axis=0, keepdims=True)
    g_bias = jnp.sum(g_dt, axis=0, keepdims=True)
    hg_ref[...] = jnp.zeros_like(hg_ref)
    hg_ref[0:1, :heads] = g_alog
    hg_ref[1:2, :heads] = g_bias
    hg_ref[2:3, :heads] = g_skip
    sib_h.start()

    def emit(j, _):
        cols = pl.ds(pl.multiple_of(j * BLOCK, BLOCK), BLOCK)
        d_in = mm_nt(dproj_ref[:, : 2 * nst], wbc_ref[cols, :]) + mm(
            dproj_ref[:, 2 * nst :], wdt_ref[:, cols]
        )
        io_ref[:, cols] = d_in.astype(BF)
        pltpu.make_async_copy(io_ref.at[:, cols], ig_hbm.at[:, cols], store_sem.at[1, j]).start()
        return 0

    lax.fori_loop(0, blocks // 2, emit, 0)

    sib_in.wait_recv()
    sib_d.wait_recv()

    def weigh(step, _):
        c = lax.rem(mine // group + (step + 1) * 5, groups)
        part = pl.ds(c * group, group)
        ours = int_ref[core, part].reshape(group * 32, seq)
        theirs = sib_ref[part].reshape(group * 32, seq)
        w = mm(ours, dproj_ref[...]) + mm(theirs, sibd_ref[...])
        for i in range(group):
            slot = c * group + i
            at = w[i * 32 : (i + 1) * 32]
            out_ref[slot, 0:32, :] = at[:, :LANES].astype(BF)
            out_ref[slot, 32:64, :] = at[:, LANES : 2 * LANES].astype(BF)
            out_ref[slot, 64:80, : 2 * heads] = jnp.concatenate(
                [at[:16, 2 * LANES :], at[16:, 2 * LANES :]], axis=1
            ).astype(BF)

            @pl.when(slot != mine)
            def _():
                send_w(slot).start()

        return 0

    lax.fori_loop(0, groups, weigh, 0)

    ga, gi = mine // group, lax.rem(mine, group)
    sib_h.wait_recv()
    ha_ref[gi] = hg_ref[...] + hsib_ref[...]

    def send_a(i):
        return remote(ha_ref.at[gi], ha_ref.at[gi], hs_sem.at[0, i], hr_sem.at[0, gi], at_slot(ga * group + i))

    def send_b(i):
        return remote(hb_ref.at[ga], hb_ref.at[ga], hs_sem.at[1, i], hr_sem.at[1, ga], at_slot(i * group + gi))

    def start_a(k, _):
        send_a(lax.rem(gi + k, group)).start()
        return 0

    lax.fori_loop(1, group, start_a, 0)
    lax.fori_loop(blocks // 2, blocks, emit, 0)

    def end_a(k, _):
        i = lax.rem(gi + k, group)
        pltpu.make_async_copy(ha_ref.at[i], ha_ref.at[i], hr_sem.at[0, i]).wait()
        send_a(i).wait_send()
        return 0

    lax.fori_loop(1, group, end_a, 0)
    hb_ref[ga] = jnp.sum(ha_ref[...], axis=0)

    def start_b(k, _):
        send_b(lax.rem(ga + k, groups)).start()
        return 0

    lax.fori_loop(1, groups, start_b, 0)

    def drain(k, _):
        f_peer = to_peer(k)
        send_f(f_peer).wait_send()
        send_g(f_peer).wait_send()
        send_h(f_peer).wait_send()
        send_p(f_peer).wait_send()
        return 0

    lax.fori_loop(1, wide, drain, 0)

    def stored_x(p, _):
        cols = pl.ds(pl.multiple_of(p * LANES, LANES), LANES)
        pltpu.make_async_copy(xo_ref.at[:, cols], xg_hbm.at[:, cols], store_sem.at[0, p]).wait()
        return 0

    lax.fori_loop(0, pairs, stored_x, 0)

    def stored_i(j, _):
        cols = pl.ds(pl.multiple_of(j * BLOCK, BLOCK), BLOCK)
        pltpu.make_async_copy(io_ref.at[:, cols], ig_hbm.at[:, cols], store_sem.at[1, j]).wait()
        return 0

    lax.fori_loop(0, blocks, stored_i, 0)
    sib_in.wait_send()
    sib_d.wait_send()
    sib_h.wait_send()

    def end_b(k, _):
        i = lax.rem(ga + k, groups)
        pltpu.make_async_copy(hb_ref.at[i], hb_ref.at[i], hr_sem.at[1, i]).wait()
        send_b(i).wait_send()
        return 0

    lax.fori_loop(1, groups, end_b, 0)
    rows = jnp.sum(hb_ref[...], axis=0)
    at = lax.broadcasted_iota(jnp.int32, rows.shape, 1)
    per = heads // wide
    for i in range(per):
        picked = jnp.sum(jnp.where(at == me * per + i, rows, 0.0), axis=1, keepdims=True)
        head_out[:, i : i + 1] = picked[:3]

    def total(k, acc):
        slot = lax.rem(mine + (slots - k) * 5, slots)
        pltpu.make_async_copy(out_ref.at[slot], got_ref.at[slot], rw_sem.at[slot]).wait()
        return acc + got_ref[slot].astype(F32)

    acc = lax.fori_loop(1, slots, total, out_ref[mine].astype(F32))
    wbc_out[:, :LANES] = acc[0:32]
    wbc_out[:, LANES:] = acc[32:64]
    wdt_out[0:16, :] = acc[64:80, :heads]
    wdt_out[16:32, :] = acc[64:80, heads : 2 * heads]

    def done(k, _):
        send_w(lax.rem(mine + k, slots)).wait_send()
        return 0

    lax.fori_loop(1, slots, done, 0)


def local(wide, dp, layer_input, inner_acts, w_bc, w_dt, a_log, dt_bias, d_skip, out_grad):
    seq, width = layer_input.shape[1:]
    heads = a_log.shape[0]
    nst = w_bc.shape[1] // 2
    slots = wide * dp // 2
    rows = width // (wide * dp)
    any_spec = pl.BlockSpec(memory_space=pl.ANY)
    vmem = pl.BlockSpec(memory_space=pltpu.VMEM)
    dma = pltpu.SemaphoreType.DMA
    v = pltpu.VMEM
    x_grad, input_grad, wbc_grad, wdt_grad, head_grads = pl.pallas_call(
        functools.partial(scan_kernel, wide, dp),
        out_shape=(
            jax.ShapeDtypeStruct((seq, width), BF),
            jax.ShapeDtypeStruct((seq, width), BF),
            jax.ShapeDtypeStruct((rows, 2 * nst), F32),
            jax.ShapeDtypeStruct((rows, heads), F32),
            jax.ShapeDtypeStruct((3, heads // wide), F32),
        ),
        in_specs=[any_spec] * 5 + [vmem] * 3,
        out_specs=(any_spec, any_spec, vmem, vmem, vmem),
        scratch_shapes=[
            v((seq, width), BF),
            v((seq, width), BF),
            v((seq, width), BF),
            v((width, 2 * nst), BF),
            v((heads, width), BF),
            v((wide, nst + 16, LANES), BF),
            v((wide, nst, LANES), BF),
            v((wide, nst + 16, LANES), BF),
            v((wide, nst, LANES), BF),
            v((wide, nst, LANES), BF),
            v((wide, nst, LANES), BF),
            v((wide, nst, LANES), BF),
            v((wide, nst, LANES), BF),
            v((seq, width), BF),
            v((seq, width), BF),
            v((seq, width), F32),
            v((2, slots, 32, seq), BF),
            v((slots, 32, seq), BF),
            v((seq, seq), F32),
            v((seq, seq), F32),
            v((heads, seq), F32),
            v((heads, 1, seq), F32),
            v((seq, heads), F32),
            v((2, width), F32),
            v((seq, width), BF),
            v((seq, width), BF),
            v((seq, 2 * nst + heads), BF),
            v((seq, 2 * nst + heads), BF),
            v((8, LANES), F32),
            v((8, LANES), F32),
            v((8, 8, LANES), F32),
            v((slots // 8, 8, LANES), F32),
            v((slots, 80, LANES), BF),
            v((slots, 80, LANES), BF),
            dma((5,)),
            dma((2, width // LANES)),
            dma((3,)),
            dma((3,)),
            dma((2, 8)),
            dma((2, 8)),
        ]
        + [dma((wide,))] * 8
        + [dma((slots,))] * 2,
        compiler_params=pltpu.CompilerParams(
            collective_id=0, has_side_effects=True, vmem_limit_bytes=56 * 1024 * 1024
        ),
        cost_estimate=pl.CostEstimate(
            flops=30 * seq * width * 256, bytes_accessed=8 * seq * width, transcendentals=0
        ),
        name="scan_backward",
    )(
        layer_input[0], inner_acts[0], out_grad[0], w_bc, w_dt.T,
        a_log[None], dt_bias[None], d_skip[None],
    )
    return x_grad[None], input_grad[None], wbc_grad, wdt_grad, head_grads


def solution(mesh):
    in_specs = (
        P("dp", "wide", None),
        P("dp", "wide", None),
        P(),
        P(),
        P(),
        P(),
        P(),
        P("dp", "wide", None),
    )
    out_specs = (
        P("dp", "wide", None),
        P("dp", "wide", None),
        P(("wide", "dp"), None),
        P(("wide", "dp"), None),
        P(None, "wide"),
    )
    return jax.shard_map(
        functools.partial(local, mesh.shape["wide"], mesh.shape["dp"]),
        mesh=mesh,
        in_specs=in_specs,
        out_specs=out_specs,
        check_vma=False,
    )
```

```python
import functools

import jax
import jax.numpy as jnp
from jax import lax
from jax.experimental import pallas as pl
from jax.experimental.pallas import tpu as pltpu
from jax.sharding import PartitionSpec as P

MESH = pl.DeviceIdType.MESH
BF = jnp.bfloat16
F32 = jnp.float32
LANES = 128
BLOCK = 512
STRIDE = 13


def mm(a, b):
    return jnp.dot(a, b, preferred_element_type=F32)


def mm_nt(a, b):
    return lax.dot_general(a, b, (((1,), (1,)), ((), ())), preferred_element_type=F32)


def split2(v):
    hi = v.astype(BF)
    return hi, (v - hi.astype(F32)).astype(BF)


def split3(v):
    hi = v.astype(BF)
    rest = v - hi.astype(F32)
    mid = rest.astype(BF)
    return hi, mid, (rest - mid.astype(F32)).astype(BF)


def scan_kernel(
    wide, dp, in_hbm, x_hbm, g_hbm, wbc_hbm, wdt_hbm, alog_ref, bias_ref, skip_ref,
    xg_hbm, ig_hbm, wbc_out, wdt_out, head_out,
    in_ref, x_ref, g_ref, wbc_ref, wdt_ref, f_ref, gt_ref, gotf_ref, gotg_ref, h_ref, p_ref,
    goth_ref, gotp_ref, xs_ref, gs_ref, gxw_ref, int_ref, sib_ref, nt_ref, st_ref, lt_ref, rt_ref,
    col_ref, hrow_ref, xo_ref, io_ref, dproj_ref, sibd_ref, hg_ref, hsib_ref, ha_ref, hb_ref,
    out_ref, got_ref,
    load_sem, store_sem, sib_send, sib_recv, hs_sem, hr_sem,
    sf_sem, rf_sem, sg_sem, rg_sem, sh_sem, rh_sem, sp_sem, rp_sem, sw_sem, rw_sem,
):
    me = lax.axis_index("wide")
    place = lax.axis_index("dp")
    core = lax.rem(place, 2)
    other = 1 - core
    sets = dp // 2
    slots = wide * sets
    mine = me * sets + place // 2
    seq, width = in_ref.shape
    heads = alog_ref.shape[1]
    half = seq // 2
    nst = wbc_ref.shape[1] // 2
    owners = BLOCK // LANES
    blocks = width // BLOCK
    per_block = BLOCK // 64
    pairs = width // LANES
    group = 8
    groups = slots // group
    sibling = {"wide": me, "dp": place - core + other}

    def at_slot(slot):
        return {"wide": slot // sets, "dp": lax.rem(slot, sets) * 2 + core}

    def to_peer(k):
        return lax.rem(me + k * STRIDE, wide)

    def from_peer(k):
        return lax.rem(me + (wide - k) * STRIDE, wide)

    barrier = pltpu.get_barrier_semaphore()
    pl.semaphore_signal(barrier, inc=1, device_id=sibling, device_id_type=MESH)

    def greet(k, _):
        pl.semaphore_signal(
            barrier, inc=1, device_id=at_slot(lax.rem(mine + k, slots)), device_id_type=MESH
        )
        return 0

    lax.fori_loop(1, slots, greet, 0)

    loads = [
        pltpu.make_async_copy(src, dst, load_sem.at[i])
        for i, (src, dst) in enumerate(
            ((in_hbm, in_ref), (wbc_hbm, wbc_ref), (wdt_hbm, wdt_ref), (x_hbm, x_ref), (g_hbm, g_ref))
        )
    ]
    for load in loads:
        load.start()

    delta = lax.rem(
        lax.broadcasted_iota(jnp.int32, (2 * heads, BLOCK), 0), heads
    ) - lax.broadcasted_iota(jnp.int32, (2 * heads, BLOCK), 1) // 64

    def spread(j):
        return (delta == j * per_block).astype(BF)

    def remote(src, dst, send, recv, target):
        return pltpu.make_async_remote_copy(
            src_ref=src, dst_ref=dst, send_sem=send, recv_sem=recv, device_id=target,
            device_id_type=MESH,
        )

    def send_f(peer):
        return remote(f_ref.at[peer], gotf_ref.at[me], sf_sem.at[peer], rf_sem.at[me], {"wide": peer})

    def send_g(peer):
        return remote(gt_ref.at[peer], gotg_ref.at[me], sg_sem.at[peer], rg_sem.at[me], {"wide": peer})

    def send_h(peer):
        return remote(h_ref.at[peer], goth_ref.at[me], sh_sem.at[peer], rh_sem.at[me], {"wide": peer})

    def send_p(peer):
        return remote(p_ref.at[peer], gotp_ref.at[me], sp_sem.at[peer], rp_sem.at[me], {"wide": peer})

    def send_w(slot):
        return remote(out_ref.at[slot], got_ref.at[mine], sw_sem.at[slot], rw_sem.at[mine], at_slot(slot))

    sib_in = remote(int_ref.at[other], sib_ref, sib_send.at[0], sib_recv.at[0], sibling)
    sib_d = remote(dproj_ref, sibd_ref, sib_send.at[1], sib_recv.at[1], sibling)
    sib_h = remote(hg_ref, hsib_ref, sib_send.at[2], sib_recv.at[2], sibling)

    loads[0].wait()
    loads[1].wait()
    bc = mm(in_ref[...], wbc_ref[...]).astype(BF)
    loads[2].wait()
    dt_raw = mm_nt(in_ref[...], wdt_ref[...]).astype(BF).astype(F32)
    b_rows = bc[:, :nst]
    c_rows = bc[:, nst:]
    b_t = b_rows.astype(F32).T.astype(BF)
    c_t = c_rows.astype(F32).T.astype(BF)
    dt_pre = dt_raw + bias_ref[...]
    dt = jnp.maximum(dt_pre, 0.0) + jnp.log1p(jnp.exp(-jnp.abs(dt_pre)))
    rate = -jnp.exp(alog_ref[...])
    log_rate = dt * rate
    pos_r = lax.broadcasted_iota(jnp.int32, (seq, seq), 0)
    pos_c = lax.broadcasted_iota(jnp.int32, (seq, seq), 1)
    lower = (pos_r >= pos_c).astype(BF)
    lr_hi, lr_mid, lr_lo = split3(log_rate)
    cumul = mm(lower, lr_hi) + mm(lower, lr_mid) + mm(lower, lr_lo)
    last = cumul[seq - 1 :, :]
    tail = dt * jnp.exp(last - cumul)
    tail2 = jnp.concatenate(split2(tail), axis=1)
    lq_hi, lq_mid, lq_lo = split3(last)
    none = jnp.zeros((1, heads), BF)
    lq_rows = jnp.concatenate(
        [jnp.concatenate([v, none], axis=1) for v in (lq_hi, lq_mid, lq_lo)]
        + [jnp.zeros((13, 2 * heads), BF)],
        axis=0,
    )

    def block_at(step):
        return lax.rem(me // owners + (step + 1) * 5, blocks)

    loads[3].wait()
    pl.semaphore_wait(barrier, slots)

    def fresh_f(step, _):
        j = block_at(step)
        cols = pl.ds(pl.multiple_of(j * BLOCK, BLOCK), BLOCK)
        r = spread(j)
        xs = (x_ref[:, cols].astype(F32) * mm(tail2, r)).astype(BF)
        xs_ref[:, cols] = xs
        f_t = mm(b_t, xs).astype(BF)
        lq = mm(lq_rows, r).astype(BF)
        for i in range(owners):
            lanes = slice(i * LANES, (i + 1) * LANES)
            peer = j * owners + i
            f_ref[peer, :nst, :] = f_t[:, lanes]
            f_ref[peer, nst:, :] = lq[:, lanes]

            @pl.when(peer != me)
            def _():
                send_f(peer).start()

        return 0

    lax.fori_loop(0, blocks, fresh_f, 0)

    head_exp = jnp.exp(cumul)
    exp2 = jnp.concatenate(split2(head_exp), axis=1)
    loads[4].wait()

    def fresh_g(step, _):
        j = block_at(step)
        cols = pl.ds(pl.multiple_of(j * BLOCK, BLOCK), BLOCK)
        gs = (g_ref[:, cols].astype(F32) * mm(exp2, spread(j))).astype(BF)
        gs_ref[:, cols] = gs
        g_t = mm(c_t, gs).astype(BF)
        for i in range(owners):
            peer = j * owners + i
            gt_ref[peer] = g_t[:, i * LANES : (i + 1) * LANES]

            @pl.when(peer != me)
            def _():
                send_g(peer).start()

        return 0

    lax.fori_loop(0, blocks, fresh_g, 0)

    lt_ref[...] = cumul.T
    u3 = jnp.concatenate(split3(jnp.log(jnp.maximum(dt, 1e-37)) - cumul), axis=1)
    st_ref[...] = mm_nt(b_rows, c_rows)
    lane = lax.broadcasted_iota(jnp.int32, (seq, LANES), 1)
    lane_head = lax.broadcasted_iota(jnp.int32, (half, heads), 1)
    upper = lax.broadcasted_iota(jnp.int32, (half, half), 0) <= lax.broadcasted_iota(
        jnp.int32, (half, half), 1
    )
    row_head = lax.rem(lax.broadcasted_iota(jnp.int32, (3 * heads, LANES), 0), heads)
    nt_ref[...] = jnp.zeros_like(nt_ref)
    col_ref[...] = jnp.zeros_like(col_ref)

    def within(pair, _):
        cols = pl.ds(pl.multiple_of(pair * LANES, LANES), LANES)
        xk = x_ref[:, cols]
        gk = g_ref[:, cols]
        total_lo = jnp.zeros((half, LANES), F32)
        total_hi = jnp.zeros((half, LANES), F32)
        for side in range(2):
            h = pair * 2 + side
            mine_lane = (lane < 64) if side == 0 else (lane >= 64)
            xm = jnp.where(mine_lane, xk, jnp.zeros_like(xk))
            gm = jnp.where(mine_lane, gk, jnp.zeros_like(gk))
            u = mm(u3, (row_head == h).astype(BF))
            lt = lt_ref[pl.ds(h, 1), :]
            w0 = mm_nt(xm[:half], gk)
            w1 = mm_nt(xm[half:], gk[half:])
            a00 = jnp.where(upper, jnp.exp(u[:half] + lt[:, :half]), 0.0)
            a01 = jnp.exp(u[:half] + lt[:, half:])
            a11 = jnp.where(upper, jnp.exp(u[half:] + lt[:, half:]), 0.0)
            s00 = st_ref[:half, :half]
            s01 = st_ref[:half, half:]
            s11 = st_ref[half:, half:]
            p00 = a00 * w0[:, :half]
            p01 = a01 * w0[:, half:]
            p11 = a11 * w1
            nt_ref[:half, :half] += p00
            nt_ref[:half, half:] += p01
            nt_ref[half:, half:] += p11
            total_lo += mm((a00 * s00).astype(BF), gm[:half]) + mm((a01 * s01).astype(BF), gm[half:])
            total_hi += mm((a11 * s11).astype(BF), gm[half:])
            z00 = p00 * s00
            z01 = p01 * s01
            z11 = p11 * s11
            rt_ref[h, :, :half] = jnp.sum(z00, axis=0, keepdims=True)
            rt_ref[h, :, half:] = jnp.sum(z01 + z11, axis=0, keepdims=True)
            col_ref[:half, :] += jnp.where(
                lane_head == h, jnp.sum(z00 + z01, axis=1, keepdims=True), 0.0
            )
            col_ref[half:, :] += jnp.where(
                lane_head == h, jnp.sum(z11, axis=1, keepdims=True), 0.0
            )
        hrow_ref[1:2, cols] = jnp.sum(xk.astype(F32) * gk.astype(F32), axis=0, keepdims=True)
        gxw_ref[:half, cols] = total_lo
        gxw_ref[half:, cols] = total_hi
        turned = in_ref[:, cols].astype(F32).T.astype(BF)
        for i in range(dp):
            int_ref[i % 2, pair * sets + i // 2] = turned[i * 32 : (i + 1) * 32]
        return 0

    first_part = (pairs * 5) // 8
    lax.fori_loop(0, first_part, within, 0)

    def decay_of(i):
        parts = gotf_ref[i, nst:, :].astype(F32)
        return jnp.exp(parts[0:1] + parts[1:2] + parts[2:3])

    def take_f(k, _):
        peer = from_peer(k)
        pltpu.make_async_copy(f_ref.at[peer], gotf_ref.at[peer], rf_sem.at[peer]).wait()
        return 0

    gotf_ref[me] = f_ref[me]
    lax.fori_loop(1, wide, take_f, 0)

    def advance_f(i, state):
        h_ref[i] = state.astype(BF)
        return state * decay_of(i) + gotf_ref[i, :nst, :].astype(F32)

    start = jnp.zeros((nst, LANES), F32)
    lax.fori_loop(0, wide, advance_f, start)

    def give_h(step, _):
        for i in range(owners):
            peer = block_at(step) * owners + i

            @pl.when(peer != me)
            def _():
                send_h(peer).start()

        return 0

    lax.fori_loop(0, blocks, give_h, 0)
    goth_ref[me] = h_ref[me]

    lax.fori_loop(first_part, pairs, within, 0)
    sib_in.start()

    def take_g(k, _):
        peer = from_peer(k)
        pltpu.make_async_copy(gt_ref.at[peer], gotg_ref.at[peer], rg_sem.at[peer]).wait()
        return 0

    gotg_ref[me] = gt_ref[me]
    lax.fori_loop(1, wide, take_g, 0)

    def advance_g(k, pull):
        i = wide - 1 - k
        p_ref[i] = pull.astype(BF)
        return pull * decay_of(i) + gotg_ref[i].astype(F32)

    lax.fori_loop(0, wide, advance_g, start)

    def give_p(step, _):
        for i in range(owners):
            peer = block_at(step) * owners + i

            @pl.when(peer != me)
            def _():
                send_p(peer).start()

        return 0

    lax.fori_loop(0, blocks, give_p, 0)
    gotp_ref[me] = p_ref[me]

    n_low = nt_ref[...].astype(BF)
    g_b = mm(n_low, c_rows)
    g_c = mm(nt_ref[...].T.astype(BF), b_rows)

    skip_hi, skip_lo = split2(skip_ref[...])
    skip_rows = jnp.concatenate(
        [jnp.concatenate([skip_hi, skip_lo], axis=1)]
        + [jnp.concatenate([v, none], axis=1) for v in (lq_hi, lq_mid, lq_lo)]
        + [jnp.zeros((12, 2 * heads), BF)],
        axis=0,
    )
    gather_delta = lax.broadcasted_iota(jnp.int32, (BLOCK, heads), 1) - lax.broadcasted_iota(
        jnp.int32, (BLOCK, heads), 0
    ) // 64

    def block_from(step):
        return lax.rem(me // owners + (blocks - 1 - step) * 5, blocks)

    def joined(ref, j):
        return jnp.concatenate([ref[j * owners + i, :nst, :] for i in range(owners)], axis=1)

    def finish_f(step, carried):
        row_st, gc = carried
        j = block_from(step)
        for i in range(owners):
            peer = j * owners + i

            @pl.when(peer != me)
            def _():
                pltpu.make_async_copy(h_ref.at[peer], goth_ref.at[peer], rh_sem.at[peer]).wait()

        cols = pl.ds(pl.multiple_of(j * BLOCK, BLOCK), BLOCK)
        gather = (gather_delta == j * per_block).astype(BF)
        h0 = joined(goth_ref, j)
        gs = gs_ref[:, cols]
        y_st = mm(c_rows, h0)
        row_st += mm((gs.astype(F32) * y_st).astype(BF), gather)
        gc += mm_nt(gs, h0)
        return row_st, gc

    zero_h = jnp.zeros((seq, heads), F32)
    row_st, g_c = lax.fori_loop(0, blocks, finish_f, (zero_h, g_c))

    def finish_g(step, carried):
        col_st, gb = carried
        j = block_from(step)
        for i in range(owners):
            peer = j * owners + i

            @pl.when(peer != me)
            def _():
                pltpu.make_async_copy(p_ref.at[peer], gotp_ref.at[peer], rp_sem.at[peer]).wait()

        cols = pl.ds(pl.multiple_of(j * BLOCK, BLOCK), BLOCK)
        r = spread(j)
        gather = (gather_delta == j * per_block).astype(BF)
        dh = joined(gotp_ref, j)
        xs = xs_ref[:, cols]
        u_st = mm(b_rows, dh)
        rows = mm(skip_rows, r)
        gx = gxw_ref[:, cols] + mm(tail2, r) * u_st + rows[0:1] * g_ref[:, cols].astype(F32)
        xo_ref[:, cols] = gx.astype(BF)
        col_st += mm((xs.astype(F32) * u_st).astype(BF), gather)
        gb += mm_nt(xs, dh)
        ended = joined(goth_ref, j).astype(F32) * jnp.exp(rows[1:2] + rows[2:3] + rows[3:4])
        ended += joined(f_ref, j).astype(F32)
        hrow_ref[0:1, cols] = jnp.sum(ended * dh.astype(F32), axis=0, keepdims=True)
        pltpu.make_async_copy(xo_ref.at[:, cols], xg_hbm.at[:, cols], store_sem.at[0, j]).start()
        return col_st, gb

    col_st, g_b = lax.fori_loop(0, blocks, finish_g, (zero_h, g_b))

    head_of = lax.broadcasted_iota(jnp.int32, (width, heads), 0) // 64
    gather_all = (head_of == lax.broadcasted_iota(jnp.int32, (width, heads), 1)).astype(BF)
    hr_hi, hr_lo = split2(hrow_ref[...])
    sums = mm(hr_hi, gather_all) + mm(hr_lo, gather_all)
    crossing, g_skip = sums[0:1], sums[1:2]

    row_all = rt_ref[:, 0, :].T + row_st
    col_all = col_ref[...] + col_st
    upper_all = (pos_r <= pos_c).astype(BF)
    d_hi, d_mid, d_lo = split3(row_all - col_all)
    d_log = mm(upper_all, d_hi) + mm(upper_all, d_mid) + mm(upper_all, d_lo) + crossing
    gate = 1.0 / (1.0 + jnp.exp(-dt_pre))
    ratio = jnp.where(dt > 0.0, gate / jnp.where(dt > 0.0, dt, 1.0), 1.0)
    g_dt = col_all * ratio + rate * d_log * gate
    d_bc = jnp.concatenate([g_b, g_c], axis=1).astype(BF)
    g_raw = g_dt.astype(BF)
    dproj_ref[:, : 2 * nst] = d_bc
    dproj_ref[:, 2 * nst :] = g_raw
    sib_d.start()
    g_alog = jnp.sum(d_log * log_rate, axis=0, keepdims=True)
    g_bias = jnp.sum(g_dt, axis=0, keepdims=True)
    hg_ref[...] = jnp.zeros_like(hg_ref)
    hg_ref[0:1, :heads] = g_alog
    hg_ref[1:2, :heads] = g_bias
    hg_ref[2:3, :heads] = g_skip
    sib_h.start()

    def emit(j, _):
        cols = pl.ds(pl.multiple_of(j * BLOCK, BLOCK), BLOCK)
        d_in = mm_nt(dproj_ref[:, : 2 * nst], wbc_ref[cols, :]) + mm(
            dproj_ref[:, 2 * nst :], wdt_ref[:, cols]
        )
        io_ref[:, cols] = d_in.astype(BF)
        pltpu.make_async_copy(io_ref.at[:, cols], ig_hbm.at[:, cols], store_sem.at[1, j]).start()
        return 0

    lax.fori_loop(0, blocks // 2, emit, 0)

    sib_in.wait_recv()
    sib_d.wait_recv()

    def weigh(step, _):
        c = lax.rem(mine // group + (step + 1) * 5, groups)
        part = pl.ds(c * group, group)
        ours = int_ref[core, part].reshape(group * 32, seq)
        theirs = sib_ref[part].reshape(group * 32, seq)
        w = mm(ours, dproj_ref[...]) + mm(theirs, sibd_ref[...])
        for i in range(group):
            slot = c * group + i
            at = w[i * 32 : (i + 1) * 32]
            out_ref[slot, 0:32, :] = at[:, :LANES].astype(BF)
            out_ref[slot, 32:64, :] = at[:, LANES : 2 * LANES].astype(BF)
            out_ref[slot, 64:80, : 2 * heads] = jnp.concatenate(
                [at[:16, 2 * LANES :], at[16:, 2 * LANES :]], axis=1
            ).astype(BF)

            @pl.when(slot != mine)
            def _():
                send_w(slot).start()

        return 0

    lax.fori_loop(0, groups, weigh, 0)

    ga, gi = mine // group, lax.rem(mine, group)
    sib_h.wait_recv()
    ha_ref[gi] = hg_ref[...] + hsib_ref[...]

    def send_a(i):
        return remote(ha_ref.at[gi], ha_ref.at[gi], hs_sem.at[0, i], hr_sem.at[0, gi], at_slot(ga * group + i))

    def send_b(i):
        return remote(hb_ref.at[ga], hb_ref.at[ga], hs_sem.at[1, i], hr_sem.at[1, ga], at_slot(i * group + gi))

    def start_a(k, _):
        send_a(lax.rem(gi + k, group)).start()
        return 0

    lax.fori_loop(1, group, start_a, 0)
    lax.fori_loop(blocks // 2, blocks, emit, 0)

    def end_a(k, _):
        i = lax.rem(gi + k, group)
        pltpu.make_async_copy(ha_ref.at[i], ha_ref.at[i], hr_sem.at[0, i]).wait()
        send_a(i).wait_send()
        return 0

    lax.fori_loop(1, group, end_a, 0)
    hb_ref[ga] = jnp.sum(ha_ref[...], axis=0)

    def start_b(k, _):
        send_b(lax.rem(ga + k, groups)).start()
        return 0

    lax.fori_loop(1, groups, start_b, 0)

    def drain(k, _):
        f_peer = to_peer(k)
        send_f(f_peer).wait_send()
        send_g(f_peer).wait_send()
        send_h(f_peer).wait_send()
        send_p(f_peer).wait_send()
        return 0

    lax.fori_loop(1, wide, drain, 0)

    def stored(j, _):
        cols = pl.ds(pl.multiple_of(j * BLOCK, BLOCK), BLOCK)
        pltpu.make_async_copy(xo_ref.at[:, cols], xg_hbm.at[:, cols], store_sem.at[0, j]).wait()
        pltpu.make_async_copy(io_ref.at[:, cols], ig_hbm.at[:, cols], store_sem.at[1, j]).wait()
        return 0

    lax.fori_loop(0, blocks, stored, 0)
    sib_in.wait_send()
    sib_d.wait_send()
    sib_h.wait_send()

    def end_b(k, _):
        i = lax.rem(ga + k, groups)
        pltpu.make_async_copy(hb_ref.at[i], hb_ref.at[i], hr_sem.at[1, i]).wait()
        send_b(i).wait_send()
        return 0

    lax.fori_loop(1, groups, end_b, 0)
    rows = jnp.sum(hb_ref[...], axis=0)
    at = lax.broadcasted_iota(jnp.int32, rows.shape, 1)
    per = heads // wide
    for i in range(per):
        picked = jnp.sum(jnp.where(at == me * per + i, rows, 0.0), axis=1, keepdims=True)
        for r in range(3):
            head_out[i : i + 1, r : r + 1] = picked[r : r + 1]

    def total(k, acc):
        slot = lax.rem(mine + (slots - k) * 5, slots)
        pltpu.make_async_copy(out_ref.at[slot], got_ref.at[slot], rw_sem.at[slot]).wait()
        return acc + got_ref[slot].astype(F32)

    acc = lax.fori_loop(1, slots, total, out_ref[mine].astype(F32))
    wbc_out[:, :LANES] = acc[0:32]
    wbc_out[:, LANES:] = acc[32:64]
    wdt_out[0:16, :] = acc[64:80, :heads]
    wdt_out[16:32, :] = acc[64:80, heads : 2 * heads]

    def done(k, _):
        send_w(lax.rem(mine + k, slots)).wait_send()
        return 0

    lax.fori_loop(1, slots, done, 0)


def place_kernel(x_in, i_in, b_in, d_in, h_in, x_out, i_out, b_out, d_out, h_out, big, small):
    copies = []
    for a, (src, dst) in enumerate(((x_in, x_out), (i_in, i_out))):
        rows = src.shape[0] // 4
        for q in range(4):
            part = pl.ds(q * rows, rows)
            copies.append(pltpu.make_async_copy(src.at[part], dst.at[part], big.at[a, q]))
    for a, (src, dst) in enumerate(((b_in, b_out), (d_in, d_out), (h_in, h_out))):
        copies.append(pltpu.make_async_copy(src, dst, small.at[a]))
    for c in copies:
        c.start()
    for c in copies:
        c.wait()


def local(wide, dp, layer_input, inner_acts, w_bc, w_dt, a_log, dt_bias, d_skip, out_grad):
    seq, width = layer_input.shape[1:]
    heads = a_log.shape[0]
    nst = w_bc.shape[1] // 2
    slots = wide * dp // 2
    rows = width // (wide * dp)
    any_spec = pl.BlockSpec(memory_space=pl.ANY)
    vmem = pl.BlockSpec(memory_space=pltpu.VMEM)
    dma = pltpu.SemaphoreType.DMA
    v = pltpu.VMEM
    x_grad, input_grad, wbc_grad, wdt_grad, head_grads = pl.pallas_call(
        functools.partial(scan_kernel, wide, dp),
        out_shape=(
            jax.ShapeDtypeStruct((seq, width), BF),
            jax.ShapeDtypeStruct((seq, width), BF),
            jax.ShapeDtypeStruct((rows, 2 * nst), F32),
            jax.ShapeDtypeStruct((rows, heads), F32),
            jax.ShapeDtypeStruct((heads // wide, 3), F32),
        ),
        in_specs=[any_spec] * 5 + [vmem] * 3,
        out_specs=(any_spec, any_spec, vmem, vmem, vmem),
        scratch_shapes=[
            v((seq, width), BF),
            v((seq, width), BF),
            v((seq, width), BF),
            v((width, 2 * nst), BF),
            v((heads, width), BF),
            v((wide, nst + 16, LANES), BF),
            v((wide, nst, LANES), BF),
            v((wide, nst + 16, LANES), BF),
            v((wide, nst, LANES), BF),
            v((wide, nst, LANES), BF),
            v((wide, nst, LANES), BF),
            v((wide, nst, LANES), BF),
            v((wide, nst, LANES), BF),
            v((seq, width), BF),
            v((seq, width), BF),
            v((seq, width), F32),
            v((2, slots, 32, seq), BF),
            v((slots, 32, seq), BF),
            v((seq, seq), F32),
            v((seq, seq), F32),
            v((heads, seq), F32),
            v((heads, 1, seq), F32),
            v((seq, heads), F32),
            v((2, width), F32),
            v((seq, width), BF),
            v((seq, width), BF),
            v((seq, 2 * nst + heads), BF),
            v((seq, 2 * nst + heads), BF),
            v((8, LANES), F32),
            v((8, LANES), F32),
            v((8, 8, LANES), F32),
            v((slots // 8, 8, LANES), F32),
            v((slots, 80, LANES), BF),
            v((slots, 80, LANES), BF),
            dma((5,)),
            dma((2, width // BLOCK)),
            dma((3,)),
            dma((3,)),
            dma((2, 8)),
            dma((2, 8)),
        ]
        + [dma((wide,))] * 8
        + [dma((slots,))] * 2,
        compiler_params=pltpu.CompilerParams(
            collective_id=0, has_side_effects=True, vmem_limit_bytes=56 * 1024 * 1024
        ),
        cost_estimate=pl.CostEstimate(
            flops=30 * seq * width * 256, bytes_accessed=8 * seq * width, transcendentals=0
        ),
        name="scan_backward",
    )(
        layer_input[0], inner_acts[0], out_grad[0], w_bc, w_dt.T,
        a_log[None], dt_bias[None], d_skip[None],
    )
    x_grad, input_grad, wbc_grad, wdt_grad, head_grads = pl.pallas_call(
        place_kernel,
        out_shape=tuple(
            jax.ShapeDtypeStruct(a.shape, a.dtype)
            for a in (x_grad, input_grad, wbc_grad, wdt_grad, head_grads)
        ),
        in_specs=[any_spec] * 5,
        out_specs=[any_spec] * 5,
        scratch_shapes=[dma((2, 4)), dma((3,))],
        compiler_params=pltpu.CompilerParams(vmem_limit_bytes=60 * 1024 * 1024),
        name="place_results",
    )(x_grad, input_grad, wbc_grad, wdt_grad, head_grads)
    return x_grad[None], input_grad[None], wbc_grad, wdt_grad, head_grads.T


def solution(mesh):
    in_specs = (
        P("dp", "wide", None),
        P("dp", "wide", None),
        P(),
        P(),
        P(),
        P(),
        P(),
        P("dp", "wide", None),
    )
    out_specs = (
        P("dp", "wide", None),
        P("dp", "wide", None),
        P(("wide", "dp"), None),
        P(("wide", "dp"), None),
        P(None, "wide"),
    )
    return jax.shard_map(
        functools.partial(local, mesh.shape["wide"], mesh.shape["dp"]),
        mesh=mesh,
        in_specs=in_specs,
        out_specs=out_specs,
        check_vma=False,
    )
```

```python
import functools

import jax
import jax.numpy as jnp
from jax import lax
from jax.experimental import pallas as pl
from jax.experimental.pallas import tpu as pltpu
from jax.sharding import PartitionSpec as P

MESH = pl.DeviceIdType.MESH
BF = jnp.bfloat16
F32 = jnp.float32
LANES = 128
BLOCK = 512
STRIDE = 13
STRIDE_W = 27
PIECES = 8


def mm(a, b):
    return jnp.dot(a, b, preferred_element_type=F32)


def mm_nt(a, b):
    return lax.dot_general(a, b, (((1,), (1,)), ((), ())), preferred_element_type=F32)


def split2(v):
    hi = v.astype(BF)
    return hi, (v - hi.astype(F32)).astype(BF)


def split3(v):
    hi = v.astype(BF)
    rest = v - hi.astype(F32)
    mid = rest.astype(BF)
    return hi, mid, (rest - mid.astype(F32)).astype(BF)


def scan_kernel(
    wide, dp, in_hbm, x_hbm, g_hbm, wbc_hbm, wdt_hbm, alog_ref, bias_ref, skip_ref,
    xg_hbm, ig_hbm, wbc_out, wdt_out, head_out,
    in_ref, x_ref, g_ref, wbc_ref, wdt_ref, f_ref, gt_ref, gotf_ref, gotg_ref, h_ref, p_ref,
    goth_ref, gotp_ref, xs_ref, gs_ref, gxw_ref, int_ref, sib_ref, nt_ref, st_ref, lt_ref, rt_ref,
    col_ref, hrow_ref, xo_ref, io_ref, mine_c, mine_b, mine_d, sib_c, sib_b, sib_d,
    hg_ref, hsib_ref, ha_ref, hb_ref, out_c, out_b, out_d, got_c, got_b, got_d,
    load_sem, store_sem, sib_send, sib_recv, hs_sem, hr_sem,
    sf_sem, rf_sem, sg_sem, rg_sem, sh_sem, rh_sem, sp_sem, rp_sem, swc_sem, rwc_sem, swb_sem, rwb_sem, swd_sem, rwd_sem,
):
    me = lax.axis_index("wide")
    place = lax.axis_index("dp")
    core = lax.rem(place, 2)
    other = 1 - core
    sets = dp // 2
    slots = wide * sets
    mine = me * sets + place // 2
    seq, width = in_ref.shape
    heads = alog_ref.shape[1]
    half = seq // 2
    nst = wbc_ref.shape[1] // 2
    owners = BLOCK // LANES
    blocks = width // BLOCK
    per_block = BLOCK // 64
    pairs = width // LANES
    group = 8
    groups = slots // group
    sibling = {"wide": me, "dp": place - core + other}

    def at_slot(slot):
        return {"wide": slot // sets, "dp": lax.rem(slot, sets) * 2 + core}

    def to_peer(k):
        return lax.rem(me + k * STRIDE, wide)

    def from_peer(k):
        return lax.rem(me + (wide - k) * STRIDE, wide)

    def targets(step):
        return [to_peer(step * owners + i + 1) for i in range(owners)]

    def sources(step):
        return [from_peer(step * owners + i + 1) for i in range(owners)]

    def lanes_of(p):
        return pl.ds(pl.multiple_of(p * LANES, LANES), LANES)

    def columns(ref, peers):
        return jnp.concatenate([ref[:, lanes_of(p)] for p in peers], axis=1)

    def joined(ref, peers):
        return jnp.concatenate([ref[p, :nst, :] for p in peers], axis=1)

    barrier = pltpu.get_barrier_semaphore()
    pl.semaphore_signal(barrier, inc=1, device_id=sibling, device_id_type=MESH)

    def greet(k, _):
        pl.semaphore_signal(
            barrier, inc=1, device_id=at_slot(lax.rem(mine + k, slots)), device_id_type=MESH
        )
        return 0

    lax.fori_loop(1, slots, greet, 0)

    quarter = width // 4
    loads = []
    for q in range(4):
        part = pl.ds(q * quarter, quarter)
        loads.append((
            pltpu.make_async_copy(in_hbm.at[:, part], in_ref.at[:, part], load_sem.at[0, q]),
            pltpu.make_async_copy(wbc_hbm.at[part], wbc_ref.at[part], load_sem.at[1, q]),
            pltpu.make_async_copy(wdt_hbm.at[:, part], wdt_ref.at[:, part], load_sem.at[2, q]),
        ))
    load_x = pltpu.make_async_copy(x_hbm, x_ref, load_sem.at[3, 0])
    load_g = pltpu.make_async_copy(g_hbm, g_ref, load_sem.at[3, 1])
    for load in loads:
        for one in load:
            one.start()
    load_x.start()
    load_g.start()

    narrow = lax.rem(
        lax.broadcasted_iota(jnp.int32, (2 * heads, LANES), 0), heads
    ) - lax.broadcasted_iota(jnp.int32, (2 * heads, LANES), 1) // 64
    gather_delta = lax.broadcasted_iota(jnp.int32, (LANES, heads), 1) - lax.broadcasted_iota(
        jnp.int32, (LANES, heads), 0
    ) // 64

    def spread(peers):
        return jnp.concatenate([(narrow == 2 * p).astype(BF) for p in peers], axis=1)

    def gathered(peers):
        return jnp.concatenate([(gather_delta == 2 * p).astype(BF) for p in peers], axis=0)

    def remote(src, dst, send, recv, target):
        return pltpu.make_async_remote_copy(
            src_ref=src, dst_ref=dst, send_sem=send, recv_sem=recv, device_id=target,
            device_id_type=MESH,
        )

    def send_f(peer):
        return remote(f_ref.at[peer], gotf_ref.at[me], sf_sem.at[peer], rf_sem.at[me], {"wide": peer})

    def send_g(peer):
        return remote(gt_ref.at[peer], gotg_ref.at[me], sg_sem.at[peer], rg_sem.at[me], {"wide": peer})

    def send_h(peer):
        return remote(h_ref.at[peer], goth_ref.at[me], sh_sem.at[peer], rh_sem.at[me], {"wide": peer})

    def send_p(peer):
        return remote(p_ref.at[peer], gotp_ref.at[me], sp_sem.at[peer], rp_sem.at[me], {"wide": peer})

    def send_w(out, got, send, recv, slot):
        return remote(out.at[slot], got.at[mine], send.at[slot], recv.at[mine], at_slot(slot))

    sib_in = remote(int_ref.at[other], sib_ref, sib_send.at[0], sib_recv.at[0], sibling)
    sibling_c = remote(mine_c, sib_c, sib_send.at[1], sib_recv.at[1], sibling)
    sibling_b = remote(mine_b, sib_b, sib_send.at[2], sib_recv.at[2], sibling)
    sibling_d = remote(mine_d, sib_d, sib_send.at[3], sib_recv.at[3], sibling)
    sib_h = remote(hg_ref, hsib_ref, sib_send.at[4], sib_recv.at[4], sibling)

    bc = jnp.zeros((seq, 2 * nst), F32)
    dt_raw = jnp.zeros((seq, heads), F32)
    for q, load in enumerate(loads):
        for one in load:
            one.wait()
        part = slice(q * quarter, (q + 1) * quarter)
        bc += mm(in_ref[:, part], wbc_ref[part, :])
        dt_raw += mm_nt(in_ref[:, part], wdt_ref[:, part])
    bc = bc.astype(BF)
    dt_raw = dt_raw.astype(BF).astype(F32)
    b_rows = bc[:, :nst]
    c_rows = bc[:, nst:]
    b_t = b_rows.astype(F32).T.astype(BF)
    c_t = c_rows.astype(F32).T.astype(BF)
    dt_pre = dt_raw + bias_ref[...]
    dt = jnp.maximum(dt_pre, 0.0) + jnp.log1p(jnp.exp(-jnp.abs(dt_pre)))
    rate = -jnp.exp(alog_ref[...])
    log_rate = dt * rate
    pos_r = lax.broadcasted_iota(jnp.int32, (seq, seq), 0)
    pos_c = lax.broadcasted_iota(jnp.int32, (seq, seq), 1)
    lower = (pos_r >= pos_c).astype(BF)
    lr_hi, lr_mid, lr_lo = split3(log_rate)
    cumul = mm(lower, lr_hi) + mm(lower, lr_mid) + mm(lower, lr_lo)
    last = cumul[seq - 1 :, :]
    tail = dt * jnp.exp(last - cumul)
    tail2 = jnp.concatenate(split2(tail), axis=1)
    lq_hi, lq_mid, lq_lo = split3(last)
    none = jnp.zeros((1, heads), BF)
    lq_rows = jnp.concatenate(
        [jnp.concatenate([v, none], axis=1) for v in (lq_hi, lq_mid, lq_lo)]
        + [jnp.zeros((13, 2 * heads), BF)],
        axis=0,
    )

    load_x.wait()
    pl.semaphore_wait(barrier, slots)

    def fresh_f(step, _):
        peers = targets(step)
        r = spread(peers)
        xs = (columns(x_ref, peers).astype(F32) * mm(tail2, r)).astype(BF)
        f_t = mm(b_t, xs).astype(BF)
        lq = mm(lq_rows, r).astype(BF)
        for i, peer in enumerate(peers):
            lanes = slice(i * LANES, (i + 1) * LANES)
            xs_ref[:, lanes_of(peer)] = xs[:, lanes]
            f_ref[peer, :nst, :] = f_t[:, lanes]
            f_ref[peer, nst:, :] = lq[:, lanes]

            @pl.when(peer != me)
            def _():
                send_f(peer).start()

        return 0

    lax.fori_loop(0, blocks, fresh_f, 0)

    head_exp = jnp.exp(cumul)
    exp2 = jnp.concatenate(split2(head_exp), axis=1)
    load_g.wait()

    def fresh_g(step, _):
        peers = targets(step)
        gs = (columns(g_ref, peers).astype(F32) * mm(exp2, spread(peers))).astype(BF)
        g_t = mm(c_t, gs).astype(BF)
        for i, peer in enumerate(peers):
            lanes = slice(i * LANES, (i + 1) * LANES)
            gs_ref[:, lanes_of(peer)] = gs[:, lanes]
            gt_ref[peer] = g_t[:, lanes]

            @pl.when(peer != me)
            def _():
                send_g(peer).start()

        return 0

    lax.fori_loop(0, blocks, fresh_g, 0)

    lt_ref[...] = cumul.T
    u3 = jnp.concatenate(split3(jnp.log(jnp.maximum(dt, 1e-37)) - cumul), axis=1)
    st_ref[...] = mm_nt(b_rows, c_rows)
    lane = lax.broadcasted_iota(jnp.int32, (seq, LANES), 1)
    lane_head = lax.broadcasted_iota(jnp.int32, (half, heads), 1)
    upper = lax.broadcasted_iota(jnp.int32, (half, half), 0) <= lax.broadcasted_iota(
        jnp.int32, (half, half), 1
    )
    row_head = lax.rem(lax.broadcasted_iota(jnp.int32, (3 * heads, LANES), 0), heads)
    nt_ref[...] = jnp.zeros_like(nt_ref)
    col_ref[...] = jnp.zeros_like(col_ref)

    def within(pair, _):
        cols = pl.ds(pl.multiple_of(pair * LANES, LANES), LANES)
        xk = x_ref[:, cols]
        gk = g_ref[:, cols]
        total_lo = jnp.zeros((half, LANES), F32)
        total_hi = jnp.zeros((half, LANES), F32)
        for side in range(2):
            h = pair * 2 + side
            mine_lane = (lane < 64) if side == 0 else (lane >= 64)
            xm = jnp.where(mine_lane, xk, jnp.zeros_like(xk))
            gm = jnp.where(mine_lane, gk, jnp.zeros_like(gk))
            u = mm(u3, (row_head == h).astype(BF))
            lt = lt_ref[pl.ds(h, 1), :]
            w0 = mm_nt(xm[:half], gk)
            w1 = mm_nt(xm[half:], gk[half:])
            a00 = jnp.where(upper, jnp.exp(u[:half] + lt[:, :half]), 0.0)
            a01 = jnp.exp(u[:half] + lt[:, half:])
            a11 = jnp.where(upper, jnp.exp(u[half:] + lt[:, half:]), 0.0)
            s00 = st_ref[:half, :half]
            s01 = st_ref[:half, half:]
            s11 = st_ref[half:, half:]
            p00 = a00 * w0[:, :half]
            p01 = a01 * w0[:, half:]
            p11 = a11 * w1
            nt_ref[:half, :half] += p00
            nt_ref[:half, half:] += p01
            nt_ref[half:, half:] += p11
            total_lo += mm((a00 * s00).astype(BF), gm[:half]) + mm((a01 * s01).astype(BF), gm[half:])
            total_hi += mm((a11 * s11).astype(BF), gm[half:])
            z00 = p00 * s00
            z01 = p01 * s01
            z11 = p11 * s11
            rt_ref[h, :, :half] = jnp.sum(z00, axis=0, keepdims=True)
            rt_ref[h, :, half:] = jnp.sum(z01 + z11, axis=0, keepdims=True)
            col_ref[:half, :] += jnp.where(
                lane_head == h, jnp.sum(z00 + z01, axis=1, keepdims=True), 0.0
            )
            col_ref[half:, :] += jnp.where(
                lane_head == h, jnp.sum(z11, axis=1, keepdims=True), 0.0
            )
        hrow_ref[:, cols] = jnp.sum(xk.astype(F32) * gk.astype(F32), axis=0, keepdims=True)
        gxw_ref[:half, cols] = total_lo
        gxw_ref[half:, cols] = total_hi
        turned = in_ref[:, cols].astype(F32).T.astype(BF)
        for i in range(dp):
            int_ref[i % 2, pair * sets + i // 2] = turned[i * 32 : (i + 1) * 32]
        return 0

    first_part = (pairs * 5) // 8
    lax.fori_loop(0, first_part, within, 0)

    def decay_of(i):
        parts = gotf_ref[i, nst:, :].astype(F32)
        return jnp.exp(parts[0:1] + parts[1:2] + parts[2:3])

    def take_f(k, _):
        peer = from_peer(k)
        pltpu.make_async_copy(f_ref.at[peer], gotf_ref.at[peer], rf_sem.at[peer]).wait()
        return 0

    gotf_ref[me] = f_ref[me]
    lax.fori_loop(1, wide, take_f, 0)

    def advance_f(i, state):
        h_ref[i] = state.astype(BF)
        return state * decay_of(i) + gotf_ref[i, :nst, :].astype(F32)

    start = jnp.zeros((nst, LANES), F32)
    lax.fori_loop(0, wide, advance_f, start)

    def give_h(k, _):
        send_h(to_peer(k)).start()
        return 0

    lax.fori_loop(1, wide, give_h, 0)
    goth_ref[me] = h_ref[me]

    lax.fori_loop(first_part, pairs, within, 0)
    sib_in.start()

    def take_g(k, _):
        peer = from_peer(k)
        pltpu.make_async_copy(gt_ref.at[peer], gotg_ref.at[peer], rg_sem.at[peer]).wait()
        return 0

    gotg_ref[me] = gt_ref[me]
    lax.fori_loop(1, wide, take_g, 0)

    def advance_g(k, pull):
        i = wide - 1 - k
        p_ref[i] = pull.astype(BF)
        return pull * decay_of(i) + gotg_ref[i].astype(F32)

    lax.fori_loop(0, wide, advance_g, start)

    def give_p(k, _):
        send_p(to_peer(k)).start()
        return 0

    lax.fori_loop(1, wide, give_p, 0)
    gotp_ref[me] = p_ref[me]

    n_low = nt_ref[...].astype(BF)
    g_b = mm(n_low, c_rows)
    g_c = mm(nt_ref[...].T.astype(BF), b_rows)

    skip_hi, skip_lo = split2(skip_ref[...])
    skip_rows = jnp.concatenate(
        [jnp.concatenate([skip_hi, skip_lo], axis=1)]
        + [jnp.concatenate([v, none], axis=1) for v in (lq_hi, lq_mid, lq_lo)]
        + [jnp.zeros((12, 2 * heads), BF)],
        axis=0,
    )
    def finish_f(step, carried):
        row_st, gc = carried
        peers = sources(step)
        for peer in peers:

            @pl.when(peer != me)
            def _():
                pltpu.make_async_copy(h_ref.at[peer], goth_ref.at[peer], rh_sem.at[peer]).wait()

        h0 = joined(goth_ref, peers)
        gs = columns(gs_ref, peers)
        y_st = mm(c_rows, h0)
        row_st += mm((gs.astype(F32) * y_st).astype(BF), gathered(peers))
        gc += mm_nt(gs, h0)
        return row_st, gc

    zero_h = jnp.zeros((seq, heads), F32)
    row_st, g_c = lax.fori_loop(0, blocks, finish_f, (zero_h, g_c))
    mine_c[...] = g_c.astype(BF)
    sibling_c.start()

    upper_all = (pos_r <= pos_c).astype(BF)

    def suffix(v):
        hi, mid, lo = split3(v)
        return mm(upper_all, hi) + mm(upper_all, mid) + mm(upper_all, lo)

    early = suffix(rt_ref[:, 0, :].T + row_st - col_ref[...])
    gate = 1.0 / (1.0 + jnp.exp(-dt_pre))
    ratio = jnp.where(dt > 0.0, gate / jnp.where(dt > 0.0, dt, 1.0), 1.0)

    def finish_g(step, carried):
        col_st, gb, sums = carried
        peers = sources(step)
        for peer in peers:

            @pl.when(peer != me)
            def _():
                pltpu.make_async_copy(p_ref.at[peer], gotp_ref.at[peer], rp_sem.at[peer]).wait()

        r = spread(peers)
        gather = gathered(peers)
        dh = joined(gotp_ref, peers)
        xs = columns(xs_ref, peers)
        u_st = mm(b_rows, dh)
        rows = mm(skip_rows, r)
        gx = columns(gxw_ref, peers) + mm(tail2, r) * u_st
        gx = (gx + rows[0:1] * columns(g_ref, peers).astype(F32)).astype(BF)
        col_st += mm((xs.astype(F32) * u_st).astype(BF), gather)
        gb += mm_nt(xs, dh)
        ended = joined(goth_ref, peers).astype(F32) * jnp.exp(rows[1:2] + rows[2:3] + rows[3:4])
        ended += joined(f_ref, peers).astype(F32)
        heads_in = jnp.concatenate(
            [jnp.sum(ended * dh.astype(F32), axis=0, keepdims=True), columns(hrow_ref, peers)], axis=0
        )
        hi, lo = split2(heads_in)
        sums += mm(hi, gather) + mm(lo, gather)
        for i, peer in enumerate(peers):
            cols = lanes_of(peer)
            xo_ref[:, cols] = gx[:, i * LANES : (i + 1) * LANES]
            pltpu.make_async_copy(xo_ref.at[:, cols], xg_hbm.at[:, cols], store_sem.at[0, peer]).start()
        return col_st, gb, sums

    def weigh(mine_p, sib_p, out, got, send, recv, packed):
        def step_of(step, _):
            order = [lax.rem(mine + (step * group + i + 1) * STRIDE_W, slots) for i in range(group)]
            ours = jnp.concatenate([int_ref[core, slot] for slot in order], axis=0)
            theirs = jnp.concatenate([sib_ref[slot] for slot in order], axis=0)
            w = mm(ours, mine_p[...]) + mm(theirs, sib_p[...])
            for i, slot in enumerate(order):
                at = w[i * 32 : (i + 1) * 32]
                if packed:
                    out[slot, :, : 2 * heads] = jnp.concatenate([at[:16], at[16:]], axis=1).astype(BF)
                else:
                    out[slot] = at.astype(BF)

                @pl.when(slot != mine)
                def _():
                    send_w(out, got, send, recv, slot).start()

            return 0

        lax.fori_loop(0, groups, step_of, 0)

    carried = lax.fori_loop(0, blocks // 4, finish_g, (zero_h, g_b, jnp.zeros((2, heads), F32)))
    sib_in.wait_recv()
    sibling_c.wait_recv()
    weigh(mine_c, sib_c, out_c, got_c, swc_sem, rwc_sem, False)
    col_st, g_b, sums = lax.fori_loop(blocks // 4, blocks, finish_g, carried)
    mine_b[...] = g_b.astype(BF)
    sibling_b.start()

    d_log = early - suffix(col_st) + sums[0:1]
    g_dt = (col_ref[...] + col_st) * ratio + rate * d_log * gate
    mine_d[...] = g_dt.astype(BF)
    sibling_d.start()
    g_alog = jnp.sum(d_log * log_rate, axis=0, keepdims=True)
    g_bias = jnp.sum(g_dt, axis=0, keepdims=True)
    hg_ref[...] = jnp.zeros_like(hg_ref)
    hg_ref[0:1, :heads] = g_alog
    hg_ref[1:2, :heads] = g_bias
    hg_ref[2:3, :heads] = sums[1:2]
    sib_h.start()

    sibling_b.wait_recv()
    weigh(mine_b, sib_b, out_b, got_b, swb_sem, rwb_sem, False)
    sibling_d.wait_recv()
    weigh(mine_d, sib_d, out_d, got_d, swd_sem, rwd_sem, True)

    def emit(j, _):
        cols = pl.ds(pl.multiple_of(j * BLOCK, BLOCK), BLOCK)
        d_in = mm_nt(mine_b[...], wbc_ref[cols, :nst]) + mm_nt(mine_c[...], wbc_ref[cols, nst:])
        d_in += mm(mine_d[...], wdt_ref[:, cols])
        io_ref[:, cols] = d_in.astype(BF)
        pltpu.make_async_copy(io_ref.at[:, cols], ig_hbm.at[:, cols], store_sem.at[1, j]).start()
        return 0

    ga, gi = mine // group, lax.rem(mine, group)
    sib_h.wait_recv()
    ha_ref[gi] = hg_ref[...] + hsib_ref[...]

    def send_a(i):
        return remote(ha_ref.at[gi], ha_ref.at[gi], hs_sem.at[0, i], hr_sem.at[0, gi], at_slot(ga * group + i))

    def send_b(i):
        return remote(hb_ref.at[ga], hb_ref.at[ga], hs_sem.at[1, i], hr_sem.at[1, ga], at_slot(i * group + gi))

    def start_a(k, _):
        send_a(lax.rem(gi + k, group)).start()
        return 0

    lax.fori_loop(1, group, start_a, 0)
    lax.fori_loop(0, blocks, emit, 0)

    def end_a(k, _):
        i = lax.rem(gi + k, group)
        pltpu.make_async_copy(ha_ref.at[i], ha_ref.at[i], hr_sem.at[0, i]).wait()
        send_a(i).wait_send()
        return 0

    lax.fori_loop(1, group, end_a, 0)
    hb_ref[ga] = jnp.sum(ha_ref[...], axis=0)

    def start_b(k, _):
        send_b(lax.rem(ga + k, groups)).start()
        return 0

    lax.fori_loop(1, groups, start_b, 0)

    def drain(k, _):
        f_peer = to_peer(k)
        send_f(f_peer).wait_send()
        send_g(f_peer).wait_send()
        send_h(f_peer).wait_send()
        send_p(f_peer).wait_send()
        return 0

    lax.fori_loop(1, wide, drain, 0)

    def stored_x(p, _):
        cols = lanes_of(p)
        pltpu.make_async_copy(xo_ref.at[:, cols], xg_hbm.at[:, cols], store_sem.at[0, p]).wait()
        return 0

    lax.fori_loop(0, wide, stored_x, 0)

    def stored_i(j, _):
        cols = pl.ds(pl.multiple_of(j * BLOCK, BLOCK), BLOCK)
        pltpu.make_async_copy(io_ref.at[:, cols], ig_hbm.at[:, cols], store_sem.at[1, j]).wait()
        return 0

    lax.fori_loop(0, blocks, stored_i, 0)
    sib_in.wait_send()
    sibling_c.wait_send()
    sibling_b.wait_send()
    sibling_d.wait_send()
    sib_h.wait_send()

    def end_b(k, _):
        i = lax.rem(ga + k, groups)
        pltpu.make_async_copy(hb_ref.at[i], hb_ref.at[i], hr_sem.at[1, i]).wait()
        send_b(i).wait_send()
        return 0

    lax.fori_loop(1, groups, end_b, 0)
    rows = jnp.sum(hb_ref[...], axis=0)
    at = lax.broadcasted_iota(jnp.int32, rows.shape, 1)
    per = heads // wide
    for i in range(per):
        picked = jnp.sum(jnp.where(at == me * per + i, rows, 0.0), axis=1, keepdims=True)
        for r in range(3):
            head_out[i : i + 1, r : r + 1] = picked[r : r + 1]

    def total(out, got, recv, acc):
        def add(k, acc):
            slot = lax.rem(mine + (slots - k) * STRIDE_W, slots)
            pltpu.make_async_copy(out.at[slot], got.at[slot], recv.at[slot]).wait()
            return acc + got[slot].astype(F32)

        return lax.fori_loop(1, slots, add, acc)

    wbc_out[:, LANES:] = total(out_c, got_c, rwc_sem, out_c[mine].astype(F32))
    wbc_out[:, :LANES] = total(out_b, got_b, rwb_sem, out_b[mine].astype(F32))
    acc = total(out_d, got_d, rwd_sem, out_d[mine].astype(F32))
    wdt_out[0:16, :] = acc[:, :heads]
    wdt_out[16:32, :] = acc[:, heads : 2 * heads]

    def done(k, _):
        slot = lax.rem(mine + k, slots)
        send_w(out_c, got_c, swc_sem, rwc_sem, slot).wait_send()
        send_w(out_b, got_b, swb_sem, rwb_sem, slot).wait_send()
        send_w(out_d, got_d, swd_sem, rwd_sem, slot).wait_send()
        return 0

    lax.fori_loop(1, slots, done, 0)


def place_kernel(
    x_in, i_in, b_in, d_in, h_in, x_out, i_out, b_out, d_out, h_out,
    x_ref, i_ref, b_ref, d_ref, h_ref, come, go, come_small, go_small,
):
    steps = []
    for a, (src, mid, dst) in enumerate(((b_in, b_ref, b_out), (d_in, d_ref, d_out), (h_in, h_ref, h_out))):
        steps.append((
            pltpu.make_async_copy(src, mid, come_small.at[a]),
            pltpu.make_async_copy(mid, dst, go_small.at[a]),
        ))
    for q in range(PIECES):
        for a, (src, mid, dst) in enumerate(((x_in, x_ref, x_out), (i_in, i_ref, i_out))):
            rows = src.shape[0] // PIECES
            part = pl.ds(q * rows, rows)
            steps.append((
                pltpu.make_async_copy(src.at[part], mid.at[part], come.at[a, q]),
                pltpu.make_async_copy(mid.at[part], dst.at[part], go.at[a, q]),
            ))
    for first, _ in steps:
        first.start()
    for first, second in steps:
        first.wait()
        second.start()
    for _, second in steps:
        second.wait()


def local(wide, dp, layer_input, inner_acts, w_bc, w_dt, a_log, dt_bias, d_skip, out_grad):
    seq, width = layer_input.shape[1:]
    heads = a_log.shape[0]
    nst = w_bc.shape[1] // 2
    slots = wide * dp // 2
    rows = width // (wide * dp)
    any_spec = pl.BlockSpec(memory_space=pl.ANY)
    vmem = pl.BlockSpec(memory_space=pltpu.VMEM)
    dma = pltpu.SemaphoreType.DMA
    v = pltpu.VMEM
    x_grad, input_grad, wbc_grad, wdt_grad, head_grads = pl.pallas_call(
        functools.partial(scan_kernel, wide, dp),
        out_shape=(
            jax.ShapeDtypeStruct((seq, width), BF),
            jax.ShapeDtypeStruct((seq, width), BF),
            jax.ShapeDtypeStruct((rows, 2 * nst), F32),
            jax.ShapeDtypeStruct((rows, heads), F32),
            jax.ShapeDtypeStruct((heads // wide, 3), F32),
        ),
        in_specs=[any_spec] * 5 + [vmem] * 3,
        out_specs=(any_spec, any_spec, vmem, vmem, vmem),
        scratch_shapes=[
            v((seq, width), BF),
            v((seq, width), BF),
            v((seq, width), BF),
            v((width, 2 * nst), BF),
            v((heads, width), BF),
            v((wide, nst + 16, LANES), BF),
            v((wide, nst, LANES), BF),
            v((wide, nst + 16, LANES), BF),
            v((wide, nst, LANES), BF),
            v((wide, nst, LANES), BF),
            v((wide, nst, LANES), BF),
            v((wide, nst, LANES), BF),
            v((wide, nst, LANES), BF),
            v((seq, width), BF),
            v((seq, width), BF),
            v((seq, width), F32),
            v((2, slots, 32, seq), BF),
            v((slots, 32, seq), BF),
            v((seq, seq), F32),
            v((seq, seq), F32),
            v((heads, seq), F32),
            v((heads, 1, seq), F32),
            v((seq, heads), F32),
            v((1, width), F32),
            v((seq, width), BF),
            v((seq, width), BF),
            v((seq, nst), BF),
            v((seq, nst), BF),
            v((seq, heads), BF),
            v((seq, nst), BF),
            v((seq, nst), BF),
            v((seq, heads), BF),
            v((8, LANES), F32),
            v((8, LANES), F32),
            v((8, 8, LANES), F32),
            v((slots // 8, 8, LANES), F32),
            v((slots, 32, LANES), BF),
            v((slots, 32, LANES), BF),
            v((slots, 16, LANES), BF),
            v((slots, 32, LANES), BF),
            v((slots, 32, LANES), BF),
            v((slots, 16, LANES), BF),
            dma((4, 4)),
            dma((2, wide)),
            dma((5,)),
            dma((5,)),
            dma((2, 8)),
            dma((2, 8)),
        ]
        + [dma((wide,))] * 8
        + [dma((slots,))] * 6,
        compiler_params=pltpu.CompilerParams(
            collective_id=0, has_side_effects=True, vmem_limit_bytes=56 * 1024 * 1024
        ),
        cost_estimate=pl.CostEstimate(
            flops=30 * seq * width * 256, bytes_accessed=8 * seq * width, transcendentals=0
        ),
        name="scan_backward",
    )(
        layer_input[0], inner_acts[0], out_grad[0], w_bc, w_dt.T,
        a_log[None], dt_bias[None], d_skip[None],
    )
    x_grad, input_grad, wbc_grad, wdt_grad, head_grads = pl.pallas_call(
        place_kernel,
        out_shape=tuple(
            jax.ShapeDtypeStruct(a.shape, a.dtype)
            for a in (x_grad, input_grad, wbc_grad, wdt_grad, head_grads)
        ),
        in_specs=[any_spec] * 5,
        out_specs=[any_spec] * 5,
        scratch_shapes=[
            v(a.shape, a.dtype) for a in (x_grad, input_grad, wbc_grad, wdt_grad, head_grads)
        ]
        + [dma((2, PIECES)), dma((2, PIECES)), dma((3,)), dma((3,))],
        compiler_params=pltpu.CompilerParams(vmem_limit_bytes=60 * 1024 * 1024),
        name="place_results",
    )(x_grad, input_grad, wbc_grad, wdt_grad, head_grads)
    return x_grad[None], input_grad[None], wbc_grad, wdt_grad, head_grads.T


def solution(mesh):
    in_specs = (
        P("dp", "wide", None),
        P("dp", "wide", None),
        P(),
        P(),
        P(),
        P(),
        P(),
        P("dp", "wide", None),
    )
    out_specs = (
        P("dp", "wide", None),
        P("dp", "wide", None),
        P(("wide", "dp"), None),
        P(("wide", "dp"), None),
        P(None, "wide"),
    )
    return jax.shard_map(
        functools.partial(local, mesh.shape["wide"], mesh.shape["dp"]),
        mesh=mesh,
        in_specs=in_specs,
        out_specs=out_specs,
        check_vma=False,
    )
```

```python
import functools

import jax
import jax.numpy as jnp
from jax import lax
from jax.experimental import pallas as pl
from jax.experimental.pallas import tpu as pltpu
from jax.sharding import PartitionSpec as P

MESH = pl.DeviceIdType.MESH
BF = jnp.bfloat16
F32 = jnp.float32
LANES = 128
BLOCK = 512
STRIDE = 13
STRIDE_W = 27
WEIGHED = 16
PIECES = 8


def mm(a, b):
    return jnp.dot(a, b, preferred_element_type=F32)


def mm_nt(a, b):
    return lax.dot_general(a, b, (((1,), (1,)), ((), ())), preferred_element_type=F32)


def split2(v):
    hi = v.astype(BF)
    return hi, (v - hi.astype(F32)).astype(BF)


def split3(v):
    hi = v.astype(BF)
    rest = v - hi.astype(F32)
    mid = rest.astype(BF)
    return hi, mid, (rest - mid.astype(F32)).astype(BF)


def scan_kernel(
    wide, dp, in_hbm, x_hbm, g_hbm, wbc_hbm, wdt_hbm, alog_ref, bias_ref, skip_ref,
    xg_hbm, ig_hbm, wbc_out, wdt_out, head_out,
    in_ref, x_ref, g_ref, wbc_ref, wdt_ref, f_ref, gt_ref, gotf_ref, gotg_ref, h_ref, p_ref,
    goth_ref, gotp_ref, xs_ref, gs_ref, gxw_ref, int_ref, sib_ref, nt_ref, st_ref, lt_ref, rt_ref,
    col_ref, hrow_ref, xo_ref, io_ref, mine_c, mine_b, mine_d, sib_c, sib_b, sib_d,
    hg_ref, hsib_ref, ha_ref, hb_ref, out_c, out_b, out_d, got_c, got_b, got_d,
    load_sem, store_sem, sib_send, sib_recv,
    out_sem, in_sem, rh_sem, rp_sem,
):
    me = lax.axis_index("wide")
    place = lax.axis_index("dp")
    core = lax.rem(place, 2)
    other = 1 - core
    sets = dp // 2
    slots = wide * sets
    mine = me * sets + place // 2
    seq, width = in_ref.shape
    heads = alog_ref.shape[1]
    half = seq // 2
    nst = wbc_ref.shape[1] // 2
    owners = BLOCK // LANES
    blocks = width // BLOCK
    per_block = BLOCK // 64
    pairs = width // LANES
    group = 8
    groups = slots // group
    sibling = {"wide": me, "dp": place - core + other}

    def at_slot(slot):
        return {"wide": slot // sets, "dp": lax.rem(slot, sets) * 2 + core}

    def to_peer(k):
        return lax.rem(me + k * STRIDE, wide)

    def from_peer(k):
        return lax.rem(me + (wide - k) * STRIDE, wide)

    def targets(step):
        return [to_peer(step * owners + i + 1) for i in range(owners)]

    def sources(step):
        return [from_peer(step * owners + i + 1) for i in range(owners)]

    def lanes_of(p):
        return pl.ds(pl.multiple_of(p * LANES, LANES), LANES)

    def columns(ref, peers):
        return jnp.concatenate([ref[:, lanes_of(p)] for p in peers], axis=1)

    def joined(ref, peers):
        return jnp.concatenate([ref[p, :nst, :] for p in peers], axis=1)

    barrier = pltpu.get_barrier_semaphore()
    pl.semaphore_signal(barrier, inc=1, device_id=sibling, device_id_type=MESH)

    def greet(k, _):
        pl.semaphore_signal(
            barrier, inc=1, device_id=at_slot(lax.rem(mine + k, slots)), device_id_type=MESH
        )
        return 0

    lax.fori_loop(1, slots, greet, 0)

    quarter = width // 4
    loads = []
    for q in range(4):
        part = pl.ds(q * quarter, quarter)
        loads.append((
            pltpu.make_async_copy(in_hbm.at[:, part], in_ref.at[:, part], load_sem.at[0, q]),
            pltpu.make_async_copy(wbc_hbm.at[part], wbc_ref.at[part], load_sem.at[1, q]),
            pltpu.make_async_copy(wdt_hbm.at[:, part], wdt_ref.at[:, part], load_sem.at[2, q]),
        ))
    load_x = pltpu.make_async_copy(x_hbm, x_ref, load_sem.at[3, 0])
    load_g = pltpu.make_async_copy(g_hbm, g_ref, load_sem.at[3, 1])
    for load in loads:
        for one in load:
            one.start()
    load_x.start()
    load_g.start()

    narrow = lax.rem(
        lax.broadcasted_iota(jnp.int32, (2 * heads, LANES), 0), heads
    ) - lax.broadcasted_iota(jnp.int32, (2 * heads, LANES), 1) // 64
    gather_delta = lax.broadcasted_iota(jnp.int32, (LANES, heads), 1) - lax.broadcasted_iota(
        jnp.int32, (LANES, heads), 0
    ) // 64

    def spread(peers):
        return jnp.concatenate([(narrow == 2 * p).astype(BF) for p in peers], axis=1)

    def gathered(peers):
        return jnp.concatenate([(gather_delta == 2 * p).astype(BF) for p in peers], axis=0)

    def remote(src, dst, send, recv, target):
        return pltpu.make_async_remote_copy(
            src_ref=src, dst_ref=dst, send_sem=send, recv_sem=recv, device_id=target,
            device_id_type=MESH,
        )

    def send_f(peer):
        return remote(f_ref.at[peer], gotf_ref.at[me], out_sem.at[0], in_sem.at[0], {"wide": peer})

    def send_g(peer):
        return remote(gt_ref.at[peer], gotg_ref.at[me], out_sem.at[1], in_sem.at[1], {"wide": peer})

    def send_h(k):
        peer = to_peer(k)
        step = (k - 1) // owners
        return remote(h_ref.at[peer], goth_ref.at[me], out_sem.at[2], rh_sem.at[step], {"wide": peer})

    def send_p(k):
        peer = to_peer(k)
        step = (k - 1) // owners
        return remote(p_ref.at[peer], gotp_ref.at[me], out_sem.at[3], rp_sem.at[step], {"wide": peer})

    def send_w(out, got, which, slot):
        return remote(out.at[slot], got.at[mine], out_sem.at[which], in_sem.at[which], at_slot(slot))

    def wait_for(ref, count, sem):
        part = ref.at[pl.ds(0, count)]
        pltpu.make_async_copy(part, part, sem).wait()

    def wait_step(ref, sem, step):
        @pl.when(step < blocks - 1)
        def _():
            wait_for(ref, owners, sem.at[step])

        @pl.when(step == blocks - 1)
        def _():
            wait_for(ref, owners - 1, sem.at[step])

    sib_in = remote(int_ref.at[other], sib_ref, sib_send.at[0], sib_recv.at[0], sibling)
    sibling_c = remote(mine_c, sib_c, sib_send.at[1], sib_recv.at[1], sibling)
    sibling_b = remote(mine_b, sib_b, sib_send.at[2], sib_recv.at[2], sibling)
    sibling_d = remote(mine_d, sib_d, sib_send.at[3], sib_recv.at[3], sibling)
    sib_h = remote(hg_ref, hsib_ref, sib_send.at[4], sib_recv.at[4], sibling)

    bc = jnp.zeros((seq, 2 * nst), F32)
    dt_raw = jnp.zeros((seq, heads), F32)
    for q, load in enumerate(loads):
        for one in load:
            one.wait()
        part = slice(q * quarter, (q + 1) * quarter)
        bc += mm(in_ref[:, part], wbc_ref[part, :])
        dt_raw += mm_nt(in_ref[:, part], wdt_ref[:, part])
    bc = bc.astype(BF)
    dt_raw = dt_raw.astype(BF).astype(F32)
    b_rows = bc[:, :nst]
    c_rows = bc[:, nst:]
    b_t = b_rows.astype(F32).T.astype(BF)
    c_t = c_rows.astype(F32).T.astype(BF)
    dt_pre = dt_raw + bias_ref[...]
    dt = jnp.maximum(dt_pre, 0.0) + jnp.log1p(jnp.exp(-jnp.abs(dt_pre)))
    rate = -jnp.exp(alog_ref[...])
    log_rate = dt * rate
    pos_r = lax.broadcasted_iota(jnp.int32, (seq, seq), 0)
    pos_c = lax.broadcasted_iota(jnp.int32, (seq, seq), 1)
    lower = (pos_r >= pos_c).astype(BF)
    lr_hi, lr_mid, lr_lo = split3(log_rate)
    cumul = mm(lower, lr_hi) + mm(lower, lr_mid) + mm(lower, lr_lo)
    last = cumul[seq - 1 :, :]
    tail = dt * jnp.exp(last - cumul)
    tail2 = jnp.concatenate(split2(tail), axis=1)
    lq_hi, lq_mid, lq_lo = split3(last)
    none = jnp.zeros((1, heads), BF)
    lq_rows = jnp.concatenate(
        [jnp.concatenate([v, none], axis=1) for v in (lq_hi, lq_mid, lq_lo)]
        + [jnp.zeros((13, 2 * heads), BF)],
        axis=0,
    )

    load_x.wait()
    pl.semaphore_wait(barrier, slots)

    def fresh_f(step, _):
        peers = targets(step)
        r = spread(peers)
        xs = (columns(x_ref, peers).astype(F32) * mm(tail2, r)).astype(BF)
        f_t = mm(b_t, xs).astype(BF)
        lq = mm(lq_rows, r).astype(BF)
        for i, peer in enumerate(peers):
            lanes = slice(i * LANES, (i + 1) * LANES)
            xs_ref[:, lanes_of(peer)] = xs[:, lanes]
            f_ref[peer, :nst, :] = f_t[:, lanes]
            f_ref[peer, nst:, :] = lq[:, lanes]

            @pl.when(peer != me)
            def _():
                send_f(peer).start()

        return 0

    lax.fori_loop(0, blocks, fresh_f, 0)

    head_exp = jnp.exp(cumul)
    exp2 = jnp.concatenate(split2(head_exp), axis=1)
    load_g.wait()

    def fresh_g(step, _):
        peers = targets(step)
        gs = (columns(g_ref, peers).astype(F32) * mm(exp2, spread(peers))).astype(BF)
        g_t = mm(c_t, gs).astype(BF)
        for i, peer in enumerate(peers):
            lanes = slice(i * LANES, (i + 1) * LANES)
            gs_ref[:, lanes_of(peer)] = gs[:, lanes]
            gt_ref[peer] = g_t[:, lanes]

            @pl.when(peer != me)
            def _():
                send_g(peer).start()

        return 0

    lax.fori_loop(0, blocks, fresh_g, 0)

    lt_ref[...] = cumul.T
    u3 = jnp.concatenate(split3(jnp.log(jnp.maximum(dt, 1e-37)) - cumul), axis=1)
    st_ref[...] = mm_nt(b_rows, c_rows)
    lane = lax.broadcasted_iota(jnp.int32, (seq, LANES), 1)
    lane_head = lax.broadcasted_iota(jnp.int32, (half, heads), 1)
    upper = lax.broadcasted_iota(jnp.int32, (half, half), 0) <= lax.broadcasted_iota(
        jnp.int32, (half, half), 1
    )
    row_head = lax.rem(lax.broadcasted_iota(jnp.int32, (3 * heads, LANES), 0), heads)
    nt_ref[...] = jnp.zeros_like(nt_ref)
    col_ref[...] = jnp.zeros_like(col_ref)

    def within(pair, _):
        cols = pl.ds(pl.multiple_of(pair * LANES, LANES), LANES)
        xk = x_ref[:, cols]
        gk = g_ref[:, cols]
        total_lo = jnp.zeros((half, LANES), F32)
        total_hi = jnp.zeros((half, LANES), F32)
        for side in range(2):
            h = pair * 2 + side
            mine_lane = (lane < 64) if side == 0 else (lane >= 64)
            xm = jnp.where(mine_lane, xk, jnp.zeros_like(xk))
            gm = jnp.where(mine_lane, gk, jnp.zeros_like(gk))
            u = mm(u3, (row_head == h).astype(BF))
            lt = lt_ref[pl.ds(h, 1), :]
            w0 = mm_nt(xm[:half], gk)
            w1 = mm_nt(xm[half:], gk[half:])
            a00 = jnp.where(upper, jnp.exp(u[:half] + lt[:, :half]), 0.0)
            a01 = jnp.exp(u[:half] + lt[:, half:])
            a11 = jnp.where(upper, jnp.exp(u[half:] + lt[:, half:]), 0.0)
            s00 = st_ref[:half, :half]
            s01 = st_ref[:half, half:]
            s11 = st_ref[half:, half:]
            p00 = a00 * w0[:, :half]
            p01 = a01 * w0[:, half:]
            p11 = a11 * w1
            nt_ref[:half, :half] += p00
            nt_ref[:half, half:] += p01
            nt_ref[half:, half:] += p11
            total_lo += mm((a00 * s00).astype(BF), gm[:half]) + mm((a01 * s01).astype(BF), gm[half:])
            total_hi += mm((a11 * s11).astype(BF), gm[half:])
            z00 = p00 * s00
            z01 = p01 * s01
            z11 = p11 * s11
            rt_ref[h, :, :half] = jnp.sum(z00, axis=0, keepdims=True)
            rt_ref[h, :, half:] = jnp.sum(z01 + z11, axis=0, keepdims=True)
            col_ref[:half, :] += jnp.where(
                lane_head == h, jnp.sum(z00 + z01, axis=1, keepdims=True), 0.0
            )
            col_ref[half:, :] += jnp.where(
                lane_head == h, jnp.sum(z11, axis=1, keepdims=True), 0.0
            )
        hrow_ref[:, cols] = jnp.sum(xk.astype(F32) * gk.astype(F32), axis=0, keepdims=True)
        gxw_ref[:half, cols] = total_lo
        gxw_ref[half:, cols] = total_hi
        turned = in_ref[:, cols].astype(F32).T.astype(BF)
        for i in range(dp):
            int_ref[i % 2, pair * sets + i // 2] = turned[i * 32 : (i + 1) * 32]
        return 0

    first_part = (pairs * 5) // 8
    lax.fori_loop(0, first_part, within, 0)

    def decay_of(i):
        parts = gotf_ref[i, nst:, :].astype(F32)
        return jnp.exp(parts[0:1] + parts[1:2] + parts[2:3])

    gotf_ref[me] = f_ref[me]
    wait_for(gotf_ref, wide - 1, in_sem.at[0])

    def advance_f(i, state):
        h_ref[i] = state.astype(BF)
        return state * decay_of(i) + gotf_ref[i, :nst, :].astype(F32)

    start = jnp.zeros((nst, LANES), F32)
    lax.fori_loop(0, wide, advance_f, start)

    def give_h(k, _):
        send_h(k).start()
        return 0

    lax.fori_loop(1, wide, give_h, 0)
    goth_ref[me] = h_ref[me]

    lax.fori_loop(first_part, pairs, within, 0)
    sib_in.start()

    gotg_ref[me] = gt_ref[me]
    wait_for(gotg_ref, wide - 1, in_sem.at[1])

    def advance_g(k, pull):
        i = wide - 1 - k
        p_ref[i] = pull.astype(BF)
        return pull * decay_of(i) + gotg_ref[i].astype(F32)

    lax.fori_loop(0, wide, advance_g, start)

    def give_p(k, _):
        send_p(k).start()
        return 0

    lax.fori_loop(1, wide, give_p, 0)
    gotp_ref[me] = p_ref[me]

    n_low = nt_ref[...].astype(BF)
    g_b = mm(n_low, c_rows)
    g_c = mm(nt_ref[...].T.astype(BF), b_rows)

    skip_hi, skip_lo = split2(skip_ref[...])
    skip_rows = jnp.concatenate(
        [jnp.concatenate([skip_hi, skip_lo], axis=1)]
        + [jnp.concatenate([v, none], axis=1) for v in (lq_hi, lq_mid, lq_lo)]
        + [jnp.zeros((12, 2 * heads), BF)],
        axis=0,
    )
    def finish_f(step, carried):
        row_st, gc = carried
        peers = sources(step)
        wait_step(goth_ref, rh_sem, step)
        h0 = joined(goth_ref, peers)
        gs = columns(gs_ref, peers)
        y_st = mm(c_rows, h0)
        row_st += mm((gs.astype(F32) * y_st).astype(BF), gathered(peers))
        gc += mm_nt(gs, h0)
        return row_st, gc

    zero_h = jnp.zeros((seq, heads), F32)
    row_st, g_c = lax.fori_loop(0, blocks, finish_f, (zero_h, g_c))
    mine_c[...] = g_c.astype(BF)
    sibling_c.start()

    upper_all = (pos_r <= pos_c).astype(BF)

    def suffix(v):
        hi, mid, lo = split3(v)
        return mm(upper_all, hi) + mm(upper_all, mid) + mm(upper_all, lo)

    early = suffix(rt_ref[:, 0, :].T + row_st - col_ref[...])
    gate = 1.0 / (1.0 + jnp.exp(-dt_pre))
    ratio = jnp.where(dt > 0.0, gate / jnp.where(dt > 0.0, dt, 1.0), 1.0)

    def finish_g(step, carried):
        col_st, gb, sums = carried
        peers = sources(step)
        wait_step(gotp_ref, rp_sem, step)
        r = spread(peers)
        gather = gathered(peers)
        dh = joined(gotp_ref, peers)
        xs = columns(xs_ref, peers)
        u_st = mm(b_rows, dh)
        rows = mm(skip_rows, r)
        gx = columns(gxw_ref, peers) + mm(tail2, r) * u_st
        gx = (gx + rows[0:1] * columns(g_ref, peers).astype(F32)).astype(BF)
        col_st += mm((xs.astype(F32) * u_st).astype(BF), gather)
        gb += mm_nt(xs, dh)
        ended = joined(goth_ref, peers).astype(F32) * jnp.exp(rows[1:2] + rows[2:3] + rows[3:4])
        ended += joined(f_ref, peers).astype(F32)
        heads_in = jnp.concatenate(
            [jnp.sum(ended * dh.astype(F32), axis=0, keepdims=True), columns(hrow_ref, peers)], axis=0
        )
        hi, lo = split2(heads_in)
        sums += mm(hi, gather) + mm(lo, gather)
        for i, peer in enumerate(peers):
            cols = lanes_of(peer)
            xo_ref[:, cols] = gx[:, i * LANES : (i + 1) * LANES]
            pltpu.make_async_copy(xo_ref.at[:, cols], xg_hbm.at[:, cols], store_sem.at[0]).start()
        return col_st, gb, sums

    def weigh(mine_p, sib_p, out, got, which, packed):
        def step_of(step, _):
            order = [
                lax.rem(mine + (step * WEIGHED + i + 1) * STRIDE_W, slots) for i in range(WEIGHED)
            ]
            ours = jnp.concatenate([int_ref[core, slot] for slot in order], axis=0)
            theirs = jnp.concatenate([sib_ref[slot] for slot in order], axis=0)
            w = mm(ours, mine_p[...]) + mm(theirs, sib_p[...])
            for i, slot in enumerate(order):
                at = w[i * 32 : (i + 1) * 32]
                if packed:
                    out[slot, :, : 2 * heads] = jnp.concatenate([at[:16], at[16:]], axis=1).astype(BF)
                else:
                    out[slot] = at.astype(BF)

                @pl.when(slot != mine)
                def _():
                    send_w(out, got, which, slot).start()

            return 0

        lax.fori_loop(0, slots // WEIGHED, step_of, 0)

    carried = lax.fori_loop(0, blocks // 4, finish_g, (zero_h, g_b, jnp.zeros((2, heads), F32)))
    sib_in.wait_recv()
    sibling_c.wait_recv()
    weigh(mine_c, sib_c, out_c, got_c, 4, False)
    col_st, g_b, sums = lax.fori_loop(blocks // 4, blocks, finish_g, carried)
    mine_b[...] = g_b.astype(BF)
    sibling_b.start()

    d_log = early - suffix(col_st) + sums[0:1]
    g_dt = (col_ref[...] + col_st) * ratio + rate * d_log * gate
    mine_d[...] = g_dt.astype(BF)
    sibling_d.start()
    g_alog = jnp.sum(d_log * log_rate, axis=0, keepdims=True)
    g_bias = jnp.sum(g_dt, axis=0, keepdims=True)
    hg_ref[...] = jnp.zeros_like(hg_ref)
    hg_ref[0:1, :heads] = g_alog
    hg_ref[1:2, :heads] = g_bias
    hg_ref[2:3, :heads] = sums[1:2]
    sib_h.start()

    ga, gi = mine // group, lax.rem(mine, group)

    def send_a(i):
        return remote(ha_ref.at[gi], ha_ref.at[gi], out_sem.at[7], in_sem.at[7], at_slot(ga * group + i))

    def send_b(i):
        return remote(hb_ref.at[ga], hb_ref.at[ga], out_sem.at[8], in_sem.at[8], at_slot(i * group + gi))

    def start_a(k, _):
        send_a(lax.rem(gi + k, group)).start()
        return 0

    def start_b(k, _):
        send_b(lax.rem(ga + k, groups)).start()
        return 0

    sibling_b.wait_recv()
    weigh(mine_b, sib_b, out_b, got_b, 5, False)
    sib_h.wait_recv()
    ha_ref[gi] = hg_ref[...] + hsib_ref[...]
    lax.fori_loop(1, group, start_a, 0)
    sibling_d.wait_recv()
    weigh(mine_d, sib_d, out_d, got_d, 6, True)

    def emit(j, _):
        cols = pl.ds(pl.multiple_of(j * BLOCK, BLOCK), BLOCK)
        d_in = mm_nt(mine_b[...], wbc_ref[cols, :nst]) + mm_nt(mine_c[...], wbc_ref[cols, nst:])
        d_in += mm(mine_d[...], wdt_ref[:, cols])
        io_ref[:, cols] = d_in.astype(BF)
        pltpu.make_async_copy(io_ref.at[:, cols], ig_hbm.at[:, cols], store_sem.at[1]).start()
        return 0

    lax.fori_loop(0, blocks // 2, emit, 0)
    wait_for(ha_ref, group - 1, in_sem.at[7])
    hb_ref[ga] = jnp.sum(ha_ref[...], axis=0)
    lax.fori_loop(1, groups, start_b, 0)
    lax.fori_loop(blocks // 2, blocks, emit, 0)

    for at, ref in enumerate((f_ref, gt_ref, h_ref, p_ref)):
        wait_for(ref, wide - 1, out_sem.at[at])
    wait_for(ha_ref, group - 1, out_sem.at[7])
    pltpu.make_async_copy(xo_ref, xg_hbm, store_sem.at[0]).wait()
    pltpu.make_async_copy(io_ref, ig_hbm, store_sem.at[1]).wait()
    sib_in.wait_send()
    sibling_c.wait_send()
    sibling_b.wait_send()
    sibling_d.wait_send()
    sib_h.wait_send()

    wait_for(hb_ref, groups - 1, in_sem.at[8])
    rows = jnp.sum(hb_ref[...], axis=0)
    at = lax.broadcasted_iota(jnp.int32, rows.shape, 1)
    per = heads // wide
    for i in range(per):
        picked = jnp.sum(jnp.where(at == me * per + i, rows, 0.0), axis=1, keepdims=True)
        for r in range(3):
            head_out[i : i + 1, r : r + 1] = picked[r : r + 1]

    def total(out, got, which):
        got[mine] = out[mine]
        wait_for(got, slots - 1, in_sem.at[which])

        def add(k, acc):
            return acc + jnp.sum(got[pl.ds(k * group, group)].astype(F32), axis=0)

        return lax.fori_loop(0, groups, add, jnp.zeros(got.shape[1:], F32))

    wbc_out[:, LANES:] = total(out_c, got_c, 4)
    wbc_out[:, :LANES] = total(out_b, got_b, 5)
    acc = total(out_d, got_d, 6)
    wdt_out[0:16, :] = acc[:, :heads]
    wdt_out[16:32, :] = acc[:, heads : 2 * heads]
    for which, ref in ((4, out_c), (5, out_b), (6, out_d)):
        wait_for(ref, slots - 1, out_sem.at[which])
    wait_for(hb_ref, groups - 1, out_sem.at[8])


def place_kernel(
    x_in, i_in, b_in, d_in, h_in, x_out, i_out, b_out, d_out, h_out,
    x_ref, i_ref, b_ref, d_ref, h_ref, come, go, come_small, go_small,
):
    steps = []
    for a, (src, mid, dst) in enumerate(((b_in, b_ref, b_out), (d_in, d_ref, d_out), (h_in, h_ref, h_out))):
        steps.append((
            pltpu.make_async_copy(src, mid, come_small.at[a]),
            pltpu.make_async_copy(mid, dst, go_small.at[a]),
        ))
    for q in range(PIECES):
        for a, (src, mid, dst) in enumerate(((x_in, x_ref, x_out), (i_in, i_ref, i_out))):
            rows = src.shape[0] // PIECES
            part = pl.ds(q * rows, rows)
            steps.append((
                pltpu.make_async_copy(src.at[part], mid.at[part], come.at[a, q]),
                pltpu.make_async_copy(mid.at[part], dst.at[part], go.at[a, q]),
            ))
    for first, _ in steps:
        first.start()
    for first, second in steps:
        first.wait()
        second.start()
    for _, second in steps:
        second.wait()


def local(wide, dp, layer_input, inner_acts, w_bc, w_dt, a_log, dt_bias, d_skip, out_grad):
    seq, width = layer_input.shape[1:]
    heads = a_log.shape[0]
    nst = w_bc.shape[1] // 2
    slots = wide * dp // 2
    rows = width // (wide * dp)
    any_spec = pl.BlockSpec(memory_space=pl.ANY)
    vmem = pl.BlockSpec(memory_space=pltpu.VMEM)
    dma = pltpu.SemaphoreType.DMA
    v = pltpu.VMEM
    x_grad, input_grad, wbc_grad, wdt_grad, head_grads = pl.pallas_call(
        functools.partial(scan_kernel, wide, dp),
        out_shape=(
            jax.ShapeDtypeStruct((seq, width), BF),
            jax.ShapeDtypeStruct((seq, width), BF),
            jax.ShapeDtypeStruct((rows, 2 * nst), F32),
            jax.ShapeDtypeStruct((rows, heads), F32),
            jax.ShapeDtypeStruct((heads // wide, 3), F32),
        ),
        in_specs=[any_spec] * 5 + [vmem] * 3,
        out_specs=(any_spec, any_spec, vmem, vmem, vmem),
        scratch_shapes=[
            v((seq, width), BF),
            v((seq, width), BF),
            v((seq, width), BF),
            v((width, 2 * nst), BF),
            v((heads, width), BF),
            v((wide, nst + 16, LANES), BF),
            v((wide, nst, LANES), BF),
            v((wide, nst + 16, LANES), BF),
            v((wide, nst, LANES), BF),
            v((wide, nst, LANES), BF),
            v((wide, nst, LANES), BF),
            v((wide, nst, LANES), BF),
            v((wide, nst, LANES), BF),
            v((seq, width), BF),
            v((seq, width), BF),
            v((seq, width), F32),
            v((2, slots, 32, seq), BF),
            v((slots, 32, seq), BF),
            v((seq, seq), F32),
            v((seq, seq), F32),
            v((heads, seq), F32),
            v((heads, 1, seq), F32),
            v((seq, heads), F32),
            v((1, width), F32),
            v((seq, width), BF),
            v((seq, width), BF),
            v((seq, nst), BF),
            v((seq, nst), BF),
            v((seq, heads), BF),
            v((seq, nst), BF),
            v((seq, nst), BF),
            v((seq, heads), BF),
            v((8, LANES), F32),
            v((8, LANES), F32),
            v((8, 8, LANES), F32),
            v((slots // 8, 8, LANES), F32),
            v((slots, 32, LANES), BF),
            v((slots, 32, LANES), BF),
            v((slots, 16, LANES), BF),
            v((slots, 32, LANES), BF),
            v((slots, 32, LANES), BF),
            v((slots, 16, LANES), BF),
            dma((4, 4)),
            dma((2,)),
            dma((5,)),
            dma((5,)),
            dma((9,)),
            dma((9,)),
            dma((width // BLOCK,)),
            dma((width // BLOCK,)),
        ],
        compiler_params=pltpu.CompilerParams(
            collective_id=0, has_side_effects=True, vmem_limit_bytes=56 * 1024 * 1024
        ),
        cost_estimate=pl.CostEstimate(
            flops=30 * seq * width * 256, bytes_accessed=8 * seq * width, transcendentals=0
        ),
        name="scan_backward",
    )(
        layer_input[0], inner_acts[0], out_grad[0], w_bc, w_dt.T,
        a_log[None], dt_bias[None], d_skip[None],
    )
    x_grad, input_grad, wbc_grad, wdt_grad, head_grads = pl.pallas_call(
        place_kernel,
        out_shape=tuple(
            jax.ShapeDtypeStruct(a.shape, a.dtype)
            for a in (x_grad, input_grad, wbc_grad, wdt_grad, head_grads)
        ),
        in_specs=[any_spec] * 5,
        out_specs=[any_spec] * 5,
        scratch_shapes=[
            v(a.shape, a.dtype) for a in (x_grad, input_grad, wbc_grad, wdt_grad, head_grads)
        ]
        + [dma((2, PIECES)), dma((2, PIECES)), dma((3,)), dma((3,))],
        compiler_params=pltpu.CompilerParams(vmem_limit_bytes=60 * 1024 * 1024),
        name="place_results",
    )(x_grad, input_grad, wbc_grad, wdt_grad, head_grads)
    return x_grad[None], input_grad[None], wbc_grad, wdt_grad, head_grads.T


def solution(mesh):
    in_specs = (
        P("dp", "wide", None),
        P("dp", "wide", None),
        P(),
        P(),
        P(),
        P(),
        P(),
        P("dp", "wide", None),
    )
    out_specs = (
        P("dp", "wide", None),
        P("dp", "wide", None),
        P(("wide", "dp"), None),
        P(("wide", "dp"), None),
        P(None, "wide"),
    )
    return jax.shard_map(
        functools.partial(local, mesh.shape["wide"], mesh.shape["dp"]),
        mesh=mesh,
        in_specs=in_specs,
        out_specs=out_specs,
        check_vma=False,
    )
```

```python
import functools

import jax
import jax.numpy as jnp
from jax import lax
from jax.experimental import pallas as pl
from jax.experimental.pallas import tpu as pltpu
from jax.sharding import PartitionSpec as P

MESH = pl.DeviceIdType.MESH
BF = jnp.bfloat16
F32 = jnp.float32
LANES = 128
BLOCK = 512
STRIDE = 13
STRIDE_W = 27
WEIGHED = 16
PIECES = 2


def mm(a, b):
    return jnp.dot(a, b, preferred_element_type=F32)


def mm_nt(a, b):
    return lax.dot_general(a, b, (((1,), (1,)), ((), ())), preferred_element_type=F32)


def split2(v):
    hi = v.astype(BF)
    return hi, (v - hi.astype(F32)).astype(BF)


def split3(v):
    hi = v.astype(BF)
    rest = v - hi.astype(F32)
    mid = rest.astype(BF)
    return hi, mid, (rest - mid.astype(F32)).astype(BF)


def scan_kernel(
    wide, dp, in_hbm, x_hbm, g_hbm, wbc_hbm, wdt_hbm, alog_hbm, bias_hbm, skip_hbm,
    xg_hbm, ig_hbm, wbc_out, wdt_out, head_out,
    small_ref, in_ref, x_ref, g_ref, wbc_ref, wdt_ref, end_ref, gote_ref, f_ref, gt_ref, gotf_ref, gotg_ref, h_ref, p_ref,
    goth_ref, gotp_ref, xs_ref, gs_ref, gxw_ref, int_ref, sib_ref, nt_ref, st_ref, lt_ref, rt_ref,
    col_ref, hrow_ref, xo_ref, io_ref, mine_c, mine_b, mine_d, sib_c, sib_b, sib_d,
    hg_ref, hsib_ref, ha_ref, hb_ref, out_c, out_b, out_d, got_c, got_b, got_d,
    load_sem, store_sem, sib_send, sib_recv,
    out_sem, in_sem, rh_sem, rp_sem,
):
    me = lax.axis_index("wide")
    place = lax.axis_index("dp")
    core = lax.rem(place, 2)
    other = 1 - core
    sets = dp // 2
    slots = wide * sets
    mine = me * sets + place // 2
    seq, width = in_ref.shape
    heads = alog_hbm.shape[1]
    half = seq // 2
    nst = wbc_ref.shape[1] // 2
    owners = BLOCK // LANES
    blocks = width // BLOCK
    per_block = BLOCK // 64
    pairs = width // LANES
    group = 8
    groups = slots // group
    sibling = {"wide": me, "dp": place - core + other}

    def at_slot(slot):
        return {"wide": slot // sets, "dp": lax.rem(slot, sets) * 2 + core}

    def to_peer(k):
        return lax.rem(me + k * STRIDE, wide)

    def from_peer(k):
        return lax.rem(me + (wide - k) * STRIDE, wide)

    def targets(step):
        return [to_peer(step * owners + i + 1) for i in range(owners)]

    def sources(step):
        return [from_peer(step * owners + i + 1) for i in range(owners)]

    def lanes_of(p):
        return pl.ds(pl.multiple_of(p * LANES, LANES), LANES)

    def columns(ref, peers):
        return jnp.concatenate([ref[:, lanes_of(p)] for p in peers], axis=1)

    def joined(ref, peers):
        return jnp.concatenate([ref[p, :nst, :] for p in peers], axis=1)

    barrier = pltpu.get_barrier_semaphore()
    pl.semaphore_signal(barrier, inc=1, device_id=sibling, device_id_type=MESH)

    def greet(k, _):
        pl.semaphore_signal(
            barrier, inc=1, device_id=at_slot(lax.rem(mine + k, slots)), device_id_type=MESH
        )
        return 0

    lax.fori_loop(1, slots, greet, 0)

    quarter = width // 4
    loads = []
    for q in range(4):
        part = pl.ds(q * quarter, quarter)
        loads.append((
            pltpu.make_async_copy(in_hbm.at[:, part], in_ref.at[:, part], load_sem.at[0, q]),
            pltpu.make_async_copy(wbc_hbm.at[part], wbc_ref.at[part], load_sem.at[1, q]),
            pltpu.make_async_copy(wdt_hbm.at[:, part], wdt_ref.at[:, part], load_sem.at[2, q]),
        ))
    smalls = [
        pltpu.make_async_copy(src, dst, load_sem.at[3, 2])
        for src, dst in ((alog_hbm, small_ref.at[0]), (bias_hbm, small_ref.at[1]), (skip_hbm, small_ref.at[2]))
    ]
    load_x = pltpu.make_async_copy(x_hbm, x_ref, load_sem.at[3, 0])
    load_g = pltpu.make_async_copy(g_hbm, g_ref, load_sem.at[3, 1])
    for load in loads:
        for one in load:
            one.start()
    for one in smalls:
        one.start()
    load_x.start()
    load_g.start()

    narrow = lax.rem(
        lax.broadcasted_iota(jnp.int32, (2 * heads, LANES), 0), heads
    ) - lax.broadcasted_iota(jnp.int32, (2 * heads, LANES), 1) // 64
    gather_delta = lax.broadcasted_iota(jnp.int32, (LANES, heads), 1) - lax.broadcasted_iota(
        jnp.int32, (LANES, heads), 0
    ) // 64

    def spread(peers):
        return jnp.concatenate([(narrow == 2 * p).astype(BF) for p in peers], axis=1)

    def gathered(peers):
        return jnp.concatenate([(gather_delta == 2 * p).astype(BF) for p in peers], axis=0)

    def remote(src, dst, send, recv, target):
        return pltpu.make_async_remote_copy(
            src_ref=src, dst_ref=dst, send_sem=send, recv_sem=recv, device_id=target,
            device_id_type=MESH,
        )

    def send_f(peer):
        return remote(f_ref.at[peer], gotf_ref.at[me], out_sem.at[0], in_sem.at[0], {"wide": peer})

    def send_e(peer):
        return remote(end_ref.at[peer], gote_ref.at[me], out_sem.at[9], in_sem.at[9], {"wide": peer})

    def send_g(peer):
        return remote(gt_ref.at[peer], gotg_ref.at[me], out_sem.at[1], in_sem.at[1], {"wide": peer})

    def send_h(k):
        peer = to_peer(k)
        step = (k - 1) // owners
        return remote(h_ref.at[peer], goth_ref.at[me], out_sem.at[2], rh_sem.at[step], {"wide": peer})

    def send_p(k):
        peer = to_peer(k)
        step = (k - 1) // owners
        return remote(p_ref.at[peer], gotp_ref.at[me], out_sem.at[3], rp_sem.at[step], {"wide": peer})

    def send_w(out, got, which, slot):
        return remote(out.at[slot], got.at[mine], out_sem.at[which], in_sem.at[which], at_slot(slot))

    def wait_for(ref, count, sem):
        part = ref.at[pl.ds(0, count)]
        pltpu.make_async_copy(part, part, sem).wait()

    def wait_step(ref, sem, step):
        @pl.when(step < blocks - 1)
        def _():
            wait_for(ref, owners, sem.at[step])

        @pl.when(step == blocks - 1)
        def _():
            wait_for(ref, owners - 1, sem.at[step])

    sib_in = remote(int_ref.at[other], sib_ref, sib_send.at[0], sib_recv.at[0], sibling)
    sibling_c = remote(mine_c, sib_c, sib_send.at[1], sib_recv.at[1], sibling)
    sibling_b = remote(mine_b, sib_b, sib_send.at[2], sib_recv.at[2], sibling)
    sibling_d = remote(mine_d, sib_d, sib_send.at[3], sib_recv.at[3], sibling)
    sib_h = remote(hg_ref, hsib_ref, sib_send.at[4], sib_recv.at[4], sibling)

    pltpu.make_async_copy(small_ref, small_ref, load_sem.at[3, 2]).wait()
    bc = jnp.zeros((seq, 2 * nst), F32)
    dt_raw = jnp.zeros((seq, heads), F32)
    for q, load in enumerate(loads):
        for one in load:
            one.wait()
        part = slice(q * quarter, (q + 1) * quarter)
        bc += mm(in_ref[:, part], wbc_ref[part, :])
        dt_raw += mm_nt(in_ref[:, part], wdt_ref[:, part])
    bc = bc.astype(BF)
    dt_raw = dt_raw.astype(BF).astype(F32)
    b_rows = bc[:, :nst]
    c_rows = bc[:, nst:]
    b_t = b_rows.astype(F32).T.astype(BF)
    c_t = c_rows.astype(F32).T.astype(BF)
    dt_pre = dt_raw + small_ref[1]
    dt = jnp.maximum(dt_pre, 0.0) + jnp.log1p(jnp.exp(-jnp.abs(dt_pre)))
    rate = -jnp.exp(small_ref[0])
    log_rate = dt * rate
    pos_r = lax.broadcasted_iota(jnp.int32, (seq, seq), 0)
    pos_c = lax.broadcasted_iota(jnp.int32, (seq, seq), 1)
    lower = (pos_r >= pos_c).astype(BF)
    lr_hi, lr_mid, lr_lo = split3(log_rate)
    cumul = mm(lower, lr_hi) + mm(lower, lr_mid) + mm(lower, lr_lo)
    last = cumul[seq - 1 :, :]
    tail = dt * jnp.exp(last - cumul)
    tail2 = jnp.concatenate(split2(tail), axis=1)
    lq_hi, lq_mid, lq_lo = split3(last)
    none = jnp.zeros((1, heads), BF)
    lq_rows = jnp.concatenate(
        [jnp.concatenate([v, none], axis=1) for v in (lq_hi, lq_mid, lq_lo)]
        + [jnp.zeros((13, 2 * heads), BF)],
        axis=0,
    )

    load_x.wait()
    pl.semaphore_wait(barrier, slots)

    def fresh_f(step, _):
        peers = targets(step)
        r = spread(peers)
        xs = (columns(x_ref, peers).astype(F32) * mm(tail2, r)).astype(BF)
        f_t = mm(b_t, xs).astype(BF)
        ends = mm(lq_rows, r)
        ends = ends[0:1] + ends[1:2] + ends[2:3]
        for i, peer in enumerate(peers):
            lanes = slice(i * LANES, (i + 1) * LANES)
            xs_ref[:, lanes_of(peer)] = xs[:, lanes]
            f_ref[peer] = f_t[:, lanes]
            end_ref[peer] = ends[:, lanes]

            @pl.when(peer != me)
            def _():
                send_f(peer).start()
                send_e(peer).start()

        return 0

    lax.fori_loop(0, blocks, fresh_f, 0)

    head_exp = jnp.exp(cumul)
    exp2 = jnp.concatenate(split2(head_exp), axis=1)
    load_g.wait()

    def fresh_g(step, _):
        peers = targets(step)
        gs = (columns(g_ref, peers).astype(F32) * mm(exp2, spread(peers))).astype(BF)
        g_t = mm(c_t, gs).astype(BF)
        for i, peer in enumerate(peers):
            lanes = slice(i * LANES, (i + 1) * LANES)
            gs_ref[:, lanes_of(peer)] = gs[:, lanes]
            gt_ref[peer] = g_t[:, lanes]

            @pl.when(peer != me)
            def _():
                send_g(peer).start()

        return 0

    lax.fori_loop(0, blocks, fresh_g, 0)

    lt_ref[...] = cumul.T
    u3 = jnp.concatenate(split3(jnp.log(jnp.maximum(dt, 1e-37)) - cumul), axis=1)
    st_ref[...] = mm_nt(b_rows, c_rows)
    lane = lax.broadcasted_iota(jnp.int32, (seq, LANES), 1)
    lane_head = lax.broadcasted_iota(jnp.int32, (half, heads), 1)
    upper = lax.broadcasted_iota(jnp.int32, (half, half), 0) <= lax.broadcasted_iota(
        jnp.int32, (half, half), 1
    )
    row_head = lax.rem(lax.broadcasted_iota(jnp.int32, (3 * heads, LANES), 0), heads)
    nt_ref[...] = jnp.zeros_like(nt_ref)
    col_ref[...] = jnp.zeros_like(col_ref)

    def within(pair, _):
        cols = pl.ds(pl.multiple_of(pair * LANES, LANES), LANES)
        xk = x_ref[:, cols]
        gk = g_ref[:, cols]
        total_lo = jnp.zeros((half, LANES), F32)
        total_hi = jnp.zeros((half, LANES), F32)
        for side in range(2):
            h = pair * 2 + side
            mine_lane = (lane < 64) if side == 0 else (lane >= 64)
            xm = jnp.where(mine_lane, xk, jnp.zeros_like(xk))
            gm = jnp.where(mine_lane, gk, jnp.zeros_like(gk))
            u = mm(u3, (row_head == h).astype(BF))
            lt = lt_ref[pl.ds(h, 1), :]
            w0 = mm_nt(xm[:half], gk)
            w1 = mm_nt(xm[half:], gk[half:])
            a00 = jnp.where(upper, jnp.exp(u[:half] + lt[:, :half]), 0.0)
            a01 = jnp.exp(u[:half] + lt[:, half:])
            a11 = jnp.where(upper, jnp.exp(u[half:] + lt[:, half:]), 0.0)
            s00 = st_ref[:half, :half]
            s01 = st_ref[:half, half:]
            s11 = st_ref[half:, half:]
            p00 = a00 * w0[:, :half]
            p01 = a01 * w0[:, half:]
            p11 = a11 * w1
            nt_ref[:half, :half] += p00
            nt_ref[:half, half:] += p01
            nt_ref[half:, half:] += p11
            total_lo += mm((a00 * s00).astype(BF), gm[:half]) + mm((a01 * s01).astype(BF), gm[half:])
            total_hi += mm((a11 * s11).astype(BF), gm[half:])
            z00 = p00 * s00
            z01 = p01 * s01
            z11 = p11 * s11
            rt_ref[h, :, :half] = jnp.sum(z00, axis=0, keepdims=True)
            rt_ref[h, :, half:] = jnp.sum(z01 + z11, axis=0, keepdims=True)
            col_ref[:half, :] += jnp.where(
                lane_head == h, jnp.sum(z00 + z01, axis=1, keepdims=True), 0.0
            )
            col_ref[half:, :] += jnp.where(
                lane_head == h, jnp.sum(z11, axis=1, keepdims=True), 0.0
            )
        hrow_ref[:, cols] = jnp.sum(xk.astype(F32) * gk.astype(F32), axis=0, keepdims=True)
        gxw_ref[:half, cols] = total_lo
        gxw_ref[half:, cols] = total_hi
        turned = in_ref[:, cols].astype(F32).T.astype(BF)
        for i in range(dp):
            int_ref[i % 2, pair * sets + i // 2] = turned[i * 32 : (i + 1) * 32]
        return 0

    first_part = (pairs * 5) // 8
    lax.fori_loop(0, first_part, within, 0)

    def decay_of(i):
        return jnp.exp(gote_ref[i])

    gotf_ref[me] = f_ref[me]
    gote_ref[me] = end_ref[me]
    wait_for(gote_ref, wide - 1, in_sem.at[9])
    wait_for(gotf_ref, wide - 1, in_sem.at[0])

    def advance_f(i, state):
        h_ref[i] = state.astype(BF)
        return state * decay_of(i) + gotf_ref[i].astype(F32)

    start = jnp.zeros((nst, LANES), F32)
    lax.fori_loop(0, wide, advance_f, start)

    def give_h(k, _):
        send_h(k).start()
        return 0

    lax.fori_loop(1, wide, give_h, 0)
    goth_ref[me] = h_ref[me]

    lax.fori_loop(first_part, pairs, within, 0)
    sib_in.start()

    gotg_ref[me] = gt_ref[me]
    wait_for(gotg_ref, wide - 1, in_sem.at[1])

    def advance_g(k, pull):
        i = wide - 1 - k
        p_ref[i] = pull.astype(BF)
        return pull * decay_of(i) + gotg_ref[i].astype(F32)

    lax.fori_loop(0, wide, advance_g, start)

    def give_p(k, _):
        send_p(k).start()
        return 0

    lax.fori_loop(1, wide, give_p, 0)
    gotp_ref[me] = p_ref[me]

    n_low = nt_ref[...].astype(BF)
    g_b = mm(n_low, c_rows)
    g_c = mm(nt_ref[...].T.astype(BF), b_rows)

    skip_hi, skip_lo = split2(small_ref[2])
    skip_rows = jnp.concatenate(
        [jnp.concatenate([skip_hi, skip_lo], axis=1)]
        + [jnp.concatenate([v, none], axis=1) for v in (lq_hi, lq_mid, lq_lo)]
        + [jnp.zeros((12, 2 * heads), BF)],
        axis=0,
    )
    def finish_f(step, carried):
        row_st, gc = carried
        peers = sources(step)
        wait_step(goth_ref, rh_sem, step)
        h0 = joined(goth_ref, peers)
        gs = columns(gs_ref, peers)
        y_st = mm(c_rows, h0)
        row_st += mm((gs.astype(F32) * y_st).astype(BF), gathered(peers))
        gc += mm_nt(gs, h0)
        return row_st, gc

    zero_h = jnp.zeros((seq, heads), F32)
    row_st, g_c = lax.fori_loop(0, blocks, finish_f, (zero_h, g_c))
    mine_c[...] = g_c.astype(BF)
    sibling_c.start()

    upper_all = (pos_r <= pos_c).astype(BF)

    def suffix(v):
        hi, mid, lo = split3(v)
        return mm(upper_all, hi) + mm(upper_all, mid) + mm(upper_all, lo)

    early = suffix(rt_ref[:, 0, :].T + row_st - col_ref[...])
    gate = 1.0 / (1.0 + jnp.exp(-dt_pre))
    ratio = jnp.where(dt > 0.0, gate / jnp.where(dt > 0.0, dt, 1.0), 1.0)

    def finish_g(step, carried):
        col_st, gb, sums = carried
        peers = sources(step)
        wait_step(gotp_ref, rp_sem, step)
        r = spread(peers)
        gather = gathered(peers)
        dh = joined(gotp_ref, peers)
        xs = columns(xs_ref, peers)
        u_st = mm(b_rows, dh)
        rows = mm(skip_rows, r)
        gx = columns(gxw_ref, peers) + mm(tail2, r) * u_st
        gx = (gx + rows[0:1] * columns(g_ref, peers).astype(F32)).astype(BF)
        col_st += mm((xs.astype(F32) * u_st).astype(BF), gather)
        gb += mm_nt(xs, dh)
        ended = joined(goth_ref, peers).astype(F32) * jnp.exp(rows[1:2] + rows[2:3] + rows[3:4])
        ended += joined(f_ref, peers).astype(F32)
        heads_in = jnp.concatenate(
            [jnp.sum(ended * dh.astype(F32), axis=0, keepdims=True), columns(hrow_ref, peers)], axis=0
        )
        hi, lo = split2(heads_in)
        sums += mm(hi, gather) + mm(lo, gather)
        for i, peer in enumerate(peers):
            cols = lanes_of(peer)
            xo_ref[:, cols] = gx[:, i * LANES : (i + 1) * LANES]
        return col_st, gb, sums

    def weigh(mine_p, sib_p, out, got, which, packed):
        def step_of(step, _):
            order = [
                lax.rem(mine + (step * WEIGHED + i + 1) * STRIDE_W, slots) for i in range(WEIGHED)
            ]
            ours = jnp.concatenate([int_ref[core, slot] for slot in order], axis=0)
            theirs = jnp.concatenate([sib_ref[slot] for slot in order], axis=0)
            w = mm(ours, mine_p[...]) + mm(theirs, sib_p[...])
            for i, slot in enumerate(order):
                at = w[i * 32 : (i + 1) * 32]
                if packed:
                    out[slot, :, : 2 * heads] = jnp.concatenate([at[:16], at[16:]], axis=1).astype(BF)
                else:
                    out[slot] = at.astype(BF)

                @pl.when(slot != mine)
                def _():
                    send_w(out, got, which, slot).start()

            return 0

        lax.fori_loop(0, slots // WEIGHED, step_of, 0)

    early_steps = blocks // 2
    carried = lax.fori_loop(0, early_steps, finish_g, (zero_h, g_b, jnp.zeros((2, heads), F32)))
    sib_in.wait_recv()
    sibling_c.wait_recv()
    weigh(mine_c, sib_c, out_c, got_c, 4, False)
    col_st, g_b, sums = lax.fori_loop(early_steps, blocks, finish_g, carried)
    mine_b[...] = g_b.astype(BF)
    sibling_b.start()
    store_x = pltpu.make_async_copy(xo_ref, xg_hbm, store_sem.at[0])
    store_x.start()

    late_hi, late_lo = split2(col_st)
    d_log = early - mm(upper_all, late_hi) - mm(upper_all, late_lo) + sums[0:1]
    g_dt = (col_ref[...] + col_st) * ratio + rate * d_log * gate
    mine_d[...] = g_dt.astype(BF)
    sibling_d.start()
    g_alog = jnp.sum(d_log * log_rate, axis=0, keepdims=True)
    g_bias = jnp.sum(g_dt, axis=0, keepdims=True)
    hg_ref[...] = jnp.zeros_like(hg_ref)
    hg_ref[0:1, :heads] = g_alog
    hg_ref[1:2, :heads] = g_bias
    hg_ref[2:3, :heads] = sums[1:2]
    sib_h.start()

    ga, gi = mine // group, lax.rem(mine, group)

    def send_a(i):
        return remote(ha_ref.at[gi], ha_ref.at[gi], out_sem.at[7], in_sem.at[7], at_slot(ga * group + i))

    def send_b(i):
        return remote(hb_ref.at[ga], hb_ref.at[ga], out_sem.at[8], in_sem.at[8], at_slot(i * group + gi))

    def start_a(k, _):
        send_a(lax.rem(gi + k, group)).start()
        return 0

    def start_b(k, _):
        send_b(lax.rem(ga + k, groups)).start()
        return 0

    sibling_b.wait_recv()
    weigh(mine_b, sib_b, out_b, got_b, 5, False)
    sib_h.wait_recv()
    ha_ref[gi] = hg_ref[...] + hsib_ref[...]
    lax.fori_loop(1, group, start_a, 0)
    sibling_d.wait_recv()
    weigh(mine_d, sib_d, out_d, got_d, 6, True)

    def emit(j, _):
        cols = pl.ds(pl.multiple_of(j * BLOCK, BLOCK), BLOCK)
        d_in = mm_nt(mine_b[...], wbc_ref[cols, :nst]) + mm_nt(mine_c[...], wbc_ref[cols, nst:])
        d_in += mm(mine_d[...], wdt_ref[:, cols])
        io_ref[:, cols] = d_in.astype(BF)
        pltpu.make_async_copy(io_ref.at[:, cols], ig_hbm.at[:, cols], store_sem.at[1]).start()
        return 0

    lax.fori_loop(0, blocks // 2, emit, 0)
    wait_for(ha_ref, group - 1, in_sem.at[7])
    hb_ref[ga] = jnp.sum(ha_ref[...], axis=0)
    lax.fori_loop(1, groups, start_b, 0)
    lax.fori_loop(blocks // 2, blocks, emit, 0)

    for at, ref in ((0, f_ref), (1, gt_ref), (2, h_ref), (3, p_ref), (9, end_ref)):
        wait_for(ref, wide - 1, out_sem.at[at])
    wait_for(ha_ref, group - 1, out_sem.at[7])
    store_x.wait()
    pltpu.make_async_copy(io_ref, ig_hbm, store_sem.at[1]).wait()
    sib_in.wait_send()
    sibling_c.wait_send()
    sibling_b.wait_send()
    sibling_d.wait_send()
    sib_h.wait_send()

    wait_for(hb_ref, groups - 1, in_sem.at[8])
    rows = jnp.sum(hb_ref[...], axis=0)
    at = lax.broadcasted_iota(jnp.int32, rows.shape, 1)
    per = heads // wide
    for i in range(per):
        picked = jnp.sum(jnp.where(at == me * per + i, rows, 0.0), axis=1, keepdims=True)
        for r in range(3):
            head_out[i : i + 1, r : r + 1] = picked[r : r + 1]

    def total(out, got, which):
        got[mine] = out[mine]
        wait_for(got, slots - 1, in_sem.at[which])

        def add(k, acc):
            return acc + jnp.sum(got[pl.ds(k * group, group)].astype(F32), axis=0)

        return lax.fori_loop(0, groups, add, jnp.zeros(got.shape[1:], F32))

    wbc_out[:, LANES:] = total(out_c, got_c, 4)
    wbc_out[:, :LANES] = total(out_b, got_b, 5)
    acc = total(out_d, got_d, 6)
    wdt_out[0:16, :] = acc[:, :heads]
    wdt_out[16:32, :] = acc[:, heads : 2 * heads]
    for which, ref in ((4, out_c), (5, out_b), (6, out_d)):
        wait_for(ref, slots - 1, out_sem.at[which])
    wait_for(hb_ref, groups - 1, out_sem.at[8])


def place_kernel(
    x_in, i_in, b_in, d_in, h_in, x_out, i_out, b_out, d_out, h_out,
    x_ref, i_ref, b_ref, d_ref, h_ref, come, go, come_small, go_small,
):
    steps = []
    for a, (src, mid, dst) in enumerate(((b_in, b_ref, b_out), (d_in, d_ref, d_out), (h_in, h_ref, h_out))):
        steps.append((
            pltpu.make_async_copy(src, mid, come_small.at[a]),
            pltpu.make_async_copy(mid, dst, go_small.at[a]),
        ))
    for q in range(PIECES):
        for a, (src, mid, dst) in enumerate(((x_in, x_ref, x_out), (i_in, i_ref, i_out))):
            rows = src.shape[0] // PIECES
            part = pl.ds(q * rows, rows)
            steps.append((
                pltpu.make_async_copy(src.at[part], mid.at[part], come.at[a, q]),
                pltpu.make_async_copy(mid.at[part], dst.at[part], go.at[a, q]),
            ))
    for first, _ in steps:
        first.start()
    for first, second in steps:
        first.wait()
        second.start()
    for _, second in steps:
        second.wait()


def local(wide, dp, layer_input, inner_acts, w_bc, w_dt, a_log, dt_bias, d_skip, out_grad):
    seq, width = layer_input.shape[1:]
    heads = a_log.shape[0]
    nst = w_bc.shape[1] // 2
    slots = wide * dp // 2
    rows = width // (wide * dp)
    any_spec = pl.BlockSpec(memory_space=pl.ANY)
    vmem = pl.BlockSpec(memory_space=pltpu.VMEM)
    dma = pltpu.SemaphoreType.DMA
    v = pltpu.VMEM
    x_grad, input_grad, wbc_grad, wdt_grad, head_grads = pl.pallas_call(
        functools.partial(scan_kernel, wide, dp),
        out_shape=(
            jax.ShapeDtypeStruct((seq, width), BF),
            jax.ShapeDtypeStruct((seq, width), BF),
            jax.ShapeDtypeStruct((rows, 2 * nst), F32),
            jax.ShapeDtypeStruct((rows, heads), F32),
            jax.ShapeDtypeStruct((heads // wide, 3), F32),
        ),
        in_specs=[any_spec] * 8,
        out_specs=(any_spec, any_spec, vmem, vmem, vmem),
        scratch_shapes=[
            v((3, 1, heads), F32),
            v((seq, width), BF),
            v((seq, width), BF),
            v((seq, width), BF),
            v((width, 2 * nst), BF),
            v((heads, width), BF),
            v((wide, 1, LANES), F32),
            v((wide, 1, LANES), F32),
            v((wide, nst, LANES), BF),
            v((wide, nst, LANES), BF),
            v((wide, nst, LANES), BF),
            v((wide, nst, LANES), BF),
            v((wide, nst, LANES), BF),
            v((wide, nst, LANES), BF),
            v((wide, nst, LANES), BF),
            v((wide, nst, LANES), BF),
            v((seq, width), BF),
            v((seq, width), BF),
            v((seq, width), F32),
            v((2, slots, 32, seq), BF),
            v((slots, 32, seq), BF),
            v((seq, seq), F32),
            v((seq, seq), F32),
            v((heads, seq), F32),
            v((heads, 1, seq), F32),
            v((seq, heads), F32),
            v((1, width), F32),
            v((seq, width), BF),
            v((seq, width), BF),
            v((seq, nst), BF),
            v((seq, nst), BF),
            v((seq, heads), BF),
            v((seq, nst), BF),
            v((seq, nst), BF),
            v((seq, heads), BF),
            v((8, LANES), F32),
            v((8, LANES), F32),
            v((8, 8, LANES), F32),
            v((slots // 8, 8, LANES), F32),
            v((slots, 32, LANES), BF),
            v((slots, 32, LANES), BF),
            v((slots, 16, LANES), BF),
            v((slots, 32, LANES), BF),
            v((slots, 32, LANES), BF),
            v((slots, 16, LANES), BF),
            dma((4, 4)),
            dma((2,)),
            dma((5,)),
            dma((5,)),
            dma((10,)),
            dma((10,)),
            dma((width // BLOCK,)),
            dma((width // BLOCK,)),
        ],
        compiler_params=pltpu.CompilerParams(
            collective_id=0, has_side_effects=True, vmem_limit_bytes=56 * 1024 * 1024
        ),
        cost_estimate=pl.CostEstimate(
            flops=30 * seq * width * 256, bytes_accessed=8 * seq * width, transcendentals=0
        ),
        name="scan_backward",
    )(
        layer_input[0], inner_acts[0], out_grad[0], w_bc, w_dt.T,
        a_log[None], dt_bias[None], d_skip[None],
    )
    x_grad, input_grad, wbc_grad, wdt_grad, head_grads = pl.pallas_call(
        place_kernel,
        out_shape=tuple(
            jax.ShapeDtypeStruct(a.shape, a.dtype)
            for a in (x_grad, input_grad, wbc_grad, wdt_grad, head_grads)
        ),
        in_specs=[any_spec] * 5,
        out_specs=[any_spec] * 5,
        scratch_shapes=[
            v(a.shape, a.dtype) for a in (x_grad, input_grad, wbc_grad, wdt_grad, head_grads)
        ]
        + [dma((2, PIECES)), dma((2, PIECES)), dma((3,)), dma((3,))],
        compiler_params=pltpu.CompilerParams(vmem_limit_bytes=60 * 1024 * 1024),
        name="place_results",
    )(x_grad, input_grad, wbc_grad, wdt_grad, head_grads)
    return x_grad[None], input_grad[None], wbc_grad, wdt_grad, head_grads.T


def solution(mesh):
    in_specs = (
        P("dp", "wide", None),
        P("dp", "wide", None),
        P(),
        P(),
        P(),
        P(),
        P(),
        P("dp", "wide", None),
    )
    out_specs = (
        P("dp", "wide", None),
        P("dp", "wide", None),
        P(("wide", "dp"), None),
        P(("wide", "dp"), None),
        P(None, "wide"),
    )
    return jax.shard_map(
        functools.partial(local, mesh.shape["wide"], mesh.shape["dp"]),
        mesh=mesh,
        in_specs=in_specs,
        out_specs=out_specs,
        check_vma=False,
    )
```

```python
import functools

import jax
import jax.numpy as jnp
from jax import lax
from jax.experimental import pallas as pl
from jax.experimental.pallas import tpu as pltpu
from jax.sharding import PartitionSpec as P

MESH = pl.DeviceIdType.MESH
BF = jnp.bfloat16
F32 = jnp.float32
LANES = 128
BLOCK = 512
STRIDE = 13
STRIDE_W = 27
WEIGHED = 16
PIECES = 2


def mm(a, b):
    return jnp.dot(a, b, preferred_element_type=F32)


def mm_nt(a, b):
    return lax.dot_general(a, b, (((1,), (1,)), ((), ())), preferred_element_type=F32)


def split2(v):
    hi = v.astype(BF)
    return hi, (v - hi.astype(F32)).astype(BF)


def split3(v):
    hi = v.astype(BF)
    rest = v - hi.astype(F32)
    mid = rest.astype(BF)
    return hi, mid, (rest - mid.astype(F32)).astype(BF)


def scan_kernel(
    wide, dp, in_hbm, x_hbm, g_hbm, wbc_hbm, wdt_hbm, alog_hbm, bias_hbm, skip_hbm,
    xg_hbm, ig_hbm, wbc_out, wdt_out, head_out,
    small_ref, in_ref, x_ref, g_ref, wbc_ref, wdt_ref, end_ref, gote_ref, f_ref, gt_ref, gotf_ref, gotg_ref, h_ref, p_ref,
    goth_ref, gotp_ref, xs_ref, gs_ref, gxw_ref, int_ref, sib_ref, nt_ref, st_ref, lt_ref, rt_ref,
    col_ref, hrow_ref, xo_ref, io_ref, mine_c, mine_b, mine_d, sib_c, sib_b, sib_d,
    hg_ref, hsib_ref, ha_ref, hb_ref, out_c, out_b, out_d, got_c, got_b, got_d,
    load_sem, store_sem, sib_send, sib_recv,
    out_sem, in_sem, rh_sem, rp_sem,
):
    me = lax.axis_index("wide")
    place = lax.axis_index("dp")
    core = lax.rem(place, 2)
    other = 1 - core
    sets = dp // 2
    slots = wide * sets
    mine = me * sets + place // 2
    seq, width = in_ref.shape
    heads = alog_hbm.shape[1]
    half = seq // 2
    nst = wbc_ref.shape[1] // 2
    owners = BLOCK // LANES
    blocks = width // BLOCK
    per_block = BLOCK // 64
    pairs = width // LANES
    group = 8
    groups = slots // group
    sibling = {"wide": me, "dp": place - core + other}

    def at_slot(slot):
        return {"wide": slot // sets, "dp": lax.rem(slot, sets) * 2 + core}

    def to_peer(k):
        return lax.rem(me + k * STRIDE, wide)

    def from_peer(k):
        return lax.rem(me + (wide - k) * STRIDE, wide)

    def targets(step):
        return [to_peer(step * owners + i + 1) for i in range(owners)]

    def sources(step):
        return [from_peer(step * owners + i + 1) for i in range(owners)]

    def lanes_of(p):
        return pl.ds(pl.multiple_of(p * LANES, LANES), LANES)

    def columns(ref, peers):
        return jnp.concatenate([ref[:, lanes_of(p)] for p in peers], axis=1)

    def joined(ref, peers):
        return jnp.concatenate([ref[p, :nst, :] for p in peers], axis=1)

    barrier = pltpu.get_barrier_semaphore()
    pl.semaphore_signal(barrier, inc=1, device_id=sibling, device_id_type=MESH)

    def greet(k, _):
        pl.semaphore_signal(
            barrier, inc=1, device_id=at_slot(lax.rem(mine + k, slots)), device_id_type=MESH
        )
        return 0

    lax.fori_loop(1, slots, greet, 0)

    quarter = width // 4
    loads = []
    for q in range(4):
        part = pl.ds(q * quarter, quarter)
        loads.append((
            pltpu.make_async_copy(in_hbm.at[:, part], in_ref.at[:, part], load_sem.at[0, q]),
            pltpu.make_async_copy(wbc_hbm.at[part], wbc_ref.at[part], load_sem.at[1, q]),
            pltpu.make_async_copy(wdt_hbm.at[:, part], wdt_ref.at[:, part], load_sem.at[2, q]),
        ))
    smalls = [
        pltpu.make_async_copy(src, dst, load_sem.at[3, 2])
        for src, dst in ((alog_hbm, small_ref.at[0]), (bias_hbm, small_ref.at[1]), (skip_hbm, small_ref.at[2]))
    ]
    load_x = pltpu.make_async_copy(x_hbm, x_ref, load_sem.at[3, 0])
    load_g = pltpu.make_async_copy(g_hbm, g_ref, load_sem.at[3, 1])
    for load in loads:
        for one in load:
            one.start()
    for one in smalls:
        one.start()
    load_x.start()
    load_g.start()

    narrow = lax.rem(
        lax.broadcasted_iota(jnp.int32, (2 * heads, LANES), 0), heads
    ) - lax.broadcasted_iota(jnp.int32, (2 * heads, LANES), 1) // 64
    gather_delta = lax.broadcasted_iota(jnp.int32, (LANES, heads), 1) - lax.broadcasted_iota(
        jnp.int32, (LANES, heads), 0
    ) // 64

    def spread(peers):
        return jnp.concatenate([(narrow == 2 * p).astype(BF) for p in peers], axis=1)

    def gathered(peers):
        return jnp.concatenate([(gather_delta == 2 * p).astype(BF) for p in peers], axis=0)

    def remote(src, dst, send, recv, target):
        return pltpu.make_async_remote_copy(
            src_ref=src, dst_ref=dst, send_sem=send, recv_sem=recv, device_id=target,
            device_id_type=MESH,
        )

    def send_f(peer):
        return remote(f_ref.at[peer], gotf_ref.at[me], out_sem.at[0], in_sem.at[0], {"wide": peer})

    def send_e(peer):
        return remote(end_ref.at[peer], gote_ref.at[me], out_sem.at[9], in_sem.at[9], {"wide": peer})

    def send_g(peer):
        return remote(gt_ref.at[peer], gotg_ref.at[me], out_sem.at[1], in_sem.at[1], {"wide": peer})

    def send_h(k):
        peer = to_peer(k)
        step = (k - 1) // owners
        return remote(h_ref.at[peer], goth_ref.at[me], out_sem.at[2], rh_sem.at[step], {"wide": peer})

    def send_p(k):
        peer = to_peer(k)
        step = (k - 1) // owners
        return remote(p_ref.at[peer], gotp_ref.at[me], out_sem.at[3], rp_sem.at[step], {"wide": peer})

    def send_w(out, got, which, slot):
        return remote(out.at[slot], got.at[mine], out_sem.at[which], in_sem.at[which], at_slot(slot))

    def wait_for(ref, count, sem):
        part = ref.at[pl.ds(0, count)]
        pltpu.make_async_copy(part, part, sem).wait()

    def wait_step(ref, sem, step):
        @pl.when(step < blocks - 1)
        def _():
            wait_for(ref, owners, sem.at[step])

        @pl.when(step == blocks - 1)
        def _():
            wait_for(ref, owners - 1, sem.at[step])

    sib_in = remote(int_ref.at[other], sib_ref, sib_send.at[0], sib_recv.at[0], sibling)
    sibling_c = remote(mine_c, sib_c, sib_send.at[1], sib_recv.at[1], sibling)
    sibling_b = remote(mine_b, sib_b, sib_send.at[2], sib_recv.at[2], sibling)
    sibling_d = remote(mine_d, sib_d, sib_send.at[3], sib_recv.at[3], sibling)
    sib_h = remote(hg_ref, hsib_ref, sib_send.at[4], sib_recv.at[4], sibling)

    pltpu.make_async_copy(small_ref, small_ref, load_sem.at[3, 2]).wait()
    bc = jnp.zeros((seq, 2 * nst), F32)
    dt_raw = jnp.zeros((seq, heads), F32)
    for q, load in enumerate(loads):
        for one in load:
            one.wait()
        part = slice(q * quarter, (q + 1) * quarter)
        bc += mm(in_ref[:, part], wbc_ref[part, :])
        dt_raw += mm_nt(in_ref[:, part], wdt_ref[:, part])
    bc = bc.astype(BF)
    dt_raw = dt_raw.astype(BF).astype(F32)
    b_rows = bc[:, :nst]
    c_rows = bc[:, nst:]
    b_t = b_rows.astype(F32).T.astype(BF)
    c_t = c_rows.astype(F32).T.astype(BF)
    dt_pre = dt_raw + small_ref[1]
    dt = jnp.maximum(dt_pre, 0.0) + jnp.log1p(jnp.exp(-jnp.abs(dt_pre)))
    rate = -jnp.exp(small_ref[0])
    log_rate = dt * rate
    pos_r = lax.broadcasted_iota(jnp.int32, (seq, seq), 0)
    pos_c = lax.broadcasted_iota(jnp.int32, (seq, seq), 1)
    lower = (pos_r >= pos_c).astype(BF)
    lr_hi, lr_mid, lr_lo = split3(log_rate)
    cumul = mm(lower, lr_hi) + mm(lower, lr_mid) + mm(lower, lr_lo)
    last = cumul[seq - 1 :, :]
    tail = dt * jnp.exp(last - cumul)
    tail2 = jnp.concatenate(split2(tail), axis=1)
    lq_hi, lq_mid, lq_lo = split3(last)
    none = jnp.zeros((1, heads), BF)
    lq_rows = jnp.concatenate(
        [jnp.concatenate([v, none], axis=1) for v in (lq_hi, lq_mid, lq_lo)]
        + [jnp.zeros((13, 2 * heads), BF)],
        axis=0,
    )

    load_x.wait()
    pl.semaphore_wait(barrier, slots)

    def fresh_f(step, _):
        peers = targets(step)
        r = spread(peers)
        xs = (columns(x_ref, peers).astype(F32) * mm(tail2, r)).astype(BF)
        f_t = mm(b_t, xs).astype(BF)
        ends = mm(lq_rows, r)
        ends = ends[0:1] + ends[1:2] + ends[2:3]
        for i, peer in enumerate(peers):
            lanes = slice(i * LANES, (i + 1) * LANES)
            xs_ref[:, lanes_of(peer)] = xs[:, lanes]
            f_ref[peer] = f_t[:, lanes]
            end_ref[peer] = ends[:, lanes]

            @pl.when(peer != me)
            def _():
                send_f(peer).start()
                send_e(peer).start()

        return 0

    lax.fori_loop(0, blocks, fresh_f, 0)

    head_exp = jnp.exp(cumul)
    exp2 = jnp.concatenate(split2(head_exp), axis=1)
    load_g.wait()

    def fresh_g(step, _):
        peers = targets(step)
        gs = (columns(g_ref, peers).astype(F32) * mm(exp2, spread(peers))).astype(BF)
        g_t = mm(c_t, gs).astype(BF)
        for i, peer in enumerate(peers):
            lanes = slice(i * LANES, (i + 1) * LANES)
            gs_ref[:, lanes_of(peer)] = gs[:, lanes]
            gt_ref[peer] = g_t[:, lanes]

            @pl.when(peer != me)
            def _():
                send_g(peer).start()

        return 0

    lax.fori_loop(0, blocks, fresh_g, 0)

    lt_ref[...] = cumul.T
    u3 = jnp.concatenate(split3(jnp.log(jnp.maximum(dt, 1e-37)) - cumul), axis=1)
    st_ref[...] = mm_nt(b_rows, c_rows)
    lane = lax.broadcasted_iota(jnp.int32, (seq, LANES), 1)
    lane_head = lax.broadcasted_iota(jnp.int32, (half, heads), 1)
    upper = lax.broadcasted_iota(jnp.int32, (half, half), 0) <= lax.broadcasted_iota(
        jnp.int32, (half, half), 1
    )
    row_head = lax.rem(lax.broadcasted_iota(jnp.int32, (3 * heads, LANES), 0), heads)
    nt_ref[...] = jnp.zeros_like(nt_ref)
    col_ref[...] = jnp.zeros_like(col_ref)

    def within(pair, _):
        cols = pl.ds(pl.multiple_of(pair * LANES, LANES), LANES)
        xk = x_ref[:, cols]
        gk = g_ref[:, cols]
        total_lo = jnp.zeros((half, LANES), F32)
        total_hi = jnp.zeros((half, LANES), F32)
        for side in range(2):
            h = pair * 2 + side
            mine_lane = (lane < 64) if side == 0 else (lane >= 64)
            xm = jnp.where(mine_lane, xk, jnp.zeros_like(xk))
            gm = jnp.where(mine_lane, gk, jnp.zeros_like(gk))
            u = mm(u3, (row_head == h).astype(BF))
            lt = lt_ref[pl.ds(h, 1), :]
            w0 = mm_nt(xm[:half], gk)
            w1 = mm_nt(xm[half:], gk[half:])
            a00 = jnp.where(upper, jnp.exp(u[:half] + lt[:, :half]), 0.0)
            a01 = jnp.exp(u[:half] + lt[:, half:])
            a11 = jnp.where(upper, jnp.exp(u[half:] + lt[:, half:]), 0.0)
            s00 = st_ref[:half, :half]
            s01 = st_ref[:half, half:]
            s11 = st_ref[half:, half:]
            p00 = a00 * w0[:, :half]
            p01 = a01 * w0[:, half:]
            p11 = a11 * w1
            nt_ref[:half, :half] += p00
            nt_ref[:half, half:] += p01
            nt_ref[half:, half:] += p11
            total_lo += mm((a00 * s00).astype(BF), gm[:half]) + mm((a01 * s01).astype(BF), gm[half:])
            total_hi += mm((a11 * s11).astype(BF), gm[half:])
            z00 = p00 * s00
            z01 = p01 * s01
            z11 = p11 * s11
            rt_ref[h, :, :half] = jnp.sum(z00, axis=0, keepdims=True)
            rt_ref[h, :, half:] = jnp.sum(z01 + z11, axis=0, keepdims=True)
            col_ref[:half, :] += jnp.where(
                lane_head == h, jnp.sum(z00 + z01, axis=1, keepdims=True), 0.0
            )
            col_ref[half:, :] += jnp.where(
                lane_head == h, jnp.sum(z11, axis=1, keepdims=True), 0.0
            )
        hrow_ref[:, cols] = jnp.sum(xk.astype(F32) * gk.astype(F32), axis=0, keepdims=True)
        gxw_ref[:half, cols] = total_lo
        gxw_ref[half:, cols] = total_hi
        turned = in_ref[:, cols].astype(F32).T.astype(BF)
        for i in range(dp):
            int_ref[i % 2, pair * sets + i // 2] = turned[i * 32 : (i + 1) * 32]
        return 0

    first_part = (pairs * 5) // 8
    lax.fori_loop(0, first_part, within, 0)

    def decay_of(i):
        return jnp.exp(gote_ref[i])

    gotf_ref[me] = f_ref[me]
    gote_ref[me] = end_ref[me]
    wait_for(gote_ref, wide - 1, in_sem.at[9])
    wait_for(gotf_ref, wide - 1, in_sem.at[0])

    def advance_f(i, state):
        h_ref[i] = state.astype(BF)
        return state * decay_of(i) + gotf_ref[i].astype(F32)

    start = jnp.zeros((nst, LANES), F32)
    lax.fori_loop(0, wide, advance_f, start)

    def give_h(k, _):
        send_h(k).start()
        return 0

    lax.fori_loop(1, wide, give_h, 0)
    goth_ref[me] = h_ref[me]

    lax.fori_loop(first_part, pairs, within, 0)
    sib_in.start()

    gotg_ref[me] = gt_ref[me]
    wait_for(gotg_ref, wide - 1, in_sem.at[1])

    def advance_g(k, pull):
        i = wide - 1 - k
        p_ref[i] = pull.astype(BF)
        return pull * decay_of(i) + gotg_ref[i].astype(F32)

    lax.fori_loop(0, wide, advance_g, start)

    def give_p(k, _):
        send_p(k).start()
        return 0

    lax.fori_loop(1, wide, give_p, 0)
    gotp_ref[me] = p_ref[me]

    n_low = nt_ref[...].astype(BF)
    g_b = mm(n_low, c_rows)
    g_c = mm(nt_ref[...].T.astype(BF), b_rows)

    skip_hi, skip_lo = split2(small_ref[2])
    skip_rows = jnp.concatenate(
        [jnp.concatenate([skip_hi, skip_lo], axis=1)]
        + [jnp.concatenate([v, none], axis=1) for v in (lq_hi, lq_mid, lq_lo)]
        + [jnp.zeros((12, 2 * heads), BF)],
        axis=0,
    )
    def finish_f(step, carried):
        row_st, gc = carried
        peers = sources(step)
        wait_step(goth_ref, rh_sem, step)
        h0 = joined(goth_ref, peers)
        gs = columns(gs_ref, peers)
        y_st = mm(c_rows, h0)
        row_st += mm((gs.astype(F32) * y_st).astype(BF), gathered(peers))
        gc += mm_nt(gs, h0)
        return row_st, gc

    zero_h = jnp.zeros((seq, heads), F32)
    row_st, g_c = lax.fori_loop(0, blocks, finish_f, (zero_h, g_c))
    mine_c[...] = g_c.astype(BF)
    sibling_c.start()

    upper_all = (pos_r <= pos_c).astype(BF)

    def suffix(v):
        hi, mid, lo = split3(v)
        return mm(upper_all, hi) + mm(upper_all, mid) + mm(upper_all, lo)

    early = suffix(rt_ref[:, 0, :].T + row_st - col_ref[...])
    gate = 1.0 / (1.0 + jnp.exp(-dt_pre))
    ratio = jnp.where(dt > 0.0, gate / jnp.where(dt > 0.0, dt, 1.0), 1.0)

    def finish_g(step, carried):
        col_st, gb, sums = carried
        peers = sources(step)
        wait_step(gotp_ref, rp_sem, step)
        r = spread(peers)
        gather = gathered(peers)
        dh = joined(gotp_ref, peers)
        xs = columns(xs_ref, peers)
        u_st = mm(b_rows, dh)
        rows = mm(skip_rows, r)
        gx = columns(gxw_ref, peers) + mm(tail2, r) * u_st
        gx = (gx + rows[0:1] * columns(g_ref, peers).astype(F32)).astype(BF)
        col_st += mm((xs.astype(F32) * u_st).astype(BF), gather)
        gb += mm_nt(xs, dh)
        ended = joined(goth_ref, peers).astype(F32) * jnp.exp(rows[1:2] + rows[2:3] + rows[3:4])
        ended += joined(f_ref, peers).astype(F32)
        heads_in = jnp.concatenate(
            [jnp.sum(ended * dh.astype(F32), axis=0, keepdims=True), columns(hrow_ref, peers)], axis=0
        )
        hi, lo = split2(heads_in)
        sums += mm(hi, gather) + mm(lo, gather)
        for i, peer in enumerate(peers):
            cols = lanes_of(peer)
            xo_ref[:, cols] = gx[:, i * LANES : (i + 1) * LANES]
        return col_st, gb, sums

    def weigh(mine_p, sib_p, out, got, which, packed):
        def step_of(step, _):
            order = [
                lax.rem(mine + (step * WEIGHED + i + 1) * STRIDE_W, slots) for i in range(WEIGHED)
            ]
            ours = jnp.concatenate([int_ref[core, slot] for slot in order], axis=0)
            theirs = jnp.concatenate([sib_ref[slot] for slot in order], axis=0)
            w = mm(ours, mine_p[...]) + mm(theirs, sib_p[...])
            for i, slot in enumerate(order):
                at = w[i * 32 : (i + 1) * 32]
                if packed:
                    out[slot, :, : 2 * heads] = jnp.concatenate([at[:16], at[16:]], axis=1).astype(BF)
                else:
                    out[slot] = at.astype(BF)

                @pl.when(slot != mine)
                def _():
                    send_w(out, got, which, slot).start()

            return 0

        lax.fori_loop(0, slots // WEIGHED, step_of, 0)

    early_steps = blocks // 2
    carried = lax.fori_loop(0, early_steps, finish_g, (zero_h, g_b, jnp.zeros((2, heads), F32)))
    sib_in.wait_recv()
    sibling_c.wait_recv()
    weigh(mine_c, sib_c, out_c, got_c, 4, False)
    col_st, g_b, sums = lax.fori_loop(early_steps, blocks, finish_g, carried)
    mine_b[...] = g_b.astype(BF)
    sibling_b.start()
    store_x = pltpu.make_async_copy(xo_ref, xg_hbm, store_sem.at[0])
    store_x.start()

    late_hi, late_lo = split2(col_st)
    d_log = early - mm(upper_all, late_hi) - mm(upper_all, late_lo) + sums[0:1]
    g_dt = (col_ref[...] + col_st) * ratio + rate * d_log * gate
    mine_d[...] = g_dt.astype(BF)
    sibling_d.start()
    g_alog = jnp.sum(d_log * log_rate, axis=0, keepdims=True)
    g_bias = jnp.sum(g_dt, axis=0, keepdims=True)
    hg_ref[...] = jnp.zeros_like(hg_ref)
    hg_ref[0:1, :heads] = g_alog
    hg_ref[1:2, :heads] = g_bias
    hg_ref[2:3, :heads] = sums[1:2]
    sib_h.start()

    def emit(j, _):
        cols = pl.ds(pl.multiple_of(j * BLOCK, BLOCK), BLOCK)
        d_in = mm_nt(mine_b[...], wbc_ref[cols, :nst]) + mm_nt(mine_c[...], wbc_ref[cols, nst:])
        d_in += mm(mine_d[...], wdt_ref[:, cols])
        io_ref[:, cols] = d_in.astype(BF)
        pltpu.make_async_copy(io_ref.at[:, cols], ig_hbm.at[:, cols], store_sem.at[1]).start()
        return 0

    ga, gi = mine // group, lax.rem(mine, group)

    def send_a(i):
        return remote(ha_ref.at[gi], ha_ref.at[gi], out_sem.at[7], in_sem.at[7], at_slot(ga * group + i))

    def send_b(i):
        return remote(hb_ref.at[ga], hb_ref.at[ga], out_sem.at[8], in_sem.at[8], at_slot(i * group + gi))

    def start_a(k, _):
        send_a(lax.rem(gi + k, group)).start()
        return 0

    def start_b(k, _):
        send_b(lax.rem(ga + k, groups)).start()
        return 0

    sibling_b.wait_recv()
    weigh(mine_b, sib_b, out_b, got_b, 5, False)
    sib_h.wait_recv()
    ha_ref[gi] = hg_ref[...] + hsib_ref[...]
    lax.fori_loop(1, group, start_a, 0)
    lax.fori_loop(0, 2, emit, 0)
    sibling_d.wait_recv()
    weigh(mine_d, sib_d, out_d, got_d, 6, True)

    lax.fori_loop(2, blocks // 2, emit, 0)
    wait_for(ha_ref, group - 1, in_sem.at[7])
    hb_ref[ga] = jnp.sum(ha_ref[...], axis=0)
    lax.fori_loop(1, groups, start_b, 0)
    lax.fori_loop(blocks // 2, blocks, emit, 0)

    for at, ref in ((0, f_ref), (1, gt_ref), (2, h_ref), (3, p_ref), (9, end_ref)):
        wait_for(ref, wide - 1, out_sem.at[at])
    wait_for(ha_ref, group - 1, out_sem.at[7])
    store_x.wait()
    pltpu.make_async_copy(io_ref, ig_hbm, store_sem.at[1]).wait()
    sib_in.wait_send()
    sibling_c.wait_send()
    sibling_b.wait_send()
    sibling_d.wait_send()
    sib_h.wait_send()

    wait_for(hb_ref, groups - 1, in_sem.at[8])
    rows = jnp.sum(hb_ref[...], axis=0)
    at = lax.broadcasted_iota(jnp.int32, rows.shape, 1)
    per = heads // wide
    for i in range(per):
        picked = jnp.sum(jnp.where(at == me * per + i, rows, 0.0), axis=1, keepdims=True)
        for r in range(3):
            head_out[i : i + 1, r : r + 1] = picked[r : r + 1]

    def total(out, got, which):
        got[mine] = out[mine]
        wait_for(got, slots - 1, in_sem.at[which])

        def add(k, acc):
            return acc + jnp.sum(got[pl.ds(k * group, group)].astype(F32), axis=0)

        return lax.fori_loop(0, groups, add, jnp.zeros(got.shape[1:], F32))

    wbc_out[:, LANES:] = total(out_c, got_c, 4)
    wbc_out[:, :LANES] = total(out_b, got_b, 5)
    acc = total(out_d, got_d, 6)
    wdt_out[0:16, :] = acc[:, :heads]
    wdt_out[16:32, :] = acc[:, heads : 2 * heads]
    for which, ref in ((4, out_c), (5, out_b), (6, out_d)):
        wait_for(ref, slots - 1, out_sem.at[which])
    wait_for(hb_ref, groups - 1, out_sem.at[8])


def place_kernel(
    x_in, i_in, b_in, d_in, h_in, x_out, i_out, b_out, d_out, h_out,
    x_ref, i_ref, b_ref, d_ref, h_ref, come, go, come_small, go_small,
):
    steps = []
    for a, (src, mid, dst) in enumerate(((b_in, b_ref, b_out), (d_in, d_ref, d_out), (h_in, h_ref, h_out))):
        steps.append((
            pltpu.make_async_copy(src, mid, come_small.at[a]),
            pltpu.make_async_copy(mid, dst, go_small.at[a]),
        ))
    for q in range(PIECES):
        for a, (src, mid, dst) in enumerate(((x_in, x_ref, x_out), (i_in, i_ref, i_out))):
            rows = src.shape[0] // PIECES
            part = pl.ds(q * rows, rows)
            steps.append((
                pltpu.make_async_copy(src.at[part], mid.at[part], come.at[a, q]),
                pltpu.make_async_copy(mid.at[part], dst.at[part], go.at[a, q]),
            ))
    for first, _ in steps:
        first.start()
    for first, second in steps:
        first.wait()
        second.start()
    for _, second in steps:
        second.wait()


def local(wide, dp, layer_input, inner_acts, w_bc, w_dt, a_log, dt_bias, d_skip, out_grad):
    seq, width = layer_input.shape[1:]
    heads = a_log.shape[0]
    nst = w_bc.shape[1] // 2
    slots = wide * dp // 2
    rows = width // (wide * dp)
    any_spec = pl.BlockSpec(memory_space=pl.ANY)
    vmem = pl.BlockSpec(memory_space=pltpu.VMEM)
    dma = pltpu.SemaphoreType.DMA
    v = pltpu.VMEM
    x_grad, input_grad, wbc_grad, wdt_grad, head_grads = pl.pallas_call(
        functools.partial(scan_kernel, wide, dp),
        out_shape=(
            jax.ShapeDtypeStruct((seq, width), BF),
            jax.ShapeDtypeStruct((seq, width), BF),
            jax.ShapeDtypeStruct((rows, 2 * nst), F32),
            jax.ShapeDtypeStruct((rows, heads), F32),
            jax.ShapeDtypeStruct((heads // wide, 3), F32),
        ),
        in_specs=[any_spec] * 8,
        out_specs=(any_spec, any_spec, vmem, vmem, vmem),
        scratch_shapes=[
            v((3, 1, heads), F32),
            v((seq, width), BF),
            v((seq, width), BF),
            v((seq, width), BF),
            v((width, 2 * nst), BF),
            v((heads, width), BF),
            v((wide, 1, LANES), F32),
            v((wide, 1, LANES), F32),
            v((wide, nst, LANES), BF),
            v((wide, nst, LANES), BF),
            v((wide, nst, LANES), BF),
            v((wide, nst, LANES), BF),
            v((wide, nst, LANES), BF),
            v((wide, nst, LANES), BF),
            v((wide, nst, LANES), BF),
            v((wide, nst, LANES), BF),
            v((seq, width), BF),
            v((seq, width), BF),
            v((seq, width), F32),
            v((2, slots, 32, seq), BF),
            v((slots, 32, seq), BF),
            v((seq, seq), F32),
            v((seq, seq), F32),
            v((heads, seq), F32),
            v((heads, 1, seq), F32),
            v((seq, heads), F32),
            v((1, width), F32),
            v((seq, width), BF),
            v((seq, width), BF),
            v((seq, nst), BF),
            v((seq, nst), BF),
            v((seq, heads), BF),
            v((seq, nst), BF),
            v((seq, nst), BF),
            v((seq, heads), BF),
            v((8, LANES), F32),
            v((8, LANES), F32),
            v((8, 8, LANES), F32),
            v((slots // 8, 8, LANES), F32),
            v((slots, 32, LANES), BF),
            v((slots, 32, LANES), BF),
            v((slots, 16, LANES), BF),
            v((slots, 32, LANES), BF),
            v((slots, 32, LANES), BF),
            v((slots, 16, LANES), BF),
            dma((4, 4)),
            dma((2,)),
            dma((5,)),
            dma((5,)),
            dma((10,)),
            dma((10,)),
            dma((width // BLOCK,)),
            dma((width // BLOCK,)),
        ],
        compiler_params=pltpu.CompilerParams(
            collective_id=0, has_side_effects=True, vmem_limit_bytes=56 * 1024 * 1024
        ),
        cost_estimate=pl.CostEstimate(
            flops=30 * seq * width * 256, bytes_accessed=8 * seq * width, transcendentals=0
        ),
        name="scan_backward",
    )(
        layer_input[0], inner_acts[0], out_grad[0], w_bc, w_dt.T,
        a_log[None], dt_bias[None], d_skip[None],
    )
    x_grad, input_grad, wbc_grad, wdt_grad, head_grads = pl.pallas_call(
        place_kernel,
        out_shape=tuple(
            jax.ShapeDtypeStruct(a.shape, a.dtype)
            for a in (x_grad, input_grad, wbc_grad, wdt_grad, head_grads)
        ),
        in_specs=[any_spec] * 5,
        out_specs=[any_spec] * 5,
        scratch_shapes=[
            v(a.shape, a.dtype) for a in (x_grad, input_grad, wbc_grad, wdt_grad, head_grads)
        ]
        + [dma((2, PIECES)), dma((2, PIECES)), dma((3,)), dma((3,))],
        compiler_params=pltpu.CompilerParams(vmem_limit_bytes=60 * 1024 * 1024),
        name="place_results",
    )(x_grad, input_grad, wbc_grad, wdt_grad, head_grads)
    return x_grad[None], input_grad[None], wbc_grad, wdt_grad, head_grads.T


def solution(mesh):
    in_specs = (
        P("dp", "wide", None),
        P("dp", "wide", None),
        P(),
        P(),
        P(),
        P(),
        P(),
        P("dp", "wide", None),
    )
    out_specs = (
        P("dp", "wide", None),
        P("dp", "wide", None),
        P(("wide", "dp"), None),
        P(("wide", "dp"), None),
        P(None, "wide"),
    )
    return jax.shard_map(
        functools.partial(local, mesh.shape["wide"], mesh.shape["dp"]),
        mesh=mesh,
        in_specs=in_specs,
        out_specs=out_specs,
        check_vma=False,
    )
```

```python
import functools

import jax
import jax.numpy as jnp
from jax import lax
from jax.experimental import pallas as pl
from jax.experimental.pallas import tpu as pltpu
from jax.sharding import PartitionSpec as P

MESH = pl.DeviceIdType.MESH
BF = jnp.bfloat16
F32 = jnp.float32
LANES = 128
BLOCK = 512
STRIDE = 13
STRIDE_W = 27
WEIGHED = 16
PIECES = 2


def mm(a, b):
    return jnp.dot(a, b, preferred_element_type=F32)


def mm_nt(a, b):
    return lax.dot_general(a, b, (((1,), (1,)), ((), ())), preferred_element_type=F32)


def split2(v):
    hi = v.astype(BF)
    return hi, (v - hi.astype(F32)).astype(BF)


def split3(v):
    hi = v.astype(BF)
    rest = v - hi.astype(F32)
    mid = rest.astype(BF)
    return hi, mid, (rest - mid.astype(F32)).astype(BF)


def scan_kernel(
    wide, dp, in_hbm, x_hbm, g_hbm, wbc_hbm, wdt_hbm, alog_hbm, bias_hbm, skip_hbm,
    xg_hbm, ig_hbm, wbc_out, wdt_out, head_out,
    small_ref, in_ref, x_ref, g_ref, wbc_ref, wdt_ref, end_ref, gote_ref, f_ref, gt_ref, gotf_ref, gotg_ref, h_ref, p_ref,
    goth_ref, gotp_ref, xs_ref, gs_ref, gxw_ref, int_ref, sib_ref, nt_ref, st_ref, lt_ref, rt_ref,
    col_ref, hrow_ref, xo_ref, io_ref, mine_c, mine_b, mine_d, sib_c, sib_b, sib_d,
    hg_ref, hsib_ref, ha_ref, hb_ref, out_c, out_b, out_d, got_c, got_b, got_d,
    load_sem, store_sem, sib_send, sib_recv,
    out_sem, in_sem, rh_sem, rp_sem,
):
    me = lax.axis_index("wide")
    place = lax.axis_index("dp")
    core = lax.rem(place, 2)
    other = 1 - core
    sets = dp // 2
    slots = wide * sets
    mine = me * sets + place // 2
    seq, width = in_ref.shape
    heads = alog_hbm.shape[1]
    half = seq // 2
    nst = wbc_ref.shape[1] // 2
    owners = BLOCK // LANES
    blocks = width // BLOCK
    per_block = BLOCK // 64
    pairs = width // LANES
    group = 8
    groups = slots // group
    sibling = {"wide": me, "dp": place - core + other}

    def at_slot(slot):
        return {"wide": slot // sets, "dp": lax.rem(slot, sets) * 2 + core}

    def to_peer(k):
        return lax.rem(me + k * STRIDE, wide)

    def from_peer(k):
        return lax.rem(me + (wide - k) * STRIDE, wide)

    def targets(step):
        return [to_peer(step * owners + i + 1) for i in range(owners)]

    def sources(step):
        return [from_peer(step * owners + i + 1) for i in range(owners)]

    def lanes_of(p):
        return pl.ds(pl.multiple_of(p * LANES, LANES), LANES)

    def columns(ref, peers):
        return jnp.concatenate([ref[:, lanes_of(p)] for p in peers], axis=1)

    def joined(ref, peers):
        return jnp.concatenate([ref[p, :nst, :] for p in peers], axis=1)

    barrier = pltpu.get_barrier_semaphore()
    pl.semaphore_signal(barrier, inc=1, device_id=sibling, device_id_type=MESH)

    def greet(k, _):
        pl.semaphore_signal(
            barrier, inc=1, device_id=at_slot(lax.rem(mine + k, slots)), device_id_type=MESH
        )
        return 0

    lax.fori_loop(1, slots, greet, 0)

    quarter = width // 4
    loads = []
    for q in range(4):
        part = pl.ds(q * quarter, quarter)
        loads.append((
            pltpu.make_async_copy(in_hbm.at[:, part], in_ref.at[:, part], load_sem.at[0, q]),
            pltpu.make_async_copy(wbc_hbm.at[part], wbc_ref.at[part], load_sem.at[1, q]),
            pltpu.make_async_copy(wdt_hbm.at[:, part], wdt_ref.at[:, part], load_sem.at[2, q]),
        ))
    smalls = [
        pltpu.make_async_copy(src, dst, load_sem.at[3, 2])
        for src, dst in ((alog_hbm, small_ref.at[0]), (bias_hbm, small_ref.at[1]), (skip_hbm, small_ref.at[2]))
    ]
    load_x = pltpu.make_async_copy(x_hbm, x_ref, load_sem.at[3, 0])
    load_g = pltpu.make_async_copy(g_hbm, g_ref, load_sem.at[3, 1])
    for load in loads:
        for one in load:
            one.start()
    for one in smalls:
        one.start()
    load_x.start()
    load_g.start()

    narrow = lax.rem(
        lax.broadcasted_iota(jnp.int32, (2 * heads, LANES), 0), heads
    ) - lax.broadcasted_iota(jnp.int32, (2 * heads, LANES), 1) // 64
    gather_delta = lax.broadcasted_iota(jnp.int32, (LANES, heads), 1) - lax.broadcasted_iota(
        jnp.int32, (LANES, heads), 0
    ) // 64

    def spread(peers):
        return jnp.concatenate([(narrow == 2 * p).astype(BF) for p in peers], axis=1)

    def gathered(peers):
        return jnp.concatenate([(gather_delta == 2 * p).astype(BF) for p in peers], axis=0)

    def remote(src, dst, send, recv, target):
        return pltpu.make_async_remote_copy(
            src_ref=src, dst_ref=dst, send_sem=send, recv_sem=recv, device_id=target,
            device_id_type=MESH,
        )

    def send_f(peer):
        return remote(f_ref.at[peer], gotf_ref.at[me], out_sem.at[0], in_sem.at[0], {"wide": peer})

    def send_e(peer):
        return remote(end_ref.at[peer], gote_ref.at[me], out_sem.at[9], in_sem.at[9], {"wide": peer})

    def send_g(peer):
        return remote(gt_ref.at[peer], gotg_ref.at[me], out_sem.at[1], in_sem.at[1], {"wide": peer})

    def send_h(k):
        peer = to_peer(k)
        step = (k - 1) // owners
        return remote(h_ref.at[peer], goth_ref.at[me], out_sem.at[2], rh_sem.at[step], {"wide": peer})

    def send_p(k):
        peer = to_peer(k)
        step = (k - 1) // owners
        return remote(p_ref.at[peer], gotp_ref.at[me], out_sem.at[3], rp_sem.at[step], {"wide": peer})

    def send_w(out, got, which, slot):
        return remote(out.at[slot], got.at[mine], out_sem.at[which], in_sem.at[which], at_slot(slot))

    def wait_for(ref, count, sem):
        part = ref.at[pl.ds(0, count)]
        pltpu.make_async_copy(part, part, sem).wait()

    def wait_step(ref, sem, step):
        @pl.when(step < blocks - 1)
        def _():
            wait_for(ref, owners, sem.at[step])

        @pl.when(step == blocks - 1)
        def _():
            wait_for(ref, owners - 1, sem.at[step])

    sib_in = remote(int_ref.at[other], sib_ref, sib_send.at[0], sib_recv.at[0], sibling)
    sibling_c = remote(mine_c, sib_c, sib_send.at[1], sib_recv.at[1], sibling)
    sibling_b = remote(mine_b, sib_b, sib_send.at[2], sib_recv.at[2], sibling)
    sibling_d = remote(mine_d, sib_d, sib_send.at[3], sib_recv.at[3], sibling)
    sib_h = remote(hg_ref, hsib_ref, sib_send.at[4], sib_recv.at[4], sibling)

    pltpu.make_async_copy(small_ref, small_ref, load_sem.at[3, 2]).wait()
    bc = jnp.zeros((seq, 2 * nst), F32)
    dt_raw = jnp.zeros((seq, heads), F32)
    for q, load in enumerate(loads):
        for one in load:
            one.wait()
        part = slice(q * quarter, (q + 1) * quarter)
        bc += mm(in_ref[:, part], wbc_ref[part, :])
        dt_raw += mm_nt(in_ref[:, part], wdt_ref[:, part])
    bc = bc.astype(BF)
    dt_raw = dt_raw.astype(BF).astype(F32)
    b_rows = bc[:, :nst]
    c_rows = bc[:, nst:]
    b_t = b_rows.astype(F32).T.astype(BF)
    c_t = c_rows.astype(F32).T.astype(BF)
    dt_pre = dt_raw + small_ref[1]
    dt = jnp.maximum(dt_pre, 0.0) + jnp.log1p(jnp.exp(-jnp.abs(dt_pre)))
    rate = -jnp.exp(small_ref[0])
    log_rate = dt * rate
    pos_r = lax.broadcasted_iota(jnp.int32, (seq, seq), 0)
    pos_c = lax.broadcasted_iota(jnp.int32, (seq, seq), 1)
    lower = (pos_r >= pos_c).astype(BF)
    lr_hi, lr_mid, lr_lo = split3(log_rate)
    cumul = mm(lower, lr_hi) + mm(lower, lr_mid) + mm(lower, lr_lo)
    last = cumul[seq - 1 :, :]
    tail = dt * jnp.exp(last - cumul)
    tail2 = jnp.concatenate(split2(tail), axis=1)
    lq_hi, lq_mid, lq_lo = split3(last)
    none = jnp.zeros((1, heads), BF)
    lq_rows = jnp.concatenate(
        [jnp.concatenate([v, none], axis=1) for v in (lq_hi, lq_mid, lq_lo)]
        + [jnp.zeros((13, 2 * heads), BF)],
        axis=0,
    )

    load_x.wait()
    pl.semaphore_wait(barrier, slots)

    def fresh_f(step, _):
        peers = targets(step)
        r = spread(peers)
        xs = (columns(x_ref, peers).astype(F32) * mm(tail2, r)).astype(BF)
        f_t = mm(b_t, xs).astype(BF)
        ends = mm(lq_rows, r)
        ends = ends[0:1] + ends[1:2] + ends[2:3]
        for i, peer in enumerate(peers):
            lanes = slice(i * LANES, (i + 1) * LANES)
            xs_ref[:, lanes_of(peer)] = xs[:, lanes]
            f_ref[peer] = f_t[:, lanes]
            end_ref[peer] = ends[:, lanes]

            @pl.when(peer != me)
            def _():
                send_f(peer).start()
                send_e(peer).start()

        return 0

    lax.fori_loop(0, blocks, fresh_f, 0)

    head_exp = jnp.exp(cumul)
    exp2 = jnp.concatenate(split2(head_exp), axis=1)
    load_g.wait()

    def fresh_g(step, _):
        peers = targets(step)
        gs = (columns(g_ref, peers).astype(F32) * mm(exp2, spread(peers))).astype(BF)
        g_t = mm(c_t, gs).astype(BF)
        for i, peer in enumerate(peers):
            lanes = slice(i * LANES, (i + 1) * LANES)
            gs_ref[:, lanes_of(peer)] = gs[:, lanes]
            gt_ref[peer] = g_t[:, lanes]

            @pl.when(peer != me)
            def _():
                send_g(peer).start()

        return 0

    lax.fori_loop(0, blocks, fresh_g, 0)

    lt_ref[...] = cumul.T
    u3 = jnp.concatenate(split3(jnp.log(jnp.maximum(dt, 1e-37)) - cumul), axis=1)
    st_ref[...] = mm_nt(b_rows, c_rows)
    lane = lax.broadcasted_iota(jnp.int32, (seq, LANES), 1)
    lane_head = lax.broadcasted_iota(jnp.int32, (half, heads), 1)
    upper = lax.broadcasted_iota(jnp.int32, (half, half), 0) <= lax.broadcasted_iota(
        jnp.int32, (half, half), 1
    )
    row_head = lax.rem(lax.broadcasted_iota(jnp.int32, (3 * heads, LANES), 0), heads)
    nt_ref[...] = jnp.zeros_like(nt_ref)
    col_ref[...] = jnp.zeros_like(col_ref)

    def within(pair, _):
        cols = pl.ds(pl.multiple_of(pair * LANES, LANES), LANES)
        xk = x_ref[:, cols]
        gk = g_ref[:, cols]
        total_lo = jnp.zeros((half, LANES), F32)
        total_hi = jnp.zeros((half, LANES), F32)
        for side in range(2):
            h = pair * 2 + side
            mine_lane = (lane < 64) if side == 0 else (lane >= 64)
            xm = jnp.where(mine_lane, xk, jnp.zeros_like(xk))
            gm = jnp.where(mine_lane, gk, jnp.zeros_like(gk))
            u = mm(u3, (row_head == h).astype(BF))
            lt = lt_ref[pl.ds(h, 1), :]
            w0 = mm_nt(xm[:half], gk)
            w1 = mm_nt(xm[half:], gk[half:])
            a00 = jnp.where(upper, jnp.exp(u[:half] + lt[:, :half]), 0.0)
            a01 = jnp.exp(u[:half] + lt[:, half:])
            a11 = jnp.where(upper, jnp.exp(u[half:] + lt[:, half:]), 0.0)
            s00 = st_ref[:half, :half]
            s01 = st_ref[:half, half:]
            s11 = st_ref[half:, half:]
            p00 = a00 * w0[:, :half]
            p01 = a01 * w0[:, half:]
            p11 = a11 * w1
            nt_ref[:half, :half] += p00
            nt_ref[:half, half:] += p01
            nt_ref[half:, half:] += p11
            total_lo += mm((a00 * s00).astype(BF), gm[:half]) + mm((a01 * s01).astype(BF), gm[half:])
            total_hi += mm((a11 * s11).astype(BF), gm[half:])
            z00 = p00 * s00
            z01 = p01 * s01
            z11 = p11 * s11
            rt_ref[h, :, :half] = jnp.sum(z00, axis=0, keepdims=True)
            rt_ref[h, :, half:] = jnp.sum(z01 + z11, axis=0, keepdims=True)
            col_ref[:half, :] += jnp.where(
                lane_head == h, jnp.sum(z00 + z01, axis=1, keepdims=True), 0.0
            )
            col_ref[half:, :] += jnp.where(
                lane_head == h, jnp.sum(z11, axis=1, keepdims=True), 0.0
            )
        hrow_ref[:, cols] = jnp.sum(xk.astype(F32) * gk.astype(F32), axis=0, keepdims=True)
        gxw_ref[:half, cols] = total_lo
        gxw_ref[half:, cols] = total_hi
        turned = in_ref[:, cols].astype(F32).T.astype(BF)
        for i in range(dp):
            int_ref[i % 2, pair * sets + i // 2] = turned[i * 32 : (i + 1) * 32]
        return 0

    first_part = (pairs * 5) // 8
    lax.fori_loop(0, first_part, within, 0)

    def decay_of(i):
        return jnp.exp(gote_ref[i])

    gotf_ref[me] = f_ref[me]
    gote_ref[me] = end_ref[me]
    wait_for(gote_ref, wide - 1, in_sem.at[9])
    wait_for(gotf_ref, wide - 1, in_sem.at[0])

    def advance_f(i, state):
        h_ref[i] = state.astype(BF)
        return state * decay_of(i) + gotf_ref[i].astype(F32)

    start = jnp.zeros((nst, LANES), F32)
    lax.fori_loop(0, wide, advance_f, start)

    def give_h(k, _):
        send_h(k).start()
        return 0

    lax.fori_loop(1, wide, give_h, 0)
    goth_ref[me] = h_ref[me]

    lax.fori_loop(first_part, pairs, within, 0)
    sib_in.start()

    gotg_ref[me] = gt_ref[me]
    wait_for(gotg_ref, wide - 1, in_sem.at[1])

    def advance_g(k, pull):
        i = wide - 1 - k
        p_ref[i] = pull.astype(BF)
        return pull * decay_of(i) + gotg_ref[i].astype(F32)

    lax.fori_loop(0, wide, advance_g, start)

    def give_p(k, _):
        send_p(k).start()
        return 0

    lax.fori_loop(1, wide, give_p, 0)
    gotp_ref[me] = p_ref[me]

    n_low = nt_ref[...].astype(BF)
    g_b = mm(n_low, c_rows)
    g_c = mm(nt_ref[...].T.astype(BF), b_rows)

    skip_hi, skip_lo = split2(small_ref[2])
    skip_rows = jnp.concatenate(
        [jnp.concatenate([skip_hi, skip_lo], axis=1)]
        + [jnp.concatenate([v, none], axis=1) for v in (lq_hi, lq_mid, lq_lo)]
        + [jnp.zeros((12, 2 * heads), BF)],
        axis=0,
    )
    def finish_f(step, carried):
        row_st, gc = carried
        peers = sources(step)
        wait_step(goth_ref, rh_sem, step)
        h0 = joined(goth_ref, peers)
        gs = columns(gs_ref, peers)
        y_st = mm(c_rows, h0)
        row_st += mm((gs.astype(F32) * y_st).astype(BF), gathered(peers))
        gc += mm_nt(gs, h0)
        return row_st, gc

    zero_h = jnp.zeros((seq, heads), F32)
    row_st, g_c = lax.fori_loop(0, blocks, finish_f, (zero_h, g_c))
    mine_c[...] = g_c.astype(BF)
    sibling_c.start()

    upper_all = (pos_r <= pos_c).astype(BF)

    def suffix(v):
        hi, mid, lo = split3(v)
        return mm(upper_all, hi) + mm(upper_all, mid) + mm(upper_all, lo)

    early = suffix(rt_ref[:, 0, :].T + row_st - col_ref[...])
    gate = 1.0 / (1.0 + jnp.exp(-dt_pre))
    ratio = jnp.where(dt > 0.0, gate / jnp.where(dt > 0.0, dt, 1.0), 1.0)

    def finish_g(step, carried):
        col_st, gb, sums = carried
        peers = sources(step)
        wait_step(gotp_ref, rp_sem, step)
        r = spread(peers)
        gather = gathered(peers)
        dh = joined(gotp_ref, peers)
        xs = columns(xs_ref, peers)
        u_st = mm(b_rows, dh)
        rows = mm(skip_rows, r)
        gx = columns(gxw_ref, peers) + mm(tail2, r) * u_st
        gx = (gx + rows[0:1] * columns(g_ref, peers).astype(F32)).astype(BF)
        col_st += mm((xs.astype(F32) * u_st).astype(BF), gather)
        gb += mm_nt(xs, dh)
        ended = joined(goth_ref, peers).astype(F32) * jnp.exp(rows[1:2] + rows[2:3] + rows[3:4])
        ended += joined(f_ref, peers).astype(F32)
        heads_in = jnp.concatenate(
            [jnp.sum(ended * dh.astype(F32), axis=0, keepdims=True), columns(hrow_ref, peers)], axis=0
        )
        hi, lo = split2(heads_in)
        sums += mm(hi, gather) + mm(lo, gather)
        for i, peer in enumerate(peers):
            cols = lanes_of(peer)
            xo_ref[:, cols] = gx[:, i * LANES : (i + 1) * LANES]
        return col_st, gb, sums

    def weigh(mine_p, sib_p, out, got, which, packed):
        def step_of(step, _):
            order = [
                lax.rem(mine + (step * WEIGHED + i + 1) * STRIDE_W, slots) for i in range(WEIGHED)
            ]
            ours = jnp.concatenate([int_ref[core, slot] for slot in order], axis=0)
            theirs = jnp.concatenate([sib_ref[slot] for slot in order], axis=0)
            w = mm(ours, mine_p[...]) + mm(theirs, sib_p[...])
            for i, slot in enumerate(order):
                at = w[i * 32 : (i + 1) * 32]
                if packed:
                    out[slot, :, : 2 * heads] = jnp.concatenate([at[:16], at[16:]], axis=1).astype(BF)
                else:
                    out[slot] = at.astype(BF)

                @pl.when(slot != mine)
                def _():
                    send_w(out, got, which, slot).start()

            return 0

        lax.fori_loop(0, slots // WEIGHED, step_of, 0)

    early_steps = blocks // 2
    carried = lax.fori_loop(0, early_steps, finish_g, (zero_h, g_b, jnp.zeros((2, heads), F32)))
    sib_in.wait_recv()
    sibling_c.wait_recv()
    weigh(mine_c, sib_c, out_c, got_c, 4, False)
    col_st, g_b, sums = lax.fori_loop(early_steps, blocks, finish_g, carried)
    mine_b[...] = g_b.astype(BF)
    sibling_b.start()
    store_x = pltpu.make_async_copy(xo_ref, xg_hbm, store_sem.at[0])
    store_x.start()

    late_hi, late_lo = split2(col_st)
    d_log = early - mm(upper_all, late_hi) - mm(upper_all, late_lo) + sums[0:1]
    g_dt = (col_ref[...] + col_st) * ratio + rate * d_log * gate
    mine_d[...] = g_dt.astype(BF)
    sibling_d.start()
    g_alog = jnp.sum(d_log * log_rate, axis=0, keepdims=True)
    g_bias = jnp.sum(g_dt, axis=0, keepdims=True)
    hg_ref[...] = jnp.zeros_like(hg_ref)
    hg_ref[0:1, :heads] = g_alog
    hg_ref[1:2, :heads] = g_bias
    hg_ref[2:3, :heads] = sums[1:2]
    sib_h.start()

    def emit(j, _):
        cols = pl.ds(pl.multiple_of(j * BLOCK, BLOCK), BLOCK)
        d_in = mm_nt(mine_b[...], wbc_ref[cols, :nst]) + mm_nt(mine_c[...], wbc_ref[cols, nst:])
        d_in += mm(mine_d[...], wdt_ref[:, cols])
        io_ref[:, cols] = d_in.astype(BF)
        pltpu.make_async_copy(io_ref.at[:, cols], ig_hbm.at[:, cols], store_sem.at[1]).start()
        return 0

    ga, gi = mine // group, lax.rem(mine, group)

    def send_a(i):
        return remote(ha_ref.at[gi], ha_ref.at[gi], out_sem.at[7], in_sem.at[7], at_slot(ga * group + i))

    def send_b(i):
        return remote(hb_ref.at[ga], hb_ref.at[ga], out_sem.at[8], in_sem.at[8], at_slot(i * group + gi))

    def start_a(k, _):
        send_a(lax.rem(gi + k, group)).start()
        return 0

    def start_b(k, _):
        send_b(lax.rem(ga + k, groups)).start()
        return 0

    sibling_b.wait_recv()
    weigh(mine_b, sib_b, out_b, got_b, 5, False)
    sib_h.wait_recv()
    ha_ref[gi] = hg_ref[...] + hsib_ref[...]
    lax.fori_loop(1, group, start_a, 0)
    lax.fori_loop(0, 2, emit, 0)
    sibling_d.wait_recv()
    weigh(mine_d, sib_d, out_d, got_d, 6, True)

    lax.fori_loop(2, blocks // 2, emit, 0)
    wait_for(ha_ref, group - 1, in_sem.at[7])
    hb_ref[ga] = jnp.sum(ha_ref[...], axis=0)
    lax.fori_loop(1, groups, start_b, 0)
    lax.fori_loop(blocks // 2, blocks, emit, 0)

    for at, ref in ((0, f_ref), (1, gt_ref), (2, h_ref), (3, p_ref), (9, end_ref)):
        wait_for(ref, wide - 1, out_sem.at[at])
    wait_for(ha_ref, group - 1, out_sem.at[7])
    store_x.wait()
    pltpu.make_async_copy(io_ref, ig_hbm, store_sem.at[1]).wait()
    sib_in.wait_send()
    sibling_c.wait_send()
    sibling_b.wait_send()
    sibling_d.wait_send()
    sib_h.wait_send()

    def total(out, got, which):
        got[mine] = out[mine]
        wait_for(got, slots - 1, in_sem.at[which])

        def add(k, acc):
            return acc + jnp.sum(got[pl.ds(k * group, group)].astype(F32), axis=0)

        return lax.fori_loop(0, groups, add, jnp.zeros(got.shape[1:], F32))

    wbc_out[:, LANES:] = total(out_c, got_c, 4)
    wait_for(hb_ref, groups - 1, in_sem.at[8])
    rows = jnp.sum(hb_ref[...], axis=0)
    at = lax.broadcasted_iota(jnp.int32, rows.shape, 1)
    per = heads // wide
    for i in range(per):
        picked = jnp.sum(jnp.where(at == me * per + i, rows, 0.0), axis=1, keepdims=True)
        for r in range(3):
            head_out[i : i + 1, r : r + 1] = picked[r : r + 1]

    wbc_out[:, :LANES] = total(out_b, got_b, 5)
    acc = total(out_d, got_d, 6)
    wdt_out[0:16, :] = acc[:, :heads]
    wdt_out[16:32, :] = acc[:, heads : 2 * heads]
    for which, ref in ((4, out_c), (5, out_b), (6, out_d)):
        wait_for(ref, slots - 1, out_sem.at[which])
    wait_for(hb_ref, groups - 1, out_sem.at[8])


def place_kernel(
    x_in, i_in, b_in, d_in, h_in, x_out, i_out, b_out, d_out, h_out,
    x_ref, i_ref, b_ref, d_ref, h_ref, come, go, come_small, go_small,
):
    steps = []
    for a, (src, mid, dst) in enumerate(((b_in, b_ref, b_out), (d_in, d_ref, d_out), (h_in, h_ref, h_out))):
        steps.append((
            pltpu.make_async_copy(src, mid, come_small.at[a]),
            pltpu.make_async_copy(mid, dst, go_small.at[a]),
        ))
    for q in range(PIECES):
        for a, (src, mid, dst) in enumerate(((x_in, x_ref, x_out), (i_in, i_ref, i_out))):
            rows = src.shape[0] // PIECES
            part = pl.ds(q * rows, rows)
            steps.append((
                pltpu.make_async_copy(src.at[part], mid.at[part], come.at[a, q]),
                pltpu.make_async_copy(mid.at[part], dst.at[part], go.at[a, q]),
            ))
    for first, _ in steps:
        first.start()
    for first, second in steps:
        first.wait()
        second.start()
    for _, second in steps:
        second.wait()


def local(wide, dp, layer_input, inner_acts, w_bc, w_dt, a_log, dt_bias, d_skip, out_grad):
    seq, width = layer_input.shape[1:]
    heads = a_log.shape[0]
    nst = w_bc.shape[1] // 2
    slots = wide * dp // 2
    rows = width // (wide * dp)
    any_spec = pl.BlockSpec(memory_space=pl.ANY)
    vmem = pl.BlockSpec(memory_space=pltpu.VMEM)
    dma = pltpu.SemaphoreType.DMA
    v = pltpu.VMEM
    x_grad, input_grad, wbc_grad, wdt_grad, head_grads = pl.pallas_call(
        functools.partial(scan_kernel, wide, dp),
        out_shape=(
            jax.ShapeDtypeStruct((seq, width), BF),
            jax.ShapeDtypeStruct((seq, width), BF),
            jax.ShapeDtypeStruct((rows, 2 * nst), F32),
            jax.ShapeDtypeStruct((rows, heads), F32),
            jax.ShapeDtypeStruct((heads // wide, 3), F32),
        ),
        in_specs=[any_spec] * 8,
        out_specs=(any_spec, any_spec, vmem, vmem, vmem),
        scratch_shapes=[
            v((3, 1, heads), F32),
            v((seq, width), BF),
            v((seq, width), BF),
            v((seq, width), BF),
            v((width, 2 * nst), BF),
            v((heads, width), BF),
            v((wide, 1, LANES), F32),
            v((wide, 1, LANES), F32),
            v((wide, nst, LANES), BF),
            v((wide, nst, LANES), BF),
            v((wide, nst, LANES), BF),
            v((wide, nst, LANES), BF),
            v((wide, nst, LANES), BF),
            v((wide, nst, LANES), BF),
            v((wide, nst, LANES), BF),
            v((wide, nst, LANES), BF),
            v((seq, width), BF),
            v((seq, width), BF),
            v((seq, width), F32),
            v((2, slots, 32, seq), BF),
            v((slots, 32, seq), BF),
            v((seq, seq), F32),
            v((seq, seq), F32),
            v((heads, seq), F32),
            v((heads, 1, seq), F32),
            v((seq, heads), F32),
            v((1, width), F32),
            v((seq, width), BF),
            v((seq, width), BF),
            v((seq, nst), BF),
            v((seq, nst), BF),
            v((seq, heads), BF),
            v((seq, nst), BF),
            v((seq, nst), BF),
            v((seq, heads), BF),
            v((8, LANES), F32),
            v((8, LANES), F32),
            v((8, 8, LANES), F32),
            v((slots // 8, 8, LANES), F32),
            v((slots, 32, LANES), BF),
            v((slots, 32, LANES), BF),
            v((slots, 16, LANES), BF),
            v((slots, 32, LANES), BF),
            v((slots, 32, LANES), BF),
            v((slots, 16, LANES), BF),
            dma((4, 4)),
            dma((2,)),
            dma((5,)),
            dma((5,)),
            dma((10,)),
            dma((10,)),
            dma((width // BLOCK,)),
            dma((width // BLOCK,)),
        ],
        compiler_params=pltpu.CompilerParams(
            collective_id=0, has_side_effects=True, vmem_limit_bytes=56 * 1024 * 1024
        ),
        cost_estimate=pl.CostEstimate(
            flops=30 * seq * width * 256, bytes_accessed=8 * seq * width, transcendentals=0
        ),
        name="scan_backward",
    )(
        layer_input[0], inner_acts[0], out_grad[0], w_bc, w_dt.T,
        a_log[None], dt_bias[None], d_skip[None],
    )
    x_grad, input_grad, wbc_grad, wdt_grad, head_grads = pl.pallas_call(
        place_kernel,
        out_shape=tuple(
            jax.ShapeDtypeStruct(a.shape, a.dtype)
            for a in (x_grad, input_grad, wbc_grad, wdt_grad, head_grads)
        ),
        in_specs=[any_spec] * 5,
        out_specs=[any_spec] * 5,
        scratch_shapes=[
            v(a.shape, a.dtype) for a in (x_grad, input_grad, wbc_grad, wdt_grad, head_grads)
        ]
        + [dma((2, PIECES)), dma((2, PIECES)), dma((3,)), dma((3,))],
        compiler_params=pltpu.CompilerParams(vmem_limit_bytes=60 * 1024 * 1024),
        name="place_results",
    )(x_grad, input_grad, wbc_grad, wdt_grad, head_grads)
    return x_grad[None], input_grad[None], wbc_grad, wdt_grad, head_grads.T


def solution(mesh):
    in_specs = (
        P("dp", "wide", None),
        P("dp", "wide", None),
        P(),
        P(),
        P(),
        P(),
        P(),
        P("dp", "wide", None),
    )
    out_specs = (
        P("dp", "wide", None),
        P("dp", "wide", None),
        P(("wide", "dp"), None),
        P(("wide", "dp"), None),
        P(None, "wide"),
    )
    return jax.shard_map(
        functools.partial(local, mesh.shape["wide"], mesh.shape["dp"]),
        mesh=mesh,
        in_specs=in_specs,
        out_specs=out_specs,
        check_vma=False,
    )
```
